256 devices in a mesh: tm: 4 (over x), row: 8 (over y, core), col: 8 (over z).
Axes of the slice: x: 4, y: 4, z: 8, core: 2. Of those that a mesh axis runs over, the one named last changes fastest.
Arguments:
- features: bfloat16 [24, 128, 128, 256], P('tm', 'row', 'col'), may hold values from -86 to 86
- first_gain: float32 [256], replicated, may hold values from 0.1 to 1.9
- first_bias: float32 [256], replicated, may hold values from -3 to 3
- first_kernel: bfloat16 [3, 3, 3, 256, 256], replicated, may hold values from -0.078125 to 0.078125
- first_offset: float32 [256], replicated, may hold values from -3 to 3
- second_gain: float32 [256], replicated, may hold values from 0.1 to 1.9
- second_bias: float32 [256], replicated, may hold values from -3 to 3
- second_kernel: bfloat16 [3, 3, 3, 256, 256], replicated, may hold values from -0.21875 to 0.21875
- second_offset: float32 [256], replicated, may hold values from -3 to 3
Outputs:
- upsampled: bfloat16 [24, 256, 256, 256], P('tm', 'row', 'col')
The draws below stay inside these ranges and needn't reach their ends.
All inputs are finite; a program needn't handle non-finite values.
Results may differ from the reference program's by a relative error of at most 0.0029.
Values may be sent and summed in bfloat16 or wider, within the bound.
No kernel may reach another device: no remote copies, remote signals or barrier semaphores. Data moves between devices by JAX's collectives and lax.ppermute only.
A program may use at most 192 MiB of HBM per device.

```python
import math
import jax
import jax.numpy as jnp
from jax import lax

C = 256
G = 32
NF = 24
NH = 128
NW = 128


def draw_features(key, part):
    key = jax.random.fold_in(key, 11)
    subkeys = jax.random.split(key, 5)
    frame_scale = jnp.exp(jax.random.uniform(subkeys[0], (NF, 1, 1, 1), jnp.float32, 0.0, math.log(2.2)))
    row_scale = jnp.exp(jax.random.uniform(subkeys[1], (1, NH, 1, 1), jnp.float32, 0.0, math.log(2.2)))
    col_scale = jnp.exp(jax.random.uniform(subkeys[2], (1, 1, NW, 1), jnp.float32, 0.0, math.log(2.2)))
    chan_scale = jnp.exp(jax.random.uniform(subkeys[3], (1, 1, 1, C), jnp.float32, 0.0, math.log(2.0)))
    scales = frame_scale * row_scale * col_scale * chan_scale
    pattern = jnp.clip(jax.random.normal(subkeys[4], (NF, NH, NW, C), jnp.float32), -4.0, 4.0)
    return (pattern * scales).astype(jnp.bfloat16)


def scatter_about(own_key, extent, spread, reach, kind=jnp.bfloat16):
    result = jax.random.normal(own_key, extent, jnp.float32) * spread
    return jnp.minimum(jnp.maximum(result, -reach), reach).astype(kind)


def setup_inputs(seed: int = 0) -> dict:
    key_of = jax.random.split(jax.random.key(seed), 10)
    features = draw_features(jax.random.fold_in(key_of[9], 71), 0)
    first_gain = jnp.clip(1.0 + 0.18 * jax.random.normal(key_of[1], (C,), jnp.float32), 0.1, 1.9)
    first_bias = scatter_about(key_of[2], (C,), 0.5, 3.0, jnp.float32)
    first_kernel = scatter_about(key_of[3], (3, 3, 3, C, C), (27 * C) ** -0.5, 0.078125)
    first_offset = scatter_about(key_of[4], (C,), 0.5, 3.0, jnp.float32)
    second_gain = jnp.clip(1.0 + 0.18 * jax.random.normal(key_of[5], (C,), jnp.float32), 0.1, 1.9)
    second_bias = scatter_about(key_of[6], (C,), 0.5, 3.0, jnp.float32)
    second_kernel = scatter_about(key_of[7], (3, 3, 3, C, C), (27 * C // 8) ** -0.5, 0.21875)
    second_offset = scatter_about(key_of[8], (C,), 0.5, 3.0, jnp.float32)
    return dict(features=features, first_gain=first_gain, first_bias=first_bias, first_kernel=first_kernel, first_offset=first_offset, second_gain=second_gain, second_bias=second_bias, second_kernel=second_kernel, second_offset=second_offset)


EPSILON = 1e-06

def norm_silu(values, norm_gain, norm_bias):
    shaped = values.reshape(values.shape[:-1] + (G, values.shape[-1] // G))
    average = lax.optimization_barrier(jnp.mean(shaped, axis=(0, 1, 2, 4), keepdims=True))
    centered = shaped - average
    variance = lax.optimization_barrier(jnp.mean(centered * centered, axis=(0, 1, 2, 4), keepdims=True))
    normed = (centered * jax.lax.rsqrt(variance + EPSILON)).reshape(values.shape)
    return jax.nn.silu(normed * norm_gain + norm_bias)

def causal_conv(active, kernel, offset):
    frames, height, breadth, channels = active.shape
    padded = jnp.concatenate([active[:1], active[:1], active], axis=0)
    padded = jnp.pad(padded, ((0, 0), (1, 1), (1, 1), (0, 0)))
    shifted = jnp.concatenate([padded[:, :, col_lag:col_lag + breadth] for col_lag in range(3)], axis=-1)
    folded = kernel.reshape(3, 3, 3 * channels, channels)
    summed = jnp.zeros((frames * height * breadth, channels), jnp.float32)
    for time_lag in range(3):
        for row_lag in range(3):
            window = shifted[time_lag:time_lag + frames, row_lag:row_lag + height].reshape(-1, 3 * channels)
            summed = summed + jnp.dot(window, folded[time_lag, row_lag], preferred_element_type=jnp.float32)
    return summed.reshape(frames, height, breadth, channels) + offset

def reference(features, first_gain, first_bias, first_kernel, first_offset, second_gain, second_bias, second_kernel, second_offset):
    inputs = features.astype(jnp.float32)
    active = norm_silu(inputs, first_gain, first_bias).astype(jnp.bfloat16)
    hidden = causal_conv(active, first_kernel, first_offset)
    active = norm_silu(hidden, second_gain, second_bias).astype(jnp.bfloat16)
    branch = causal_conv(active, second_kernel, second_offset)
    blended = (inputs + branch).astype(jnp.bfloat16)
    return jnp.repeat(jnp.repeat(blended, 2, axis=1), 2, axis=2)
```

```python
import jax
import jax.numpy as jnp
from jax import lax
from jax.sharding import PartitionSpec as P

G = 32


EPSILON = 1e-06


def passed_along(x, axis, by):
    size = lax.axis_size(axis)
    pairs = [(i, i + by) for i in range(size) if 0 <= i + by < size]
    return lax.ppermute(x, axis, pairs)


def extended(x, sides, width):
    for axis, dim in sides:
        size, length = (lax.axis_size(axis), x.shape[dim])
        up = [(i, (i + 1) % size) for i in range(size - 1)]
        down = [(j, i) for i, j in up]
        last = lax.slice_in_dim(x, length - width, length, axis=dim)
        first = lax.slice_in_dim(x, 0, width, axis=dim)
        before = lax.ppermute(last, axis, up)
        after = lax.ppermute(first, axis, down)
        x = jnp.concatenate([before, x, after], axis=dim)
    return x


AXES = ("tm", "row", "col")


def statistics(values):
    shaped = values.reshape(-1, G, values.shape[-1] // G)
    own = shaped.shape[0] * shaped.shape[2]
    devices = lax.axis_size(AXES)
    mean = jnp.sum(shaped, axis=(0, 2)) / own
    centered = shaped - mean[None, :, None]
    squares = jnp.sum(centered * centered, axis=(0, 2))
    packed = jnp.concatenate([mean, squares, jnp.zeros((128 - 2 * G,), jnp.float32)])
    everyone = lax.all_to_all(
        jnp.broadcast_to(packed[None, None], (devices, 1, 128)), AXES, 0, 0
    )[:, 0]
    means, squares = (everyone[:, :G], everyone[:, G : 2 * G])
    average = jnp.mean(means, axis=0)
    apart = means - average
    total = jnp.sum(squares, axis=0) + own * jnp.sum(apart * apart, axis=0)
    return (average, lax.rsqrt(total / (own * devices) + EPSILON))


def norm_silu(values, average, inverse, norm_gain, norm_bias):
    shaped = values.reshape(values.shape[:-1] + (G, values.shape[-1] // G))
    normed = ((shaped - average[:, None]) * inverse[:, None]).reshape(values.shape)
    return jax.nn.silu(normed * norm_gain + norm_bias)


def local_conv(padded, kernel, offset, frames, height, breadth):
    channels = padded.shape[-1]
    shifted = jnp.concatenate(
        [padded[:, :, col_lag : col_lag + breadth] for col_lag in range(3)], axis=-1
    )
    folded = kernel.reshape(3, 3, 3 * channels, channels)
    summed = jnp.zeros((frames * height * breadth, channels), jnp.float32)
    for time_lag in range(3):
        for row_lag in range(3):
            window = shifted[time_lag : time_lag + frames, row_lag : row_lag + height].reshape(
                -1, 3 * channels
            )
            summed = summed + jnp.dot(
                window, folded[time_lag, row_lag], preferred_element_type=jnp.float32
            )
    return summed.reshape(frames, height, breadth, channels) + offset


def local(
    features,
    first_gain,
    first_bias,
    first_kernel,
    first_offset,
    second_gain,
    second_bias,
    second_kernel,
    second_offset,
):
    frames, height, breadth, channels = features.shape
    first_device = lax.axis_index("tm") == 0
    inputs = features.astype(jnp.float32)

    def extend(active):
        earlier = passed_along(active[-2:], "tm", 1)
        earlier = jnp.where(first_device, jnp.broadcast_to(active[:1], earlier.shape), earlier)
        joined = jnp.concatenate([earlier, active], axis=0)
        return extended(joined, (("row", 1), ("col", 2)), 1)

    first_avg, first_inv = statistics(inputs)
    active = norm_silu(inputs, first_avg, first_inv, first_gain, first_bias).astype(jnp.bfloat16)
    hidden = local_conv(extend(active), first_kernel, first_offset, frames, height, breadth)
    second_avg, second_inv = statistics(hidden)
    active = norm_silu(hidden, second_avg, second_inv, second_gain, second_bias).astype(
        jnp.bfloat16
    )
    branch = local_conv(extend(active), second_kernel, second_offset, frames, height, breadth)
    blended = (inputs + branch).astype(jnp.bfloat16)
    return jnp.repeat(jnp.repeat(blended, 2, axis=1), 2, axis=2)


def solution(mesh):
    placed = (P("tm", "row", "col", None), P(), P(), P(), P(), P(), P(), P(), P())
    return jax.shard_map(
        local, mesh=mesh, in_specs=placed, out_specs=P("tm", "row", "col", None), check_vma=False
    )
```

```python
import functools

import jax
import jax.numpy as jnp
from jax import lax
from jax.experimental import pallas as pl
from jax.experimental.pallas import tpu as pltpu
from jax.sharding import PartitionSpec as P

G = 32
EPSILON = 1e-06
LANES = 128
F32 = jnp.float32
BF16 = jnp.bfloat16
AXES = ("tm", "row", "col")


def picker(rows, cols, shift, channels_last):
    channel = lax.broadcasted_iota(jnp.int32, (rows, cols), 1 if channels_last else 0)
    lane = lax.broadcasted_iota(jnp.int32, (rows, cols), 0 if channels_last else 1)
    per = (cols if channels_last else rows) // G
    return (channel // per + shift == lane).astype(F32)


def exact_dot(a, b):
    return jnp.dot(a, b, precision=lax.Precision.HIGHEST, preferred_element_type=F32)


def fold(x, mean, squares, seen):
    n = float(x.shape[0])
    own = jnp.sum(x, axis=0, keepdims=True) / n
    apart = x - own
    spread = jnp.sum(apart * apart, axis=0, keepdims=True)
    both = seen + n
    gap = own - mean
    return mean + gap * (n / both), squares + spread + gap * gap * (seen * n / both), both


def pack(mean, squares, count):
    channels = mean.shape[-1]
    wide = jnp.broadcast_to(mean, (8, channels))
    grouped = exact_dot(wide, picker(channels, LANES, 0, False)) / (channels // G)
    apart = exact_dot(grouped, picker(LANES, channels, 0, True)) - wide
    total = squares + count * apart * apart
    return (grouped + exact_dot(total, picker(channels, LANES, G, False)))[:1]


def merge(rows, count):
    summed = jnp.sum(rows, axis=0, keepdims=True)
    average = summed / rows.shape[0]
    apart = rows - average
    spread = count * jnp.sum(apart * apart, axis=0, keepdims=True)
    lane = lax.broadcasted_iota(jnp.int32, (1, LANES), 1)
    total = jnp.where(lane < 2 * G, summed + pltpu.roll(spread, G, 1), 0.0)
    return jnp.where(lane < G, average, total)


def unpack(row, count, gain, bias):
    channels = gain.shape[-1]
    wide = jnp.broadcast_to(row, (8, LANES))
    mean = exact_dot(wide, picker(LANES, channels, 0, True))[:1]
    squares = exact_dot(wide, picker(LANES, channels, G, True))[:1]
    scale = lax.rsqrt(squares / count + EPSILON) * gain
    return mean, 0.5 * scale, 0.5 * bias


def active(x, norm):
    mean, half_scale, half_bias = norm
    half = (x.astype(F32) - mean) * half_scale + half_bias
    return half * jnp.tanh(half) + half


def stats_kernel(x_ref, o_ref):
    frames, height, breadth, channels = x_ref.shape

    def one(t, carry):
        return fold(x_ref[t].astype(F32).reshape(height * breadth, channels), *carry)

    zero = jnp.zeros((1, channels), F32)
    mean, squares, _ = lax.fori_loop(0, frames, one, (zero, zero, jnp.float32(0)))
    row = pack(mean, squares, float(frames * height * breadth))
    o_ref[...] = jnp.broadcast_to(row[None], o_ref.shape)


def merge_kernel(count, rows_ref, o_ref):
    row = merge(rows_ref[:, 0, :], count)
    o_ref[...] = jnp.broadcast_to(row[None], o_ref.shape)


def spread_rows(a_ref, t, i, y, left, right):
    a_ref[0, t, i] = jnp.concatenate([left, y[:-1]], axis=0).astype(BF16)
    a_ref[1, t, i] = y.astype(BF16)
    a_ref[2, t, i] = jnp.concatenate([y[1:], right], axis=0).astype(BF16)


def fill(a_ref, side_ref, norm, own_ref, early_ref, above_ref, below_ref, left_ref, right_ref):
    frames = a_ref.shape[1]
    height = a_ref.shape[2]
    row, rows = lax.axis_index("row"), lax.axis_size("row")
    col, cols = lax.axis_index("col"), lax.axis_size("col")
    top = jnp.where(row == 0, 0.0, 1.0).astype(F32)
    bottom = jnp.where(row == rows - 1, 0.0, 1.0).astype(F32)
    border = 0 if above_ref is None else above_ref.shape[1]
    cut = max(border, 1)
    line = lax.broadcasted_iota(jnp.int32, (height, 1), 0)
    inside = jnp.where(line < cut, top, jnp.where(line >= height - cut, bottom, 1.0))
    leftmost = inside * jnp.where(col == 0, 0.0, 1.0).astype(F32)
    rightmost = inside * jnp.where(col == cols - 1, 0.0, 1.0).astype(F32)

    def frame(source_ref, first, t):
        side_ref[0] = active(left_ref[t], norm) * leftmost
        side_ref[1] = active(right_ref[t], norm) * rightmost
        for i in range(height):
            if i < border:
                x = above_ref[t, i]
            elif i >= height - border:
                x = below_ref[t, i - (height - border)]
            else:
                x = source_ref[t - first, i - border]
            y = active(x, norm)
            if i < cut:
                y = y * top
            elif i >= height - cut:
                y = y * bottom
            spread_rows(
                a_ref, t, i, y, side_ref[0, pl.ds(i, 1), :], side_ref[1, pl.ds(i, 1), :]
            )

    def early(t, carry):
        frame(early_ref, 0, t)
        return carry

    def own(t, carry):
        frame(own_ref, 2, t)
        return carry

    lax.fori_loop(0, 2, early, 0)
    lax.fori_loop(2, frames, own, 0)


def conv_frame(a_ref, w_ref, t):
    rows, breadth, channels = a_ref.shape[2] - 2, a_ref.shape[3], a_ref.shape[4]
    total = None
    for a in range(3):
        for b in range(3):
            window = jnp.concatenate(
                [
                    a_ref[c, t + a, pl.ds(b, rows)].reshape(rows * breadth, channels)
                    for c in range(3)
                ],
                axis=1,
            )
            part = jnp.dot(window, w_ref[3 * a + b], preferred_element_type=F32)
            total = part if total is None else total + part
    return total


def first_kernel_body(
    devices,
    per_row,
    own_ref,
    early_ref,
    above_ref,
    below_ref,
    left_ref,
    right_ref,
    stats_ref,
    gain_ref,
    bias_ref,
    offset_ref,
    w_hbm,
    hidden_ref,
    packed_ref,
    w_ref,
    a_ref,
    side_ref,
    sem,
):
    load = pltpu.make_async_copy(w_hbm, w_ref, sem)
    load.start()
    frames, height, breadth, channels = own_ref.shape
    group = frames * height * breadth * (channels // G)
    norm = unpack(
        merge(stats_ref[:, 0, :], float(per_row * group)),
        float(devices * group),
        gain_ref[...],
        bias_ref[...],
    )
    fill(
        a_ref, side_ref, norm, own_ref, early_ref, above_ref, below_ref, left_ref, right_ref
    )
    load.wait()
    tall = height + 2

    def one(t, carry):
        out = conv_frame(a_ref, w_ref, t) + offset_ref[...]
        hidden_ref[t] = out.reshape(tall, breadth, channels)
        return fold(out[breadth:-breadth], *carry)

    zero = jnp.zeros((1, channels), F32)
    mean, squares, _ = lax.fori_loop(0, frames, one, (zero, zero, jnp.float32(0)))
    row = pack(mean, squares, float(frames * height * breadth))
    packed_ref[...] = jnp.broadcast_to(row[None], packed_ref.shape)


def second_kernel_body(
    devices,
    per_row,
    features_ref,
    own_ref,
    early_ref,
    left_ref,
    right_ref,
    stats_ref,
    gain_ref,
    bias_ref,
    offset_ref,
    w_hbm,
    out_hbm,
    w_ref,
    a_ref,
    side_ref,
    out_ref,
    sem,
    out_sem,
):
    load = pltpu.make_async_copy(w_hbm, w_ref, sem)
    load.start()
    frames, height, breadth, channels = features_ref.shape
    group = frames * height * breadth * (channels // G)
    norm = unpack(
        merge(stats_ref[:, 0, :], float(per_row * group)),
        float(devices * group),
        gain_ref[...],
        bias_ref[...],
    )
    fill(a_ref, side_ref, norm, own_ref, early_ref, None, None, left_ref, right_ref)
    load.wait()
    cells = height * breadth
    target = lax.broadcasted_iota(jnp.int32, (2 * cells, cells), 0)
    source = lax.broadcasted_iota(jnp.int32, (2 * cells, cells), 1)
    twice = (target // 2 == source).astype(BF16)

    def one(t, carry):
        out = conv_frame(a_ref, w_ref, t) + offset_ref[...]
        blended = (features_ref[t].astype(F32).reshape(cells, channels) + out).astype(BF16)
        wide = jnp.dot(twice, blended, preferred_element_type=F32).astype(BF16)
        wide = wide.reshape(height, 2 * breadth, channels)
        out_ref[t, :, 0] = wide
        out_ref[t, :, 1] = wide
        pltpu.make_async_copy(out_ref.at[t], out_hbm.at[t], out_sem.at[t]).start()
        return carry

    lax.fori_loop(0, frames, one, 0)
    for t in range(frames):
        pltpu.make_async_copy(out_ref.at[t], out_hbm.at[t], out_sem.at[t]).wait()


VMEM = pl.BlockSpec(memory_space=pltpu.VMEM)
ANY = pl.BlockSpec(memory_space=pl.ANY)
PARAMS = pltpu.CompilerParams(vmem_limit_bytes=40 * 2**20)


def shifted(x, axis, by):
    size = lax.axis_size(axis)
    return lax.ppermute(x, axis, [(i, i + by) for i in range(size) if 0 <= i + by < size])


def everyone(rows, axes):
    return lax.all_to_all(rows, axes, 0, 0)


def local(
    features,
    first_gain,
    first_bias,
    first_kernel,
    first_offset,
    second_gain,
    second_bias,
    second_kernel,
    second_offset,
):
    frames, height, breadth, channels = features.shape
    first_device = lax.axis_index("tm") == 0
    slabs = lax.axis_size("tm") * lax.axis_size("row")
    strips = lax.axis_size("col")
    devices = slabs * strips
    group = frames * height * breadth * (channels // G)
    rows_out = jax.ShapeDtypeStruct((slabs, 1, LANES), F32)
    strip_rows_out = jax.ShapeDtypeStruct((strips, 1, LANES), F32)

    def flat(v):
        return v.reshape(1, channels)

    def earlier(x):
        got = shifted(x[-2:], "tm", 1)
        return jnp.where(first_device, jnp.broadcast_to(x[:1], got.shape), got)

    def merged(rows):
        return pl.pallas_call(
            functools.partial(merge_kernel, float(group)),
            out_shape=strip_rows_out,
            in_specs=[VMEM],
            out_specs=VMEM,
        )(rows)

    stats = pl.pallas_call(
        stats_kernel, out_shape=rows_out, in_specs=[VMEM], out_specs=VMEM
    )(features)
    early = earlier(features)
    stats = merged(everyone(stats, ("tm", "row")))
    above = shifted(jnp.concatenate([early[:, -2:], features[:, -2:]], axis=0), "row", 1)
    below = shifted(jnp.concatenate([early[:, :2], features[:, :2]], axis=0), "row", -1)
    stats = everyone(stats, "col")

    def column(j):
        inner = jnp.concatenate([early[:, :, j], features[:, :, j]], axis=0)
        return jnp.concatenate([above[:, :, j], inner, below[:, :, j]], axis=1)

    left = shifted(column(breadth - 1), "col", 1)
    right = shifted(column(0), "col", -1)
    hidden, stats = pl.pallas_call(
        functools.partial(first_kernel_body, devices, slabs),
        out_shape=(
            jax.ShapeDtypeStruct((frames, height + 2, breadth, channels), F32),
            rows_out,
        ),
        in_specs=[VMEM] * 10 + [ANY],
        out_specs=(VMEM, VMEM),
        scratch_shapes=[
            pltpu.VMEM((9, 3 * channels, channels), BF16),
            pltpu.VMEM((3, frames + 2, height + 4, breadth, channels), BF16),
            pltpu.VMEM((2, height + 4, channels), F32),
            pltpu.SemaphoreType.DMA,
        ],
        compiler_params=PARAMS,
    )(
        features,
        early,
        above,
        below,
        left,
        right,
        stats,
        flat(first_gain),
        flat(first_bias),
        flat(first_offset),
        first_kernel.reshape(9, 3 * channels, channels),
    )
    early = earlier(hidden)
    stats = merged(everyone(stats, ("tm", "row")))
    left = shifted(
        jnp.concatenate([early[:, :, breadth - 1], hidden[:, :, breadth - 1]], axis=0), "col", 1
    )
    right = shifted(jnp.concatenate([early[:, :, 0], hidden[:, :, 0]], axis=0), "col", -1)
    stats = everyone(stats, "col")
    out = pl.pallas_call(
        functools.partial(second_kernel_body, devices, slabs),
        out_shape=jax.ShapeDtypeStruct((frames, height, 2, 2 * breadth, channels), BF16),
        in_specs=[VMEM] * 9 + [ANY],
        out_specs=ANY,
        scratch_shapes=[
            pltpu.VMEM((9, 3 * channels, channels), BF16),
            pltpu.VMEM((3, frames + 2, height + 2, breadth, channels), BF16),
            pltpu.VMEM((2, height + 2, channels), F32),
            pltpu.VMEM((frames, height, 2, 2 * breadth, channels), BF16),
            pltpu.SemaphoreType.DMA,
            pltpu.SemaphoreType.DMA((frames,)),
        ],
        compiler_params=PARAMS,
    )(
        features,
        hidden,
        early,
        left,
        right,
        stats,
        flat(second_gain),
        flat(second_bias),
        flat(second_offset),
        second_kernel.reshape(9, 3 * channels, channels),
    )
    return out.reshape(frames, 2 * height, 2 * breadth, channels)


def solution(mesh):
    placed = (P("tm", "row", "col", None), P(), P(), P(), P(), P(), P(), P(), P())
    return jax.shard_map(
        local, mesh=mesh, in_specs=placed, out_specs=P("tm", "row", "col", None), check_vma=False
    )
```

```python
import functools

import jax
import jax.numpy as jnp
from jax import lax
from jax.experimental import pallas as pl
from jax.experimental.pallas import tpu as pltpu
from jax.sharding import PartitionSpec as P

G = 32
EPSILON = 1e-06
LANES = 128
F32 = jnp.float32
BF16 = jnp.bfloat16
AXES = ("tm", "row", "col")
LINE = 16
EDGE = 24


def picked(x, chosen):
    high = x.astype(BF16).astype(F32)
    rest = x - high
    middle = rest.astype(BF16).astype(F32)
    low = rest - middle
    stacked = jnp.concatenate([high, middle, low, jnp.zeros((13, x.shape[1]), F32)], axis=0)
    return jnp.sum(
        jnp.dot(stacked.astype(BF16), chosen, preferred_element_type=F32), axis=0, keepdims=True
    )


def lanes_of(channels, channels_last):
    shape = (LANES, 2 * channels) if channels_last else (2 * channels, LANES)
    channel = lax.broadcasted_iota(jnp.int32, shape, 1 if channels_last else 0)
    lane = lax.broadcasted_iota(jnp.int32, shape, 0 if channels_last else 1)
    return (channel // (channels // G) == lane).astype(BF16)


def fold(x, mean, squares, seen):
    n = float(x.shape[0])
    own = jnp.sum(x, axis=0, keepdims=True) / n
    apart = x - own
    spread = jnp.sum(apart * apart, axis=0, keepdims=True)
    both = seen + n
    gap = own - mean
    return mean + gap * (n / both), squares + spread + gap * gap * (seen * n / both), both


def pack(mean, squares, count):
    channels = mean.shape[-1]
    per = channels // G
    one = lax.broadcasted_iota(jnp.int32, (channels, channels), 0) // per
    other = lax.broadcasted_iota(jnp.int32, (channels, channels), 1) // per
    grouped = picked(mean, (one == other).astype(BF16)) / per
    apart = grouped - mean
    total = squares + count * apart * apart
    return picked(jnp.concatenate([mean / per, total], axis=1), lanes_of(channels, False))


def merge(rows, count):
    summed = jnp.sum(rows, axis=0, keepdims=True)
    average = summed / rows.shape[0]
    apart = rows - average
    spread = count * jnp.sum(apart * apart, axis=0, keepdims=True)
    lane = lax.broadcasted_iota(jnp.int32, (1, LANES), 1)
    total = jnp.where(lane < 2 * G, summed + pltpu.roll(spread, G, 1), 0.0)
    return jnp.where(lane < G, average, total)


def norm_of(stats_ref, group, gain_ref, bias_ref):
    rows = stats_ref[...]
    channels = gain_ref.shape[-1]
    wide = picked(merge(rows, float(group)), lanes_of(channels, True))
    variance = wide[:, channels:] / float(group * rows.shape[0])
    scale = lax.rsqrt(variance + EPSILON) * gain_ref[...]
    return wide[:, :channels], 0.5 * scale, 0.5 * bias_ref[...]


def active(x, norm):
    mean, half_scale, half_bias = norm
    half = (x.astype(F32) - mean) * half_scale + half_bias
    return half * jnp.tanh(half) + half


def within():
    def unless(axis, where):
        return jnp.where(lax.axis_index(axis) == where, 0.0, 1.0).astype(F32)

    return (
        unless("row", 0),
        unless("row", lax.axis_size("row") - 1),
        unless("col", 0),
        unless("col", lax.axis_size("col") - 1),
    )


def columns_kernel(x_ref, to_left_ref, to_right_ref):
    frames, height, breadth, channels = x_ref.shape
    cells = height * breadth
    target = lax.broadcasted_iota(jnp.int32, (4 * height, cells), 0)
    source = lax.broadcasted_iota(jnp.int32, (4 * height, cells), 1)
    which = target // height
    column = jnp.where(which < 2, which, which + (breadth - 4))
    chosen = (source == (target % height) * breadth + column).astype(BF16)
    for t in range(frames):
        got = jnp.dot(
            chosen, x_ref[t].reshape(cells, channels), preferred_element_type=F32
        ).astype(BF16)
        got = got.reshape(4, height, channels)
        to_left_ref[t] = got[:2]
        to_right_ref[t] = got[2:]


def stats_kernel(x_ref, o_ref):
    frames, height, breadth, channels = x_ref.shape
    carry = (jnp.zeros((1, channels), F32), jnp.zeros((1, channels), F32), 0.0)
    for t in range(frames):
        carry = fold(x_ref[t].astype(F32).reshape(height * breadth, channels), *carry)
    row = pack(carry[0], carry[1], float(frames * height * breadth))
    o_ref[...] = jnp.broadcast_to(row[None], o_ref.shape)


def rows_kernel(x_ref, left_ref, right_ref, to_above_ref, to_below_ref):
    frames, height, breadth, channels = x_ref.shape
    for t in range(frames):
        corners = [
            ref[t, k].astype(F32) for ref in (left_ref, right_ref) for k in range(2)
        ]
        for ref, start in ((to_above_ref, 0), (to_below_ref, height - 2)):
            ref[t, 0] = x_ref[t, start]
            ref[t, 1] = x_ref[t, start + 1]
            line = [c[start : start + 2] for c in corners]
            line.append(jnp.zeros((LINE - 8, channels), F32))
            ref[t, 2] = jnp.concatenate(line, axis=0).astype(BF16)


def put(a_ref, t, i, y, left, right):
    a_ref[0, t, i] = jnp.concatenate([left, y[:-1]], axis=0).astype(BF16)
    a_ref[1, t, i] = y.astype(BF16)
    a_ref[2, t, i] = jnp.concatenate([y[1:], right], axis=0).astype(BF16)


def conv_frame(a_ref, e_ref, w_ref, t):
    rows, breadth, channels = a_ref.shape[2] - 2, a_ref.shape[3], a_ref.shape[4]
    total = None
    for a in range(3):
        for b in range(3):
            window = jnp.concatenate(
                [
                    a_ref[c, t + a, pl.ds(b, rows)].reshape(rows * breadth, channels)
                    for c in range(3)
                ],
                axis=1,
            )
            if e_ref is not None:
                window = jnp.concatenate([window, e_ref[b, t + a]], axis=0)
            part = jnp.dot(window, w_ref[3 * a + b], preferred_element_type=F32)
            total = part if total is None else total + part
    return total


def first_body(
    own_ref,
    above_ref,
    below_ref,
    left_ref,
    right_ref,
    early_ref,
    stats_ref,
    gain_ref,
    bias_ref,
    offset_ref,
    w_hbm,
    hidden_ref,
    packed_ref,
    w_ref,
    a_ref,
    e_ref,
    c_ref,
    sem,
):
    load = pltpu.make_async_copy(w_hbm, w_ref, sem)
    load.start()
    frames, height, breadth, channels = own_ref.shape
    norm = norm_of(
        stats_ref, frames * height * breadth * (channels // G), gain_ref, bias_ref
    )
    top, bottom, leftmost, rightmost = within()
    tall = height + 4

    def frame(center, above, below, left, right, s, t):
        upper = active(above[s, 2], norm) * top
        lower = active(below[s, 2], norm) * bottom
        for k in range(4):
            side = leftmost if k < 2 else rightmost
            x = left[s, k] if k < 2 else right[s, k - 2]
            c_ref[k, pl.ds(0, 2)] = upper[2 * k : 2 * k + 2] * side
            c_ref[k, pl.ds(2, height)] = active(x, norm) * side
            c_ref[k, pl.ds(2 + height, 2)] = lower[2 * k : 2 * k + 2] * side
        for i in range(tall):
            if i < 2:
                y = active(above[s, i], norm) * top
            elif i >= height + 2:
                y = active(below[s, i - height - 2], norm) * bottom
            else:
                y = active(center[s, i - 2], norm)
            put(a_ref, t, i, y, c_ref[1, pl.ds(i, 1)], c_ref[2, pl.ds(i, 1)])
            c_ref[4, pl.ds(i, 1)] = y[:1]
            c_ref[5, pl.ds(i, 1)] = y[breadth - 1 :]
        for b in range(3):
            for c, (near, far) in enumerate(((0, 5), (1, 2), (4, 3))):
                both = jnp.concatenate(
                    [c_ref[near, pl.ds(b, EDGE)], c_ref[far, pl.ds(b, EDGE)]], axis=0
                )
                e_ref[b, t, :, pl.ds(c * channels, channels)] = both.astype(BF16)

    c_ref[...] = jnp.zeros_like(c_ref)
    own = (own_ref, above_ref, below_ref, left_ref, right_ref)
    lines = [(0, height), (height, 3), (height + 3, 3), (height + 6, 2), (height + 8, 2)]
    sent = [early_ref.at[:, pl.ds(start, size)] for start, size in lines]
    first_device = lax.axis_index("tm") == 0

    @pl.when(first_device)
    def _():
        lax.fori_loop(0, 2, lambda t, _: frame(*own, 0, t), None)

    @pl.when(jnp.logical_not(first_device))
    def _():
        lax.fori_loop(0, 2, lambda t, _: frame(*sent, t, t), None)

    lax.fori_loop(0, frames, lambda t, _: frame(*own, t, t + 2), None)
    load.wait()
    inner = (height + 2) * breadth

    def one(t, carry):
        out = conv_frame(a_ref, e_ref, w_ref, t) + offset_ref[...]
        hidden_ref[t] = out.reshape(hidden_ref.shape[1:])
        return fold(out[breadth : inner - breadth], *carry)

    zero = jnp.zeros((1, channels), F32)
    mean, squares, _ = lax.fori_loop(0, frames, one, (zero, zero, jnp.float32(0)))
    row = pack(mean, squares, float(frames * height * breadth))
    packed_ref[...] = jnp.broadcast_to(row[None], packed_ref.shape)


def second_body(
    features_ref,
    own_ref,
    early_ref,
    stats_ref,
    gain_ref,
    bias_ref,
    offset_ref,
    w_hbm,
    out_hbm,
    w_ref,
    a_ref,
    c_ref,
    out_ref,
    sem,
    out_sem,
):
    load = pltpu.make_async_copy(w_hbm, w_ref, sem)
    load.start()
    frames, height, breadth, channels = features_ref.shape
    norm = norm_of(
        stats_ref, frames * height * breadth * (channels // G), gain_ref, bias_ref
    )
    top, bottom, leftmost, rightmost = within()
    tall = height + 2
    line = lax.broadcasted_iota(jnp.int32, (2 * EDGE, 1), 0)
    i_of = line % EDGE
    edges = jnp.where(line < EDGE, leftmost, rightmost)
    edges = edges * jnp.where(i_of == 0, top, jnp.where(i_of == tall - 1, bottom, 1.0))

    def frame(source, s, t):
        sides = source[s, pl.ds(tall, 2 * EDGE // LINE)].reshape(2 * EDGE, channels)
        c_ref[...] = active(sides, norm) * edges
        for i in range(tall):
            y = active(source[s, i], norm)
            if i == 0:
                y = y * top
            elif i == tall - 1:
                y = y * bottom
            put(a_ref, t, i, y, c_ref[pl.ds(i, 1)], c_ref[pl.ds(EDGE + i, 1)])

    first_device = lax.axis_index("tm") == 0

    @pl.when(first_device)
    def _():
        lax.fori_loop(0, 2, lambda t, _: frame(own_ref, 0, t), None)

    @pl.when(jnp.logical_not(first_device))
    def _():
        lax.fori_loop(0, 2, lambda t, _: frame(early_ref, t, t), None)

    lax.fori_loop(0, frames, lambda t, _: frame(own_ref, t, t + 2), None)
    load.wait()
    cells = height * breadth
    target = lax.broadcasted_iota(jnp.int32, (2 * cells, cells), 0)
    source = lax.broadcasted_iota(jnp.int32, (2 * cells, cells), 1)
    twice = (target // 2 == source).astype(BF16)

    def one(t, carry):
        out = conv_frame(a_ref, None, w_ref, t) + offset_ref[...]
        blended = (features_ref[t].astype(F32).reshape(cells, channels) + out).astype(BF16)
        wide = jnp.dot(twice, blended, preferred_element_type=F32).astype(BF16)
        wide = wide.reshape(height, 2 * breadth, channels)
        out_ref[t, :, 0] = wide
        out_ref[t, :, 1] = wide
        pltpu.make_async_copy(out_ref.at[t], out_hbm.at[t], out_sem.at[t]).start()
        return carry

    lax.fori_loop(0, frames, one, 0)
    for t in range(frames):
        pltpu.make_async_copy(out_ref.at[t], out_hbm.at[t], out_sem.at[t]).wait()


VMEM = pl.BlockSpec(memory_space=pltpu.VMEM)
HBM = pl.BlockSpec(memory_space=pltpu.HBM)
PARAMS = pltpu.CompilerParams(vmem_limit_bytes=40 * 2**20)


def shifted(x, axis, by):
    size = lax.axis_size(axis)
    return lax.ppermute(x, axis, [(i, (i + by) % size) for i in range(size)])


def everyone(rows):
    return lax.all_to_all(rows, AXES, 0, 0).reshape(rows.shape[0], LANES)


def local(
    features,
    first_gain,
    first_bias,
    first_kernel,
    first_offset,
    second_gain,
    second_bias,
    second_kernel,
    second_offset,
):
    frames, height, breadth, channels = features.shape
    tall = height + 2
    rows_out = jax.ShapeDtypeStruct((lax.axis_size(AXES), 1, LANES), F32)
    columns_out = jax.ShapeDtypeStruct((frames, 2, height, channels), BF16)
    border_out = jax.ShapeDtypeStruct((frames, 3, breadth, channels), BF16)
    hidden_lines = tall + 2 * EDGE // LINE

    def flat(v):
        return v.reshape(1, channels)

    def weights(kernel):
        return kernel.reshape(9, 3 * channels, channels)

    to_left, to_right = pl.pallas_call(
        columns_kernel,
        out_shape=(columns_out, columns_out),
        in_specs=[VMEM],
        out_specs=(VMEM, VMEM),
        compiler_params=PARAMS,
    )(features)
    right = shifted(to_left, "col", -1)
    left = shifted(to_right, "col", 1)
    stats = pl.pallas_call(
        stats_kernel,
        out_shape=rows_out,
        in_specs=[VMEM],
        out_specs=VMEM,
        compiler_params=PARAMS,
    )(features)
    to_above, to_below = pl.pallas_call(
        rows_kernel,
        out_shape=(border_out, border_out),
        in_specs=[VMEM] * 3,
        out_specs=(VMEM, VMEM),
        compiler_params=PARAMS,
    )(features, left, right)
    below = shifted(to_above, "row", -1)
    above = shifted(to_below, "row", 1)
    tail = jnp.concatenate([x[-2:] for x in (features, above, below, left, right)], axis=1)
    tail, stats = lax.optimization_barrier((tail, stats))
    early = shifted(tail, "tm", 1)
    stats = everyone(stats)
    hidden, packed = pl.pallas_call(
        first_body,
        out_shape=(
            jax.ShapeDtypeStruct((frames, hidden_lines, breadth, channels), F32),
            rows_out,
        ),
        in_specs=[VMEM] * 10 + [HBM],
        out_specs=(VMEM, VMEM),
        scratch_shapes=[
            pltpu.VMEM((9, 3 * channels, channels), BF16),
            pltpu.VMEM((3, frames + 2, height + 4, breadth, channels), BF16),
            pltpu.VMEM((3, frames + 2, 2 * EDGE, 3 * channels), BF16),
            pltpu.VMEM((6, EDGE + 8, channels), F32),
            pltpu.SemaphoreType.DMA,
        ],
        compiler_params=PARAMS,
    )(
        features,
        above,
        below,
        left,
        right,
        early,
        stats,
        flat(first_gain),
        flat(first_bias),
        flat(first_offset),
        weights(first_kernel),
    )
    early = shifted(hidden[-2:], "tm", 1)
    stats = everyone(packed)
    out = pl.pallas_call(
        second_body,
        out_shape=jax.ShapeDtypeStruct((frames, height, 2, 2 * breadth, channels), BF16),
        in_specs=[VMEM] * 7 + [HBM],
        out_specs=HBM,
        scratch_shapes=[
            pltpu.VMEM((9, 3 * channels, channels), BF16),
            pltpu.VMEM((3, frames + 2, tall, breadth, channels), BF16),
            pltpu.VMEM((2 * EDGE, channels), F32),
            pltpu.VMEM((frames, height, 2, 2 * breadth, channels), BF16),
            pltpu.SemaphoreType.DMA,
            pltpu.SemaphoreType.DMA((frames,)),
        ],
        compiler_params=PARAMS,
    )(
        features,
        hidden,
        early,
        stats,
        flat(second_gain),
        flat(second_bias),
        flat(second_offset),
        weights(second_kernel),
    )
    return out.reshape(frames, 2 * height, 2 * breadth, channels)


def solution(mesh):
    placed = (P("tm", "row", "col", None), P(), P(), P(), P(), P(), P(), P(), P())
    return jax.shard_map(
        local, mesh=mesh, in_specs=placed, out_specs=P("tm", "row", "col", None), check_vma=False
    )
```

```python
import functools

import jax
import jax.numpy as jnp
from jax import lax
from jax.experimental import pallas as pl
from jax.experimental.pallas import tpu as pltpu
from jax.sharding import PartitionSpec as P

G = 32
EPSILON = 1e-06
LANES = 128
F32 = jnp.float32
BF16 = jnp.bfloat16
AXES = ("tm", "row", "col")
LINE = 16
EDGE = 24


def picked(x, chosen):
    high = x.astype(BF16).astype(F32)
    rest = x - high
    middle = rest.astype(BF16).astype(F32)
    low = rest - middle
    stacked = jnp.concatenate([high, middle, low, jnp.zeros((13, x.shape[1]), F32)], axis=0)
    return jnp.sum(
        jnp.dot(stacked.astype(BF16), chosen, preferred_element_type=F32), axis=0, keepdims=True
    )


def lanes_of(channels, channels_last):
    shape = (LANES, 2 * channels) if channels_last else (2 * channels, LANES)
    channel = lax.broadcasted_iota(jnp.int32, shape, 1 if channels_last else 0)
    lane = lax.broadcasted_iota(jnp.int32, shape, 0 if channels_last else 1)
    return (channel // (channels // G) == lane).astype(BF16)


def fold(x, mean, squares, seen):
    n = float(x.shape[0])
    own = jnp.sum(x, axis=0, keepdims=True) / n
    apart = x - own
    spread = jnp.sum(apart * apart, axis=0, keepdims=True)
    both = seen + n
    gap = own - mean
    return mean + gap * (n / both), squares + spread + gap * gap * (seen * n / both), both


def pack(mean, squares, count):
    channels = mean.shape[-1]
    per = channels // G
    one = lax.broadcasted_iota(jnp.int32, (channels, channels), 0) // per
    other = lax.broadcasted_iota(jnp.int32, (channels, channels), 1) // per
    grouped = picked(mean, (one == other).astype(BF16)) / per
    apart = grouped - mean
    total = squares + count * apart * apart
    return picked(jnp.concatenate([mean / per, total], axis=1), lanes_of(channels, False))


def merge(rows, count):
    summed = jnp.sum(rows, axis=0, keepdims=True)
    average = summed / rows.shape[0]
    apart = rows - average
    spread = count * jnp.sum(apart * apart, axis=0, keepdims=True)
    lane = lax.broadcasted_iota(jnp.int32, (1, LANES), 1)
    total = jnp.where(lane < 2 * G, summed + pltpu.roll(spread, G, 1), 0.0)
    return jnp.where(lane < G, average, total)


def norm_of(stats_ref, group, gain_ref, bias_ref):
    rows = stats_ref[...]
    channels = gain_ref.shape[-1]
    wide = picked(merge(rows, float(group)), lanes_of(channels, True))
    variance = wide[:, channels:] / float(group * rows.shape[0])
    scale = lax.rsqrt(variance + EPSILON) * gain_ref[...]
    return wide[:, :channels], 0.5 * scale, 0.5 * bias_ref[...]


def active(x, norm):
    mean, half_scale, half_bias = norm
    half = (x.astype(F32) - mean) * half_scale + half_bias
    return half * jnp.tanh(half) + half


def within():
    def unless(axis, where):
        return jnp.where(lax.axis_index(axis) == where, 0.0, 1.0).astype(F32)

    return (
        unless("row", 0),
        unless("row", lax.axis_size("row") - 1),
        unless("col", 0),
        unless("col", lax.axis_size("col") - 1),
    )


def columns_kernel(x_ref, to_left_ref, to_right_ref):
    frames, height, breadth, channels = x_ref.shape
    cells = height * breadth
    target = lax.broadcasted_iota(jnp.int32, (4 * height, cells), 0)
    source = lax.broadcasted_iota(jnp.int32, (4 * height, cells), 1)
    which = target // height
    column = jnp.where(which < 2, which, which + (breadth - 4))
    chosen = (source == (target % height) * breadth + column).astype(BF16)
    for t in range(frames):
        got = jnp.dot(
            chosen, x_ref[t].reshape(cells, channels), preferred_element_type=F32
        ).astype(BF16)
        got = got.reshape(4, height, channels)
        to_left_ref[t] = got[:2]
        to_right_ref[t] = got[2:]


def stats_kernel(x_ref, o_ref):
    frames, height, breadth, channels = x_ref.shape
    carry = (jnp.zeros((1, channels), F32), jnp.zeros((1, channels), F32), 0.0)
    for t in range(frames):
        carry = fold(x_ref[t].astype(F32).reshape(height * breadth, channels), *carry)
    row = pack(carry[0], carry[1], float(frames * height * breadth))
    o_ref[...] = jnp.broadcast_to(row[None], o_ref.shape)


def rows_kernel(x_ref, left_ref, right_ref, to_above_ref, to_below_ref):
    frames, height, breadth, channels = x_ref.shape
    for t in range(frames):
        corners = [
            ref[t, k].astype(F32) for ref in (left_ref, right_ref) for k in range(2)
        ]
        for ref, start in ((to_above_ref, 0), (to_below_ref, height - 2)):
            ref[t, 0] = x_ref[t, start]
            ref[t, 1] = x_ref[t, start + 1]
            line = [c[start : start + 2] for c in corners]
            line.append(jnp.zeros((LINE - 8, channels), F32))
            ref[t, 2] = jnp.concatenate(line, axis=0).astype(BF16)


def put(a_ref, t, i, y, left, right):
    a_ref[0, t, i] = jnp.concatenate([left, y[:-1]], axis=0).astype(BF16)
    a_ref[1, t, i] = y.astype(BF16)
    a_ref[2, t, i] = jnp.concatenate([y[1:], right], axis=0).astype(BF16)


def conv_frame(a_ref, e_ref, w_ref, t):
    rows, breadth, channels = a_ref.shape[2] - 2, a_ref.shape[3], a_ref.shape[4]
    total = None
    for a in range(3):
        for b in range(3):
            window = jnp.concatenate(
                [
                    a_ref[c, t + a, pl.ds(b, rows)].reshape(rows * breadth, channels)
                    for c in range(3)
                ],
                axis=1,
            )
            if e_ref is not None:
                window = jnp.concatenate([window, e_ref[b, t + a]], axis=0)
            part = jnp.dot(window, w_ref[3 * a + b], preferred_element_type=F32)
            total = part if total is None else total + part
    return total


def first_body(
    own_ref,
    above_ref,
    below_ref,
    left_ref,
    right_ref,
    early_ref,
    stats_ref,
    gain_ref,
    bias_ref,
    offset_ref,
    w_ref,
    hidden_ref,
    packed_ref,
    a_ref,
    e_ref,
    c_ref,
):
    frames, height, breadth, channels = own_ref.shape
    norm = norm_of(
        stats_ref, frames * height * breadth * (channels // G), gain_ref, bias_ref
    )
    top, bottom, leftmost, rightmost = within()
    tall = height + 4

    def frame(center, above, below, left, right, s, t):
        upper = active(above[s, 2], norm) * top
        lower = active(below[s, 2], norm) * bottom
        for k in range(4):
            side = leftmost if k < 2 else rightmost
            x = left[s, k] if k < 2 else right[s, k - 2]
            c_ref[k, pl.ds(0, 2)] = upper[2 * k : 2 * k + 2] * side
            c_ref[k, pl.ds(2, height)] = active(x, norm) * side
            c_ref[k, pl.ds(2 + height, 2)] = lower[2 * k : 2 * k + 2] * side
        for i in range(tall):
            if i < 2:
                y = active(above[s, i], norm) * top
            elif i >= height + 2:
                y = active(below[s, i - height - 2], norm) * bottom
            else:
                y = active(center[s, i - 2], norm)
            put(a_ref, t, i, y, c_ref[1, pl.ds(i, 1)], c_ref[2, pl.ds(i, 1)])
            c_ref[4, pl.ds(i, 1)] = y[:1]
            c_ref[5, pl.ds(i, 1)] = y[breadth - 1 :]
        for b in range(3):
            for c, (near, far) in enumerate(((0, 5), (1, 2), (4, 3))):
                both = jnp.concatenate(
                    [c_ref[near, pl.ds(b, EDGE)], c_ref[far, pl.ds(b, EDGE)]], axis=0
                )
                e_ref[b, t, :, pl.ds(c * channels, channels)] = both.astype(BF16)

    c_ref[...] = jnp.zeros_like(c_ref)
    own = (own_ref, above_ref, below_ref, left_ref, right_ref)
    lines = [(0, height), (height, 3), (height + 3, 3), (height + 6, 2), (height + 8, 2)]
    sent = [early_ref.at[:, pl.ds(start, size)] for start, size in lines]
    first_device = lax.axis_index("tm") == 0

    @pl.when(first_device)
    def _():
        lax.fori_loop(0, 2, lambda t, _: frame(*own, 0, t), None)

    @pl.when(jnp.logical_not(first_device))
    def _():
        lax.fori_loop(0, 2, lambda t, _: frame(*sent, t, t), None)

    frame(*own, 0, 2)
    inner = (height + 2) * breadth

    def one(t, carry):
        out = conv_frame(a_ref, e_ref, w_ref, t) + offset_ref[...]
        hidden_ref[t] = out.reshape(hidden_ref.shape[1:])
        return fold(out[breadth : inner - breadth], *carry)

    carry = (jnp.zeros((1, channels), F32), jnp.zeros((1, channels), F32), 0.0)
    for t in range(frames):
        if t + 1 < frames:
            frame(*own, t + 1, t + 3)
        carry = one(t, carry)
    mean, squares, _ = carry
    row = pack(mean, squares, float(frames * height * breadth))
    packed_ref[...] = jnp.broadcast_to(row[None], packed_ref.shape)


def second_body(
    features_ref,
    own_ref,
    early_ref,
    stats_ref,
    gain_ref,
    bias_ref,
    offset_ref,
    w_ref,
    out_hbm,
    a_ref,
    c_ref,
    out_ref,
    u_ref,
    out_sem,
):
    frames, height, breadth, channels = features_ref.shape
    norm = norm_of(
        stats_ref, frames * height * breadth * (channels // G), gain_ref, bias_ref
    )
    top, bottom, leftmost, rightmost = within()
    tall = height + 2
    line = lax.broadcasted_iota(jnp.int32, (2 * EDGE, 1), 0)
    i_of = line % EDGE
    edges = jnp.where(line < EDGE, leftmost, rightmost)
    edges = edges * jnp.where(i_of == 0, top, jnp.where(i_of == tall - 1, bottom, 1.0))

    def frame(source, s, t):
        sides = source[s, pl.ds(tall, 2 * EDGE // LINE)].reshape(2 * EDGE, channels)
        c_ref[...] = active(sides, norm) * edges
        for i in range(tall):
            y = active(source[s, i], norm)
            if i == 0:
                y = y * top
            elif i == tall - 1:
                y = y * bottom
            put(a_ref, t, i, y, c_ref[pl.ds(i, 1)], c_ref[pl.ds(EDGE + i, 1)])

    first_device = lax.axis_index("tm") == 0

    @pl.when(first_device)
    def _():
        lax.fori_loop(0, 2, lambda t, _: frame(own_ref, 0, t), None)

    @pl.when(jnp.logical_not(first_device))
    def _():
        lax.fori_loop(0, 2, lambda t, _: frame(early_ref, t, t), None)

    frame(own_ref, 0, 2)
    cells = height * breadth

    def one(t, carry):
        out = conv_frame(a_ref, None, w_ref, t) + offset_ref[...]
        blended = (features_ref[t].astype(F32).reshape(cells, channels) + out)
        for k in range(channels // LANES):
            half = blended[:, k * LANES : (k + 1) * LANES]
            u_ref[k, pl.ds(0, cells, stride=2), :] = half
            u_ref[k, pl.ds(1, cells, stride=2), :] = half
        wide = jnp.concatenate([u_ref[k] for k in range(channels // LANES)], axis=1)
        wide = wide.astype(BF16).reshape(height, 2 * breadth, channels)
        out_ref[t, :, 0] = wide
        out_ref[t, :, 1] = wide
        pltpu.make_async_copy(out_ref.at[t], out_hbm.at[t], out_sem.at[t]).start()
        return carry

    for t in range(frames):
        if t + 1 < frames:
            frame(own_ref, t + 1, t + 3)
        one(t, 0)
    for t in range(frames):
        pltpu.make_async_copy(out_ref.at[t], out_hbm.at[t], out_sem.at[t]).wait()


VMEM = pl.BlockSpec(memory_space=pltpu.VMEM)
HBM = pl.BlockSpec(memory_space=pltpu.HBM)
PARAMS = pltpu.CompilerParams(vmem_limit_bytes=40 * 2**20)


def shifted(x, axis, by):
    size = lax.axis_size(axis)
    return lax.ppermute(x, axis, [(i, (i + by) % size) for i in range(size)])


def everyone(rows):
    return lax.all_to_all(rows, AXES, 0, 0).reshape(rows.shape[0], LANES)


def local(
    features,
    first_gain,
    first_bias,
    first_kernel,
    first_offset,
    second_gain,
    second_bias,
    second_kernel,
    second_offset,
):
    frames, height, breadth, channels = features.shape
    tall = height + 2
    rows_out = jax.ShapeDtypeStruct((lax.axis_size(AXES), 1, LANES), F32)
    columns_out = jax.ShapeDtypeStruct((frames, 2, height, channels), BF16)
    border_out = jax.ShapeDtypeStruct((frames, 3, breadth, channels), BF16)
    hidden_lines = tall + 2 * EDGE // LINE

    def flat(v):
        return v.reshape(1, channels)

    def weights(kernel):
        return kernel.reshape(9, 3 * channels, channels)

    to_left, to_right = pl.pallas_call(
        columns_kernel,
        out_shape=(columns_out, columns_out),
        in_specs=[VMEM],
        out_specs=(VMEM, VMEM),
        compiler_params=PARAMS,
    )(features)
    right = shifted(to_left, "col", -1)
    left = shifted(to_right, "col", 1)
    stats = pl.pallas_call(
        stats_kernel,
        out_shape=rows_out,
        in_specs=[VMEM],
        out_specs=VMEM,
        compiler_params=PARAMS,
    )(features)
    to_above, to_below = pl.pallas_call(
        rows_kernel,
        out_shape=(border_out, border_out),
        in_specs=[VMEM] * 3,
        out_specs=(VMEM, VMEM),
        compiler_params=PARAMS,
    )(features, left, right)
    below = shifted(to_above, "row", -1)
    above = shifted(to_below, "row", 1)
    tail = jnp.concatenate([x[-2:] for x in (features, above, below, left, right)], axis=1)
    tail, stats = lax.optimization_barrier((tail, stats))
    early = shifted(tail, "tm", 1)
    stats = everyone(stats)
    hidden, packed = pl.pallas_call(
        first_body,
        out_shape=(
            jax.ShapeDtypeStruct((frames, hidden_lines, breadth, channels), F32),
            rows_out,
        ),
        in_specs=[VMEM] * 11,
        out_specs=(VMEM, VMEM),
        scratch_shapes=[
            pltpu.VMEM((3, frames + 2, height + 4, breadth, channels), BF16),
            pltpu.VMEM((3, frames + 2, 2 * EDGE, 3 * channels), BF16),
            pltpu.VMEM((6, EDGE + 8, channels), F32),
        ],
        compiler_params=PARAMS,
    )(
        features,
        above,
        below,
        left,
        right,
        early,
        stats,
        flat(first_gain),
        flat(first_bias),
        flat(first_offset),
        weights(first_kernel),
    )
    early = shifted(hidden[-2:], "tm", 1)
    stats = everyone(packed)
    out = pl.pallas_call(
        second_body,
        out_shape=jax.ShapeDtypeStruct((frames, height, 2, 2 * breadth, channels), BF16),
        in_specs=[VMEM] * 8,
        out_specs=HBM,
        scratch_shapes=[
            pltpu.VMEM((3, frames + 2, tall, breadth, channels), BF16),
            pltpu.VMEM((2 * EDGE, channels), F32),
            pltpu.VMEM((frames, height, 2, 2 * breadth, channels), BF16),
            pltpu.VMEM((channels // LANES, 2 * height * breadth, LANES), F32),
            pltpu.SemaphoreType.DMA((frames,)),
        ],
        compiler_params=PARAMS,
    )(
        features,
        hidden,
        early,
        stats,
        flat(second_gain),
        flat(second_bias),
        flat(second_offset),
        weights(second_kernel),
    )
    return out.reshape(frames, 2 * height, 2 * breadth, channels)


def solution(mesh):
    placed = (P("tm", "row", "col", None), P(), P(), P(), P(), P(), P(), P(), P())
    return jax.shard_map(
        local, mesh=mesh, in_specs=placed, out_specs=P("tm", "row", "col", None), check_vma=False
    )
```

```python
import functools

import jax
import jax.numpy as jnp
from jax import lax
from jax.experimental import pallas as pl
from jax.experimental.pallas import tpu as pltpu
from jax.sharding import PartitionSpec as P

G = 32
EPSILON = 1e-06
LANES = 128
F32 = jnp.float32
BF16 = jnp.bfloat16
ROW = ("y", "core")
LINE = 16
EDGE = 24


def picked(x, chosen):
    high = x.astype(BF16).astype(F32)
    rest = x - high
    middle = rest.astype(BF16).astype(F32)
    low = rest - middle
    stacked = jnp.concatenate([high, middle, low, jnp.zeros((13, x.shape[1]), F32)], axis=0)
    return jnp.sum(
        jnp.dot(stacked.astype(BF16), chosen, preferred_element_type=F32), axis=0, keepdims=True
    )


def lanes_of(channels, channels_last):
    shape = (LANES, 2 * channels) if channels_last else (2 * channels, LANES)
    channel = lax.broadcasted_iota(jnp.int32, shape, 1 if channels_last else 0)
    lane = lax.broadcasted_iota(jnp.int32, shape, 0 if channels_last else 1)
    return (channel // (channels // G) == lane).astype(BF16)


def fold(x, mean, squares, seen):
    n = float(x.shape[0])
    own = jnp.sum(x, axis=0, keepdims=True) / n
    apart = x - own
    spread = jnp.sum(apart * apart, axis=0, keepdims=True)
    both = seen + n
    gap = own - mean
    return mean + gap * (n / both), squares + spread + gap * gap * (seen * n / both), both


def pack(mean, squares, count):
    channels = mean.shape[-1]
    per = channels // G
    one = lax.broadcasted_iota(jnp.int32, (channels, channels), 0) // per
    other = lax.broadcasted_iota(jnp.int32, (channels, channels), 1) // per
    grouped = picked(mean, (one == other).astype(BF16)) / per
    apart = grouped - mean
    total = squares + count * apart * apart
    return picked(jnp.concatenate([mean / per, total], axis=1), lanes_of(channels, False))


def merge(rows, count):
    summed = jnp.sum(rows, axis=0, keepdims=True)
    average = summed / rows.shape[0]
    apart = rows - average
    spread = count * jnp.sum(apart * apart, axis=0, keepdims=True)
    lane = lax.broadcasted_iota(jnp.int32, (1, LANES), 1)
    total = jnp.where(lane < 2 * G, summed + pltpu.roll(spread, G, 1), 0.0)
    return jnp.where(lane < G, average, total)


def join_kernel(count, own_ref, other_ref, o_ref):
    row = merge(jnp.concatenate([own_ref[0], other_ref[0]], axis=0), count)
    o_ref[...] = jnp.broadcast_to(row[None], o_ref.shape)


def norm_of(stats_ref, group, gain_ref, bias_ref):
    rows = stats_ref[...]
    channels = gain_ref.shape[-1]
    wide = picked(merge(rows, float(group)), lanes_of(channels, True))
    variance = wide[:, channels:] / float(group * rows.shape[0])
    scale = lax.rsqrt(variance + EPSILON) * gain_ref[...]
    return wide[:, :channels], 0.5 * scale, 0.5 * bias_ref[...]


def active(x, norm):
    mean, half_scale, half_bias = norm
    half = (x.astype(F32) - mean) * half_scale + half_bias
    return half * jnp.tanh(half) + half


def within():
    def place(axis):
        if axis != ROW:
            return lax.axis_index(axis)
        return lax.axis_index("y") * lax.axis_size("core") + lax.axis_index("core")

    def unless(axis, where):
        return jnp.where(place(axis) == where, 0.0, 1.0).astype(F32)

    return (
        unless(ROW, 0),
        unless(ROW, lax.axis_size(ROW) - 1),
        unless("col", 0),
        unless("col", lax.axis_size("col") - 1),
    )


def columns_kernel(x_ref, to_left_ref, to_right_ref):
    frames, height, breadth, channels = x_ref.shape
    cells = height * breadth
    target = lax.broadcasted_iota(jnp.int32, (4 * height, cells), 0)
    source = lax.broadcasted_iota(jnp.int32, (4 * height, cells), 1)
    which = target // height
    column = jnp.where(which < 2, which, which + (breadth - 4))
    chosen = (source == (target % height) * breadth + column).astype(BF16)
    for t in range(frames):
        got = jnp.dot(
            chosen, x_ref[t].reshape(cells, channels), preferred_element_type=F32
        ).astype(BF16)
        got = got.reshape(4, height, channels)
        to_left_ref[t] = got[:2]
        to_right_ref[t] = got[2:]


def stats_kernel(x_ref, o_ref):
    frames, height, breadth, channels = x_ref.shape
    carry = (jnp.zeros((1, channels), F32), jnp.zeros((1, channels), F32), 0.0)
    for t in range(frames):
        carry = fold(x_ref[t].astype(F32).reshape(height * breadth, channels), *carry)
    row = pack(carry[0], carry[1], float(frames * height * breadth))
    o_ref[...] = jnp.broadcast_to(row[None], o_ref.shape)


def rows_kernel(x_ref, left_ref, right_ref, to_above_ref, to_below_ref):
    frames, height, breadth, channels = x_ref.shape
    for t in range(frames):
        corners = [
            ref[t, k].astype(F32) for ref in (left_ref, right_ref) for k in range(2)
        ]
        for ref, start in ((to_above_ref, 0), (to_below_ref, height - 2)):
            ref[t, 0] = x_ref[t, start]
            ref[t, 1] = x_ref[t, start + 1]
            line = [c[start : start + 2] for c in corners]
            line.append(jnp.zeros((LINE - 8, channels), F32))
            ref[t, 2] = jnp.concatenate(line, axis=0).astype(BF16)


def put(a_ref, t, i, y, left, right):
    a_ref[0, t, i] = jnp.concatenate([left, y[:-1]], axis=0).astype(BF16)
    a_ref[1, t, i] = y.astype(BF16)
    a_ref[2, t, i] = jnp.concatenate([y[1:], right], axis=0).astype(BF16)


def conv_frame(a_ref, e_ref, w_ref, t):
    rows, breadth, channels = a_ref.shape[2] - 2, a_ref.shape[3], a_ref.shape[4]
    total = None
    for a in range(3):
        for b in range(3):
            window = jnp.concatenate(
                [
                    a_ref[c, t + a, pl.ds(b, rows)].reshape(rows * breadth, channels)
                    for c in range(3)
                ],
                axis=1,
            )
            if e_ref is not None:
                window = jnp.concatenate([window, e_ref[b, t + a]], axis=0)
            part = jnp.dot(window, w_ref[3 * a + b], preferred_element_type=F32)
            total = part if total is None else total + part
    return total


def first_body(
    share,
    own_ref,
    above_ref,
    below_ref,
    left_ref,
    right_ref,
    early_ref,
    stats_ref,
    gain_ref,
    bias_ref,
    offset_ref,
    w_ref,
    hidden_ref,
    packed_ref,
    a_ref,
    e_ref,
    c_ref,
):
    frames, height, breadth, channels = own_ref.shape
    group = frames * height * breadth * (channels // G)
    norm = norm_of(stats_ref, share * group, gain_ref, bias_ref)
    top, bottom, leftmost, rightmost = within()
    tall = height + 4

    def frame(center, above, below, left, right, s, t):
        upper = active(above[s, 2], norm) * top
        lower = active(below[s, 2], norm) * bottom
        for k in range(4):
            side = leftmost if k < 2 else rightmost
            x = left[s, k] if k < 2 else right[s, k - 2]
            c_ref[k, pl.ds(0, 2)] = upper[2 * k : 2 * k + 2] * side
            c_ref[k, pl.ds(2, height)] = active(x, norm) * side
            c_ref[k, pl.ds(2 + height, 2)] = lower[2 * k : 2 * k + 2] * side
        for i in range(tall):
            if i < 2:
                y = active(above[s, i], norm) * top
            elif i >= height + 2:
                y = active(below[s, i - height - 2], norm) * bottom
            else:
                y = active(center[s, i - 2], norm)
            put(a_ref, t, i, y, c_ref[1, pl.ds(i, 1)], c_ref[2, pl.ds(i, 1)])
            c_ref[4, pl.ds(i, 1)] = y[:1]
            c_ref[5, pl.ds(i, 1)] = y[breadth - 1 :]
        for b in range(3):
            for c, (near, far) in enumerate(((0, 5), (1, 2), (4, 3))):
                both = jnp.concatenate(
                    [c_ref[near, pl.ds(b, EDGE)], c_ref[far, pl.ds(b, EDGE)]], axis=0
                )
                e_ref[b, t, :, pl.ds(c * channels, channels)] = both.astype(BF16)

    c_ref[...] = jnp.zeros_like(c_ref)
    own = (own_ref, above_ref, below_ref, left_ref, right_ref)
    lines = [(0, height), (height, 3), (height + 3, 3), (height + 6, 2), (height + 8, 2)]
    sent = [early_ref.at[:, pl.ds(start, size)] for start, size in lines]
    first_device = lax.axis_index("tm") == 0

    @pl.when(first_device)
    def _():
        lax.fori_loop(0, 2, lambda t, _: frame(*own, 0, t), None)

    @pl.when(jnp.logical_not(first_device))
    def _():
        lax.fori_loop(0, 2, lambda t, _: frame(*sent, t, t), None)

    frame(*own, 0, 2)
    inner = (height + 2) * breadth

    def one(t, carry):
        out = conv_frame(a_ref, e_ref, w_ref, t) + offset_ref[...]
        hidden_ref[t] = out.reshape(hidden_ref.shape[1:])
        return fold(out[breadth : inner - breadth], *carry)

    carry = (jnp.zeros((1, channels), F32), jnp.zeros((1, channels), F32), 0.0)
    for t in range(frames):
        if t + 1 < frames:
            frame(*own, t + 1, t + 3)
        carry = one(t, carry)
    mean, squares, _ = carry
    row = pack(mean, squares, float(frames * height * breadth))
    packed_ref[...] = jnp.broadcast_to(row[None], packed_ref.shape)


def second_body(
    share,
    features_ref,
    own_ref,
    early_ref,
    stats_ref,
    gain_ref,
    bias_ref,
    offset_ref,
    w_ref,
    out_hbm,
    a_ref,
    c_ref,
    out_ref,
    u_ref,
    out_sem,
):
    frames, height, breadth, channels = features_ref.shape
    group = frames * height * breadth * (channels // G)
    norm = norm_of(stats_ref, share * group, gain_ref, bias_ref)
    top, bottom, leftmost, rightmost = within()
    tall = height + 2
    line = lax.broadcasted_iota(jnp.int32, (2 * EDGE, 1), 0)
    i_of = line % EDGE
    edges = jnp.where(line < EDGE, leftmost, rightmost)
    edges = edges * jnp.where(i_of == 0, top, jnp.where(i_of == tall - 1, bottom, 1.0))

    def frame(source, s, t):
        sides = source[s, pl.ds(tall, 2 * EDGE // LINE)].reshape(2 * EDGE, channels)
        c_ref[...] = active(sides, norm) * edges
        for i in range(tall):
            y = active(source[s, i], norm)
            if i == 0:
                y = y * top
            elif i == tall - 1:
                y = y * bottom
            put(a_ref, t, i, y, c_ref[pl.ds(i, 1)], c_ref[pl.ds(EDGE + i, 1)])

    first_device = lax.axis_index("tm") == 0

    @pl.when(first_device)
    def _():
        lax.fori_loop(0, 2, lambda t, _: frame(own_ref, 0, t), None)

    @pl.when(jnp.logical_not(first_device))
    def _():
        lax.fori_loop(0, 2, lambda t, _: frame(early_ref, t, t), None)

    frame(own_ref, 0, 2)
    cells = height * breadth

    def one(t, carry):
        out = conv_frame(a_ref, None, w_ref, t) + offset_ref[...]
        blended = (features_ref[t].astype(F32).reshape(cells, channels) + out)
        for k in range(channels // LANES):
            half = blended[:, k * LANES : (k + 1) * LANES]
            u_ref[k, pl.ds(0, cells, stride=2), :] = half
            u_ref[k, pl.ds(1, cells, stride=2), :] = half
        wide = jnp.concatenate([u_ref[k] for k in range(channels // LANES)], axis=1)
        wide = wide.astype(BF16).reshape(height, 2 * breadth, channels)
        out_ref[t, :, 0] = wide
        out_ref[t, :, 1] = wide
        pltpu.make_async_copy(out_ref.at[t], out_hbm.at[t], out_sem.at[t]).start()
        return carry

    for t in range(frames):
        if t + 1 < frames:
            frame(own_ref, t + 1, t + 3)
        one(t, 0)
    for t in range(frames):
        pltpu.make_async_copy(out_ref.at[t], out_hbm.at[t], out_sem.at[t]).wait()


VMEM = pl.BlockSpec(memory_space=pltpu.VMEM)
HBM = pl.BlockSpec(memory_space=pltpu.HBM)
PARAMS = pltpu.CompilerParams(vmem_limit_bytes=40 * 2**20)


def shifted(x, axis, by):
    size = lax.axis_size(axis)
    return lax.ppermute(x, axis, [(i, (i + by) % size) for i in range(size)])


def swapped(x, axis, bits):
    size = lax.axis_size(axis)
    return lax.ppermute(x, axis, [(i, i ^ bits) for i in range(size) if i ^ bits < size])


def joined(own, other, count, copies):
    return pl.pallas_call(
        functools.partial(join_kernel, float(count)),
        out_shape=jax.ShapeDtypeStruct((copies, 1, LANES), F32),
        in_specs=[VMEM] * 2,
        out_specs=VMEM,
        compiler_params=PARAMS,
    )(own, other)


def everyone(rows, axes):
    return lax.all_to_all(rows, axes, 0, 0).reshape(rows.shape[0], LANES)


def local(
    features,
    first_gain,
    first_bias,
    first_kernel,
    first_offset,
    second_gain,
    second_bias,
    second_kernel,
    second_offset,
):
    frames, height, breadth, channels = features.shape
    tall = height + 2
    group = frames * height * breadth * (channels // G)
    row_out = jax.ShapeDtypeStruct((1, 1, LANES), F32)
    columns_out = jax.ShapeDtypeStruct((frames, 2, height, channels), BF16)
    border_out = jax.ShapeDtypeStruct((frames, 3, breadth, channels), BF16)
    hidden_lines = tall + 2 * EDGE // LINE

    def flat(v):
        return v.reshape(1, channels)

    def weights(kernel):
        return kernel.reshape(9, 3 * channels, channels)

    to_left, to_right = pl.pallas_call(
        columns_kernel,
        out_shape=(columns_out, columns_out),
        in_specs=[VMEM],
        out_specs=(VMEM, VMEM),
        compiler_params=PARAMS,
    )(features)
    right = shifted(to_left, "col", -1)
    left = shifted(to_right, "col", 1)
    stats = pl.pallas_call(
        stats_kernel,
        out_shape=row_out,
        in_specs=[VMEM],
        out_specs=VMEM,
        compiler_params=PARAMS,
    )(features)
    other = swapped(stats, "core", 1)
    to_above, to_below = pl.pallas_call(
        rows_kernel,
        out_shape=(border_out, border_out),
        in_specs=[VMEM] * 3,
        out_specs=(VMEM, VMEM),
        compiler_params=PARAMS,
    )(features, left, right)
    below = shifted(to_above, ROW, -1)
    above = shifted(to_below, ROW, 1)
    tail = jnp.concatenate([x[-2:] for x in (features, above, below, left, right)], axis=1)
    chips = ("tm", "y", "col")
    stats = joined(stats, other, group, lax.axis_size(chips))
    tail, stats = lax.optimization_barrier((tail, stats))
    early = shifted(tail, "tm", 1)
    stats = everyone(stats, chips)
    hidden, packed = pl.pallas_call(
        functools.partial(first_body, lax.axis_size("core")),
        out_shape=(
            jax.ShapeDtypeStruct((frames, hidden_lines, breadth, channels), F32),
            row_out,
        ),
        in_specs=[VMEM] * 11,
        out_specs=(VMEM, VMEM),
        scratch_shapes=[
            pltpu.VMEM((3, frames + 2, height + 4, breadth, channels), BF16),
            pltpu.VMEM((3, frames + 2, 2 * EDGE, 3 * channels), BF16),
            pltpu.VMEM((6, EDGE + 8, channels), F32),
        ],
        compiler_params=PARAMS,
    )(
        features,
        above,
        below,
        left,
        right,
        early,
        stats,
        flat(first_gain),
        flat(first_bias),
        flat(first_offset),
        weights(first_kernel),
    )
    other = swapped(packed, "core", 1)
    early = shifted(hidden[-2:], "tm", 1)
    stats = everyone(joined(packed, other, group, lax.axis_size(chips)), chips)
    out = pl.pallas_call(
        functools.partial(second_body, lax.axis_size("core")),
        out_shape=jax.ShapeDtypeStruct((frames, height, 2, 2 * breadth, channels), BF16),
        in_specs=[VMEM] * 8,
        out_specs=HBM,
        scratch_shapes=[
            pltpu.VMEM((3, frames + 2, tall, breadth, channels), BF16),
            pltpu.VMEM((2 * EDGE, channels), F32),
            pltpu.VMEM((frames, height, 2, 2 * breadth, channels), BF16),
            pltpu.VMEM((channels // LANES, 2 * height * breadth, LANES), F32),
            pltpu.SemaphoreType.DMA((frames,)),
        ],
        compiler_params=PARAMS,
    )(
        features,
        hidden,
        early,
        stats,
        flat(second_gain),
        flat(second_bias),
        flat(second_offset),
        weights(second_kernel),
    )
    return out.reshape(frames, 2 * height, 2 * breadth, channels)


def solution(mesh):
    frames, rows, columns = mesh.devices.shape
    split = jax.sharding.Mesh(
        mesh.devices.reshape(frames, rows // 2, 2, columns), ("tm", "y", "core", "col")
    )
    cut = P("tm", ROW, "col", None)
    placed = (cut, P(), P(), P(), P(), P(), P(), P(), P())
    return jax.shard_map(local, mesh=split, in_specs=placed, out_specs=cut, check_vma=False)
```

```python
import functools

import jax
import jax.numpy as jnp
from jax import lax
from jax.experimental import pallas as pl
from jax.experimental.pallas import tpu as pltpu
from jax.sharding import PartitionSpec as P

G = 32
EPSILON = 1e-06
LANES = 128
F32 = jnp.float32
BF16 = jnp.bfloat16
ROW = ("y", "core")
LINE = 16
EDGE = 24


def picked(x, chosen):
    high = x.astype(BF16).astype(F32)
    rest = x - high
    middle = rest.astype(BF16).astype(F32)
    low = rest - middle
    stacked = jnp.concatenate([high, middle, low, jnp.zeros((13, x.shape[1]), F32)], axis=0)
    return jnp.sum(
        jnp.dot(stacked.astype(BF16), chosen, preferred_element_type=F32), axis=0, keepdims=True
    )


def lanes_of(channels, channels_last):
    shape = (LANES, 2 * channels) if channels_last else (2 * channels, LANES)
    channel = lax.broadcasted_iota(jnp.int32, shape, 1 if channels_last else 0)
    lane = lax.broadcasted_iota(jnp.int32, shape, 0 if channels_last else 1)
    return (channel // (channels // G) == lane).astype(BF16)


def fold(x, mean, squares, seen):
    n = float(x.shape[0])
    own = jnp.sum(x, axis=0, keepdims=True) / n
    apart = x - own
    spread = jnp.sum(apart * apart, axis=0, keepdims=True)
    both = seen + n
    gap = own - mean
    return mean + gap * (n / both), squares + spread + gap * gap * (seen * n / both), both


def pack(mean, squares, count):
    channels = mean.shape[-1]
    per = channels // G
    one = lax.broadcasted_iota(jnp.int32, (channels, channels), 0) // per
    other = lax.broadcasted_iota(jnp.int32, (channels, channels), 1) // per
    grouped = picked(mean, (one == other).astype(BF16)) / per
    apart = grouped - mean
    total = squares + count * apart * apart
    return picked(jnp.concatenate([mean / per, total], axis=1), lanes_of(channels, False))


def merge(rows, count):
    summed = jnp.sum(rows, axis=0, keepdims=True)
    average = summed / rows.shape[0]
    apart = rows - average
    spread = count * jnp.sum(apart * apart, axis=0, keepdims=True)
    lane = lax.broadcasted_iota(jnp.int32, (1, LANES), 1)
    total = jnp.where(lane < 2 * G, summed + pltpu.roll(spread, G, 1), 0.0)
    return jnp.where(lane < G, average, total)


def join_kernel(count, own_ref, other_ref, *refs):
    o_ref = refs[-1]
    row = merge(jnp.concatenate([own_ref[0], other_ref[0]], axis=0), count)
    o_ref[...] = jnp.broadcast_to(row[None], o_ref.shape)


def norm_of(stats_ref, group, gain_ref, bias_ref):
    rows = stats_ref[...]
    channels = gain_ref.shape[-1]
    wide = picked(merge(rows, float(group)), lanes_of(channels, True))
    variance = wide[:, channels:] / float(group * rows.shape[0])
    scale = lax.rsqrt(variance + EPSILON) * gain_ref[...]
    return wide[:, :channels], 0.5 * scale, 0.5 * bias_ref[...]


def active(x, norm):
    mean, half_scale, half_bias = norm
    half = (x.astype(F32) - mean) * half_scale + half_bias
    return half * jnp.tanh(half) + half


def within():
    def place(axis):
        if axis != ROW:
            return lax.axis_index(axis)
        return lax.axis_index("y") * lax.axis_size("core") + lax.axis_index("core")

    def unless(axis, where):
        return jnp.where(place(axis) == where, 0.0, 1.0).astype(F32)

    return (
        unless(ROW, 0),
        unless(ROW, lax.axis_size(ROW) - 1),
        unless("col", 0),
        unless("col", lax.axis_size("col") - 1),
    )


def columns_kernel(x_ref, to_left_ref, to_right_ref, rows_ref):
    frames, height, breadth, channels = x_ref.shape
    cells = height * breadth
    target = lax.broadcasted_iota(jnp.int32, (4 * height, cells), 0)
    source = lax.broadcasted_iota(jnp.int32, (4 * height, cells), 1)
    which = target // height
    column = jnp.where(which < 2, which, which + (breadth - 4))
    chosen = (source == (target % height) * breadth + column).astype(BF16)
    for t in range(frames):
        got = jnp.dot(
            chosen, x_ref[t].reshape(cells, channels), preferred_element_type=F32
        ).astype(BF16)
        got = got.reshape(4, height, channels)
        to_left_ref[t] = got[:2]
        to_right_ref[t] = got[2:]
        rows_ref[t, pl.ds(0, 2)] = x_ref[t, pl.ds(0, 2)]
        rows_ref[t, pl.ds(2, 2)] = x_ref[t, pl.ds(height - 2, 2)]


def stats_kernel(x_ref, o_ref):
    frames, height, breadth, channels = x_ref.shape
    carry = (jnp.zeros((1, channels), F32), jnp.zeros((1, channels), F32), 0.0)
    for t in range(frames):
        carry = fold(x_ref[t].astype(F32).reshape(height * breadth, channels), *carry)
    row = pack(carry[0], carry[1], float(frames * height * breadth))
    o_ref[...] = jnp.broadcast_to(row[None], o_ref.shape)


def rows_kernel(rows_ref, left_ref, right_ref, to_above_ref, to_below_ref):
    frames, _, height, channels = left_ref.shape
    for t in range(frames):
        corners = [
            ref[t, k].astype(F32) for ref in (left_ref, right_ref) for k in range(2)
        ]
        for k, (ref, start) in enumerate(((to_above_ref, 0), (to_below_ref, height - 2))):
            ref[t, pl.ds(0, 2)] = rows_ref[t, pl.ds(2 * k, 2)]
            line = [c[start : start + 2] for c in corners]
            line.append(jnp.zeros((LINE - 8, channels), F32))
            ref[t, 2] = jnp.concatenate(line, axis=0).astype(BF16)


def put(a_ref, t, i, y, left, right):
    a_ref[0, t, i] = jnp.concatenate([left, y[:-1]], axis=0).astype(BF16)
    a_ref[1, t, i] = y.astype(BF16)
    a_ref[2, t, i] = jnp.concatenate([y[1:], right], axis=0).astype(BF16)


def conv_frame(a_ref, e_ref, w_ref, t):
    rows, breadth, channels = a_ref.shape[2] - 2, a_ref.shape[3], a_ref.shape[4]
    total = None
    for a in range(3):
        for b in range(3):
            window = jnp.concatenate(
                [
                    a_ref[c, t + a, pl.ds(b, rows)].reshape(rows * breadth, channels)
                    for c in range(3)
                ],
                axis=1,
            )
            if e_ref is not None:
                window = jnp.concatenate([window, e_ref[b, t + a]], axis=0)
            part = jnp.dot(window, w_ref[3 * a + b], preferred_element_type=F32)
            total = part if total is None else total + part
    return total


def first_body(
    share,
    own_ref,
    above_ref,
    below_ref,
    left_ref,
    right_ref,
    early_ref,
    stats_ref,
    gain_ref,
    bias_ref,
    offset_ref,
    w_ref,
    hidden_ref,
    packed_ref,
    a_ref,
    e_ref,
    c_ref,
):
    frames, height, breadth, channels = own_ref.shape
    group = frames * height * breadth * (channels // G)
    norm = norm_of(stats_ref, share * group, gain_ref, bias_ref)
    top, bottom, leftmost, rightmost = within()
    tall = height + 4

    def frame(center, above, below, left, right, s, t):
        upper = active(above[s, 2], norm) * top
        lower = active(below[s, 2], norm) * bottom
        for k in range(4):
            side = leftmost if k < 2 else rightmost
            x = left[s, k] if k < 2 else right[s, k - 2]
            c_ref[k, pl.ds(0, 2)] = upper[2 * k : 2 * k + 2] * side
            c_ref[k, pl.ds(2, height)] = active(x, norm) * side
            c_ref[k, pl.ds(2 + height, 2)] = lower[2 * k : 2 * k + 2] * side
        for i in range(tall):
            if i < 2:
                y = active(above[s, i], norm) * top
            elif i >= height + 2:
                y = active(below[s, i - height - 2], norm) * bottom
            else:
                y = active(center[s, i - 2], norm)
            put(a_ref, t, i, y, c_ref[1, pl.ds(i, 1)], c_ref[2, pl.ds(i, 1)])
            c_ref[4, pl.ds(i, 1)] = y[:1]
            c_ref[5, pl.ds(i, 1)] = y[breadth - 1 :]
        for b in range(3):
            for c, (near, far) in enumerate(((0, 5), (1, 2), (4, 3))):
                both = jnp.concatenate(
                    [c_ref[near, pl.ds(b, EDGE)], c_ref[far, pl.ds(b, EDGE)]], axis=0
                )
                e_ref[b, t, :, pl.ds(c * channels, channels)] = both.astype(BF16)

    c_ref[...] = jnp.zeros_like(c_ref)
    own = (own_ref, above_ref, below_ref, left_ref, right_ref)
    lines = [(0, height), (height, 3), (height + 3, 3), (height + 6, 2), (height + 8, 2)]
    sent = [early_ref.at[:, pl.ds(start, size)] for start, size in lines]
    first_device = lax.axis_index("tm") == 0

    @pl.when(first_device)
    def _():
        lax.fori_loop(0, 2, lambda t, _: frame(*own, 0, t), None)

    @pl.when(jnp.logical_not(first_device))
    def _():
        lax.fori_loop(0, 2, lambda t, _: frame(*sent, t, t), None)

    frame(*own, 0, 2)
    inner = (height + 2) * breadth

    def one(t, carry):
        out = conv_frame(a_ref, e_ref, w_ref, t) + offset_ref[...]
        hidden_ref[t] = out.reshape(hidden_ref.shape[1:])
        return fold(out[breadth : inner - breadth], *carry)

    carry = (jnp.zeros((1, channels), F32), jnp.zeros((1, channels), F32), 0.0)
    for t in range(frames):
        if t + 1 < frames:
            frame(*own, t + 1, t + 3)
        carry = one(t, carry)
    mean, squares, _ = carry
    row = pack(mean, squares, float(frames * height * breadth))
    packed_ref[...] = jnp.broadcast_to(row[None], packed_ref.shape)


def second_body(
    share,
    features_ref,
    own_ref,
    early_ref,
    stats_ref,
    gain_ref,
    bias_ref,
    offset_ref,
    w_ref,
    out_hbm,
    a_ref,
    c_ref,
    out_ref,
    u_ref,
    out_sem,
):
    frames, height, breadth, channels = features_ref.shape
    group = frames * height * breadth * (channels // G)
    norm = norm_of(stats_ref, share * group, gain_ref, bias_ref)
    top, bottom, leftmost, rightmost = within()
    tall = height + 2
    line = lax.broadcasted_iota(jnp.int32, (2 * EDGE, 1), 0)
    i_of = line % EDGE
    edges = jnp.where(line < EDGE, leftmost, rightmost)
    edges = edges * jnp.where(i_of == 0, top, jnp.where(i_of == tall - 1, bottom, 1.0))

    def frame(source, s, t):
        sides = source[s, pl.ds(tall, 2 * EDGE // LINE)].reshape(2 * EDGE, channels)
        c_ref[...] = active(sides, norm) * edges
        for i in range(tall):
            y = active(source[s, i], norm)
            if i == 0:
                y = y * top
            elif i == tall - 1:
                y = y * bottom
            put(a_ref, t, i, y, c_ref[pl.ds(i, 1)], c_ref[pl.ds(EDGE + i, 1)])

    first_device = lax.axis_index("tm") == 0

    @pl.when(first_device)
    def _():
        lax.fori_loop(0, 2, lambda t, _: frame(own_ref, 0, t), None)

    @pl.when(jnp.logical_not(first_device))
    def _():
        lax.fori_loop(0, 2, lambda t, _: frame(early_ref, t, t), None)

    frame(own_ref, 0, 2)
    cells = height * breadth

    def one(t, carry):
        out = conv_frame(a_ref, None, w_ref, t) + offset_ref[...]
        blended = (features_ref[t].astype(F32).reshape(cells, channels) + out)
        for k in range(channels // LANES):
            half = blended[:, k * LANES : (k + 1) * LANES]
            u_ref[k, pl.ds(0, cells, stride=2), :] = half
            u_ref[k, pl.ds(1, cells, stride=2), :] = half
        wide = jnp.concatenate([u_ref[k] for k in range(channels // LANES)], axis=1)
        wide = wide.astype(BF16).reshape(height, 2 * breadth, channels)
        out_ref[t, :, 0] = wide
        out_ref[t, :, 1] = wide
        pltpu.make_async_copy(out_ref.at[t], out_hbm.at[t], out_sem.at[t]).start()
        return carry

    for t in range(frames):
        if t + 1 < frames:
            frame(own_ref, t + 1, t + 3)
        one(t, 0)
    for t in range(frames):
        pltpu.make_async_copy(out_ref.at[t], out_hbm.at[t], out_sem.at[t]).wait()


VMEM = pl.BlockSpec(memory_space=pltpu.VMEM)
HBM = pl.BlockSpec(memory_space=pltpu.HBM)
PARAMS = pltpu.CompilerParams(vmem_limit_bytes=8 * 2**20)
LARGE = pltpu.CompilerParams(vmem_limit_bytes=16 * 2**20)


def shifted(x, axis, by):
    size = lax.axis_size(axis)
    return lax.ppermute(x, axis, [(i, (i + by) % size) for i in range(size)])


def swapped(x, axis, bits):
    size = lax.axis_size(axis)
    return lax.ppermute(x, axis, [(i, i ^ bits) for i in range(size) if i ^ bits < size])


def joined(own, other, count, copies, *wanted):
    return pl.pallas_call(
        functools.partial(join_kernel, float(count)),
        out_shape=jax.ShapeDtypeStruct((copies, 1, LANES), F32),
        in_specs=[VMEM] * (2 + len(wanted)),
        out_specs=VMEM,
        compiler_params=PARAMS,
    )(own, other, *wanted)


def everyone(rows, axes):
    return lax.all_to_all(rows, axes, 0, 0).reshape(rows.shape[0], LANES)


def local(
    features,
    first_gain,
    first_bias,
    first_kernel,
    first_offset,
    second_gain,
    second_bias,
    second_kernel,
    second_offset,
):
    frames, height, breadth, channels = features.shape
    tall = height + 2
    group = frames * height * breadth * (channels // G)
    row_out = jax.ShapeDtypeStruct((1, 1, LANES), F32)
    columns_out = jax.ShapeDtypeStruct((frames, 2, height, channels), BF16)
    border_out = jax.ShapeDtypeStruct((frames, 3, breadth, channels), BF16)
    hidden_lines = tall + 2 * EDGE // LINE

    def flat(v):
        return v.reshape(1, channels)

    def weights(kernel):
        return kernel.reshape(9, 3 * channels, channels)

    to_left, to_right, outer = pl.pallas_call(
        columns_kernel,
        out_shape=(
            columns_out,
            columns_out,
            jax.ShapeDtypeStruct((frames, 4, breadth, channels), BF16),
        ),
        in_specs=[VMEM],
        out_specs=(VMEM,) * 3,
        compiler_params=PARAMS,
    )(features)
    right = shifted(to_left, "col", -1)
    left = shifted(to_right, "col", 1)
    stats = pl.pallas_call(
        stats_kernel,
        out_shape=row_out,
        in_specs=[VMEM],
        out_specs=VMEM,
        compiler_params=PARAMS,
    )(features)
    stats = joined(stats, swapped(stats, "core", 1), group, 1)
    other = swapped(stats, "tm", 1)
    to_above, to_below = pl.pallas_call(
        rows_kernel,
        out_shape=(border_out, border_out),
        in_specs=[VMEM] * 3,
        out_specs=(VMEM, VMEM),
        compiler_params=PARAMS,
    )(outer, left, right)
    below = shifted(to_above, ROW, -1)
    above = shifted(to_below, ROW, 1)
    stats, _ = lax.optimization_barrier((stats, to_above))
    stats = joined(stats, other, 2 * group, 1)
    planes = ("y", "col")
    near = weights(first_kernel)
    stats = joined(stats, swapped(stats, "tm", 3), 4 * group, lax.axis_size(planes), near)
    tail = jnp.concatenate([x[-2:] for x in (features, above, below, left, right)], axis=1)
    tail, stats = lax.optimization_barrier((tail, stats))
    early = shifted(tail, "tm", 1)
    stats = everyone(stats, planes)
    hidden, packed = pl.pallas_call(
        functools.partial(first_body, lax.axis_size(("tm", "core"))),
        out_shape=(
            jax.ShapeDtypeStruct((frames, hidden_lines, breadth, channels), F32),
            row_out,
        ),
        in_specs=[VMEM] * 11,
        out_specs=(VMEM, VMEM),
        scratch_shapes=[
            pltpu.VMEM((3, frames + 2, height + 4, breadth, channels), BF16),
            pltpu.VMEM((3, frames + 2, 2 * EDGE, 3 * channels), BF16),
            pltpu.VMEM((6, EDGE + 8, channels), F32),
        ],
        compiler_params=LARGE,
    )(
        features,
        above,
        below,
        left,
        right,
        early,
        stats,
        flat(first_gain),
        flat(first_bias),
        flat(first_offset),
        near,
    )
    chips = ("tm", "y", "col")
    other = swapped(packed, "core", 1)
    early = shifted(hidden[-2:], "tm", 1)
    stats = everyone(joined(packed, other, group, lax.axis_size(chips)), chips)
    out = pl.pallas_call(
        functools.partial(second_body, lax.axis_size("core")),
        out_shape=jax.ShapeDtypeStruct((frames, height, 2, 2 * breadth, channels), BF16),
        in_specs=[VMEM] * 8,
        out_specs=HBM,
        scratch_shapes=[
            pltpu.VMEM((3, frames + 2, tall, breadth, channels), BF16),
            pltpu.VMEM((2 * EDGE, channels), F32),
            pltpu.VMEM((frames, height, 2, 2 * breadth, channels), BF16),
            pltpu.VMEM((channels // LANES, 2 * height * breadth, LANES), F32),
            pltpu.SemaphoreType.DMA((frames,)),
        ],
        compiler_params=LARGE,
    )(
        features,
        hidden,
        early,
        stats,
        flat(second_gain),
        flat(second_bias),
        flat(second_offset),
        weights(second_kernel),
    )
    return out.reshape(frames, 2 * height, 2 * breadth, channels)


def solution(mesh):
    frames, rows, columns = mesh.devices.shape
    split = jax.sharding.Mesh(
        mesh.devices.reshape(frames, rows // 2, 2, columns), ("tm", "y", "core", "col")
    )
    cut = P("tm", ROW, "col", None)
    placed = (cut, P(), P(), P(), P(), P(), P(), P(), P())
    return jax.shard_map(local, mesh=split, in_specs=placed, out_specs=cut, check_vma=False)
```

```python
import functools

import jax
import jax.numpy as jnp
from jax import lax
from jax.experimental import pallas as pl
from jax.experimental.pallas import tpu as pltpu
from jax.sharding import PartitionSpec as P

G = 32
EPSILON = 1e-06
LANES = 128
F32 = jnp.float32
BF16 = jnp.bfloat16
ROW = ("y", "core")
LINE = 16
EDGE = 24


def picked(x, chosen):
    high = x.astype(BF16).astype(F32)
    rest = x - high
    middle = rest.astype(BF16).astype(F32)
    low = rest - middle
    stacked = jnp.concatenate([high, middle, low, jnp.zeros((13, x.shape[1]), F32)], axis=0)
    return jnp.sum(
        jnp.dot(stacked.astype(BF16), chosen, preferred_element_type=F32), axis=0, keepdims=True
    )


def lanes_of(channels, channels_last):
    shape = (LANES, 2 * channels) if channels_last else (2 * channels, LANES)
    channel = lax.broadcasted_iota(jnp.int32, shape, 1 if channels_last else 0)
    lane = lax.broadcasted_iota(jnp.int32, shape, 0 if channels_last else 1)
    return (channel // (channels // G) == lane).astype(BF16)


def fold(x, mean, squares, seen):
    n = float(x.shape[0])
    own = jnp.sum(x, axis=0, keepdims=True) / n
    apart = x - own
    spread = jnp.sum(apart * apart, axis=0, keepdims=True)
    both = seen + n
    gap = own - mean
    return mean + gap * (n / both), squares + spread + gap * gap * (seen * n / both), both


def pack(mean, squares, count):
    channels = mean.shape[-1]
    per = channels // G
    one = lax.broadcasted_iota(jnp.int32, (channels, channels), 0) // per
    other = lax.broadcasted_iota(jnp.int32, (channels, channels), 1) // per
    grouped = picked(mean, (one == other).astype(BF16)) / per
    apart = grouped - mean
    total = squares + count * apart * apart
    return picked(jnp.concatenate([mean / per, total], axis=1), lanes_of(channels, False))


def merge(rows, count):
    summed = jnp.sum(rows, axis=0, keepdims=True)
    average = summed / rows.shape[0]
    apart = rows - average
    spread = count * jnp.sum(apart * apart, axis=0, keepdims=True)
    lane = lax.broadcasted_iota(jnp.int32, (1, LANES), 1)
    total = jnp.where(lane < 2 * G, summed + pltpu.roll(spread, G, 1), 0.0)
    return jnp.where(lane < G, average, total)


def join_kernel(count, own_ref, other_ref, *refs):
    o_ref = refs[-1]
    row = merge(jnp.concatenate([own_ref[0], other_ref[0]], axis=0), count)
    o_ref[...] = jnp.broadcast_to(row[None], o_ref.shape)


def norm_of(stats_ref, group, gain_ref, bias_ref):
    rows = stats_ref[...]
    channels = gain_ref.shape[-1]
    wide = picked(merge(rows, float(group)), lanes_of(channels, True))
    variance = wide[:, channels:] / float(group * rows.shape[0])
    scale = lax.rsqrt(variance + EPSILON) * gain_ref[...]
    return wide[:, :channels], 0.5 * scale, 0.5 * bias_ref[...]


def active(x, norm):
    mean, half_scale, half_bias = norm
    half = (x.astype(F32) - mean) * half_scale + half_bias
    return half * jnp.tanh(half) + half


def within():
    def place(axis):
        if axis != ROW:
            return lax.axis_index(axis)
        return lax.axis_index("y") * lax.axis_size("core") + lax.axis_index("core")

    def unless(axis, where):
        return jnp.where(place(axis) == where, 0.0, 1.0).astype(F32)

    return (
        unless(ROW, 0),
        unless(ROW, lax.axis_size(ROW) - 1),
        unless("col", 0),
        unless("col", lax.axis_size("col") - 1),
    )


def columns_kernel(x_ref, to_left_ref, to_right_ref, rows_ref, last_ref):
    frames, height, breadth, channels = x_ref.shape
    cells = height * breadth
    target = lax.broadcasted_iota(jnp.int32, (4 * height, cells), 0)
    source = lax.broadcasted_iota(jnp.int32, (4 * height, cells), 1)
    which = target // height
    column = jnp.where(which < 2, which, which + (breadth - 4))
    chosen = (source == (target % height) * breadth + column).astype(BF16)
    last_ref[...] = x_ref[pl.ds(frames - 2, 2)]
    for t in range(frames):
        got = jnp.dot(
            chosen, x_ref[t].reshape(cells, channels), preferred_element_type=F32
        ).astype(BF16)
        got = got.reshape(4, height, channels)
        to_left_ref[t] = got[:2]
        to_right_ref[t] = got[2:]
        rows_ref[t, pl.ds(0, 2)] = x_ref[t, pl.ds(0, 2)]
        rows_ref[t, pl.ds(2, 2)] = x_ref[t, pl.ds(height - 2, 2)]


def stats_kernel(x_ref, _, o_ref):
    frames, height, breadth, channels = x_ref.shape
    carry = (jnp.zeros((1, channels), F32), jnp.zeros((1, channels), F32), 0.0)
    for t in range(frames):
        carry = fold(x_ref[t].astype(F32).reshape(height * breadth, channels), *carry)
    row = pack(carry[0], carry[1], float(frames * height * breadth))
    o_ref[...] = jnp.broadcast_to(row[None], o_ref.shape)


def rows_kernel(rows_ref, left_ref, right_ref, to_above_ref, to_below_ref):
    frames, _, height, channels = left_ref.shape
    for t in range(frames):
        corners = [
            ref[t, k].astype(F32) for ref in (left_ref, right_ref) for k in range(2)
        ]
        for k, (ref, start) in enumerate(((to_above_ref, 0), (to_below_ref, height - 2))):
            ref[t, pl.ds(0, 2)] = rows_ref[t, pl.ds(2 * k, 2)]
            line = [c[start : start + 2] for c in corners]
            line.append(jnp.zeros((LINE - 8, channels), F32))
            ref[t, 2] = jnp.concatenate(line, axis=0).astype(BF16)


def put(a_ref, t, i, y, left, right):
    a_ref[0, t, i] = jnp.concatenate([left, y[:-1]], axis=0).astype(BF16)
    a_ref[1, t, i] = y.astype(BF16)
    a_ref[2, t, i] = jnp.concatenate([y[1:], right], axis=0).astype(BF16)


def conv_frame(a_ref, e_ref, w_ref, t):
    rows, breadth, channels = a_ref.shape[2] - 2, a_ref.shape[3], a_ref.shape[4]
    total = None
    for a in range(3):
        for b in range(3):
            window = jnp.concatenate(
                [
                    a_ref[c, t + a, pl.ds(b, rows)].reshape(rows * breadth, channels)
                    for c in range(3)
                ],
                axis=1,
            )
            if e_ref is not None:
                window = jnp.concatenate([window, e_ref[b, t + a]], axis=0)
            part = jnp.dot(window, w_ref[3 * a + b], preferred_element_type=F32)
            total = part if total is None else total + part
    return total


def first_body(
    share,
    own_ref,
    above_ref,
    below_ref,
    left_ref,
    right_ref,
    early_ref,
    stats_ref,
    gain_ref,
    bias_ref,
    offset_ref,
    w_ref,
    hidden_ref,
    packed_ref,
    a_ref,
    e_ref,
    c_ref,
):
    frames, height, breadth, channels = own_ref.shape
    group = frames * height * breadth * (channels // G)
    norm = norm_of(stats_ref, share * group, gain_ref, bias_ref)
    top, bottom, leftmost, rightmost = within()
    tall = height + 4

    def frame(center, above, below, left, right, s, t):
        upper = active(above[s, 2], norm) * top
        lower = active(below[s, 2], norm) * bottom
        for k in range(4):
            side = leftmost if k < 2 else rightmost
            x = left[s, k] if k < 2 else right[s, k - 2]
            c_ref[k, pl.ds(0, 2)] = upper[2 * k : 2 * k + 2] * side
            c_ref[k, pl.ds(2, height)] = active(x, norm) * side
            c_ref[k, pl.ds(2 + height, 2)] = lower[2 * k : 2 * k + 2] * side
        for i in range(tall):
            if i < 2:
                y = active(above[s, i], norm) * top
            elif i >= height + 2:
                y = active(below[s, i - height - 2], norm) * bottom
            else:
                y = active(center[s, i - 2], norm)
            put(a_ref, t, i, y, c_ref[1, pl.ds(i, 1)], c_ref[2, pl.ds(i, 1)])
            c_ref[4, pl.ds(i, 1)] = y[:1]
            c_ref[5, pl.ds(i, 1)] = y[breadth - 1 :]
        for b in range(3):
            for c, (near, far) in enumerate(((0, 5), (1, 2), (4, 3))):
                both = jnp.concatenate(
                    [c_ref[near, pl.ds(b, EDGE)], c_ref[far, pl.ds(b, EDGE)]], axis=0
                )
                e_ref[b, t, :, pl.ds(c * channels, channels)] = both.astype(BF16)

    c_ref[...] = jnp.zeros_like(c_ref)
    own = (own_ref, above_ref, below_ref, left_ref, right_ref)
    lines = [(0, height), (height, 3), (height + 3, 3), (height + 6, 2), (height + 8, 2)]
    sent = [early_ref.at[:, pl.ds(start, size)] for start, size in lines]
    first_device = lax.axis_index("tm") == 0

    @pl.when(first_device)
    def _():
        lax.fori_loop(0, 2, lambda t, _: frame(*own, 0, t), None)

    @pl.when(jnp.logical_not(first_device))
    def _():
        lax.fori_loop(0, 2, lambda t, _: frame(*sent, t, t), None)

    frame(*own, 0, 2)
    inner = (height + 2) * breadth

    def one(t, carry):
        out = conv_frame(a_ref, e_ref, w_ref, t) + offset_ref[...]
        hidden_ref[t] = out.reshape(hidden_ref.shape[1:])
        return fold(out[breadth : inner - breadth], *carry)

    carry = (jnp.zeros((1, channels), F32), jnp.zeros((1, channels), F32), 0.0)
    for t in range(frames):
        if t + 1 < frames:
            frame(*own, t + 1, t + 3)
        carry = one(t, carry)
    mean, squares, _ = carry
    row = pack(mean, squares, float(frames * height * breadth))
    packed_ref[...] = jnp.broadcast_to(row[None], packed_ref.shape)


def second_body(
    share,
    features_ref,
    own_ref,
    early_ref,
    stats_ref,
    gain_ref,
    bias_ref,
    offset_ref,
    w_ref,
    out_hbm,
    a_ref,
    c_ref,
    out_ref,
    u_ref,
    out_sem,
):
    frames, height, breadth, channels = features_ref.shape
    group = frames * height * breadth * (channels // G)
    norm = norm_of(stats_ref, share * group, gain_ref, bias_ref)
    top, bottom, leftmost, rightmost = within()
    tall = height + 2
    line = lax.broadcasted_iota(jnp.int32, (2 * EDGE, 1), 0)
    i_of = line % EDGE
    edges = jnp.where(line < EDGE, leftmost, rightmost)
    edges = edges * jnp.where(i_of == 0, top, jnp.where(i_of == tall - 1, bottom, 1.0))

    def frame(source, s, t):
        sides = source[s, pl.ds(tall, 2 * EDGE // LINE)].reshape(2 * EDGE, channels)
        c_ref[...] = active(sides, norm) * edges
        for i in range(tall):
            y = active(source[s, i], norm)
            if i == 0:
                y = y * top
            elif i == tall - 1:
                y = y * bottom
            put(a_ref, t, i, y, c_ref[pl.ds(i, 1)], c_ref[pl.ds(EDGE + i, 1)])

    first_device = lax.axis_index("tm") == 0

    @pl.when(first_device)
    def _():
        lax.fori_loop(0, 2, lambda t, _: frame(own_ref, 0, t), None)

    @pl.when(jnp.logical_not(first_device))
    def _():
        lax.fori_loop(0, 2, lambda t, _: frame(early_ref, t, t), None)

    frame(own_ref, 0, 2)
    cells = height * breadth

    def one(t, carry):
        out = conv_frame(a_ref, None, w_ref, t) + offset_ref[...]
        blended = (features_ref[t].astype(F32).reshape(cells, channels) + out)
        for k in range(channels // LANES):
            half = blended[:, k * LANES : (k + 1) * LANES]
            u_ref[k, pl.ds(0, cells, stride=2), :] = half
            u_ref[k, pl.ds(1, cells, stride=2), :] = half
        wide = jnp.concatenate([u_ref[k] for k in range(channels // LANES)], axis=1)
        wide = wide.astype(BF16).reshape(height, 2 * breadth, channels)
        out_ref[t, :, 0] = wide
        out_ref[t, :, 1] = wide
        pltpu.make_async_copy(out_ref.at[t], out_hbm.at[t], out_sem.at[t]).start()
        return carry

    for t in range(frames):
        if t + 1 < frames:
            frame(own_ref, t + 1, t + 3)
        one(t, 0)
    for t in range(frames):
        pltpu.make_async_copy(out_ref.at[t], out_hbm.at[t], out_sem.at[t]).wait()


VMEM = pl.BlockSpec(memory_space=pltpu.VMEM)
HBM = pl.BlockSpec(memory_space=pltpu.HBM)
PARAMS = pltpu.CompilerParams(vmem_limit_bytes=8 * 2**20)
LARGE = pltpu.CompilerParams(vmem_limit_bytes=16 * 2**20)


def shifted(x, axis, by):
    size = lax.axis_size(axis)
    return lax.ppermute(x, axis, [(i, (i + by) % size) for i in range(size)])


def swapped(x, axis, bits):
    size = lax.axis_size(axis)
    return lax.ppermute(x, axis, [(i, i ^ bits) for i in range(size) if i ^ bits < size])


def joined(own, other, count, copies, *wanted):
    return pl.pallas_call(
        functools.partial(join_kernel, float(count)),
        out_shape=jax.ShapeDtypeStruct((copies, 1, LANES), F32),
        in_specs=[VMEM] * (2 + len(wanted)),
        out_specs=VMEM,
        compiler_params=PARAMS,
    )(own, other, *wanted)


def everyone(rows, axes):
    return lax.all_to_all(rows, axes, 0, 0).reshape(rows.shape[0], LANES)


def local(
    features,
    first_gain,
    first_bias,
    first_kernel,
    first_offset,
    second_gain,
    second_bias,
    second_kernel,
    second_offset,
):
    frames, height, breadth, channels = features.shape
    tall = height + 2
    group = frames * height * breadth * (channels // G)
    row_out = jax.ShapeDtypeStruct((1, 1, LANES), F32)
    columns_out = jax.ShapeDtypeStruct((frames, 2, height, channels), BF16)
    border_out = jax.ShapeDtypeStruct((frames, 3, breadth, channels), BF16)
    hidden_lines = tall + 2 * EDGE // LINE

    def flat(v):
        return v.reshape(1, channels)

    def weights(kernel):
        return kernel.reshape(9, 3 * channels, channels)

    to_left, to_right, outer, last = pl.pallas_call(
        columns_kernel,
        out_shape=(
            columns_out,
            columns_out,
            jax.ShapeDtypeStruct((frames, 4, breadth, channels), BF16),
            jax.ShapeDtypeStruct((2, height, breadth, channels), BF16),
        ),
        in_specs=[VMEM],
        out_specs=(VMEM,) * 4,
        compiler_params=PARAMS,
    )(features)
    right = shifted(to_left, "col", -1)
    left = shifted(to_right, "col", 1)
    near = weights(first_kernel)
    stats = pl.pallas_call(
        stats_kernel,
        out_shape=row_out,
        in_specs=[VMEM] * 2,
        out_specs=VMEM,
        compiler_params=PARAMS,
    )(features, near)
    other = swapped(stats, "core", 1)
    left, right, stats = lax.optimization_barrier((left, right, stats))
    to_above, to_below = pl.pallas_call(
        rows_kernel,
        out_shape=(border_out, border_out),
        in_specs=[VMEM] * 3,
        out_specs=(VMEM, VMEM),
        compiler_params=PARAMS,
    )(outer, left, right)
    below = shifted(to_above, ROW, -1)
    above = shifted(to_below, ROW, 1)
    other, to_above = lax.optimization_barrier((other, to_above))
    stats = joined(stats, other, group, 1)
    stats = joined(stats, swapped(stats, "tm", 1), 2 * group, 1)
    planes = ("y", "col")
    stats = joined(stats, swapped(stats, "tm", 3), 4 * group, lax.axis_size(planes))
    tail = jnp.concatenate([x[-2:] for x in (last, above, below, left, right)], axis=1)
    tail, stats = lax.optimization_barrier((tail, stats))
    early = shifted(tail, "tm", 1)
    stats = everyone(stats, planes)
    hidden, packed = pl.pallas_call(
        functools.partial(first_body, lax.axis_size(("tm", "core"))),
        out_shape=(
            jax.ShapeDtypeStruct((frames, hidden_lines, breadth, channels), F32),
            row_out,
        ),
        in_specs=[VMEM] * 11,
        out_specs=(VMEM, VMEM),
        scratch_shapes=[
            pltpu.VMEM((3, frames + 2, height + 4, breadth, channels), BF16),
            pltpu.VMEM((3, frames + 2, 2 * EDGE, 3 * channels), BF16),
            pltpu.VMEM((6, EDGE + 8, channels), F32),
        ],
        compiler_params=LARGE,
    )(
        features,
        above,
        below,
        left,
        right,
        early,
        stats,
        flat(first_gain),
        flat(first_bias),
        flat(first_offset),
        near,
    )
    chips = ("tm", "y", "col")
    other = swapped(packed, "core", 1)
    early = shifted(hidden[-2:], "tm", 1)
    stats = everyone(joined(packed, other, group, lax.axis_size(chips)), chips)
    out = pl.pallas_call(
        functools.partial(second_body, lax.axis_size("core")),
        out_shape=jax.ShapeDtypeStruct((frames, height, 2, 2 * breadth, channels), BF16),
        in_specs=[VMEM] * 8,
        out_specs=HBM,
        scratch_shapes=[
            pltpu.VMEM((3, frames + 2, tall, breadth, channels), BF16),
            pltpu.VMEM((2 * EDGE, channels), F32),
            pltpu.VMEM((frames, height, 2, 2 * breadth, channels), BF16),
            pltpu.VMEM((channels // LANES, 2 * height * breadth, LANES), F32),
            pltpu.SemaphoreType.DMA((frames,)),
        ],
        compiler_params=LARGE,
    )(
        features,
        hidden,
        early,
        stats,
        flat(second_gain),
        flat(second_bias),
        flat(second_offset),
        weights(second_kernel),
    )
    return out.reshape(frames, 2 * height, 2 * breadth, channels)


def solution(mesh):
    frames, rows, columns = mesh.devices.shape
    split = jax.sharding.Mesh(
        mesh.devices.reshape(frames, rows // 2, 2, columns), ("tm", "y", "core", "col")
    )
    cut = P("tm", ROW, "col", None)
    placed = (cut, P(), P(), P(), P(), P(), P(), P(), P())
    return jax.shard_map(local, mesh=split, in_specs=placed, out_specs=cut, check_vma=False)
```

```python
import functools

import jax
import jax.numpy as jnp
from jax import lax
from jax.experimental import pallas as pl
from jax.experimental.pallas import tpu as pltpu
from jax.sharding import PartitionSpec as P

G = 32
EPSILON = 1e-06
LANES = 128
F32 = jnp.float32
BF16 = jnp.bfloat16
TIME = ("half", "pair")
ROW = ("y", "core")
LINE = 16
EDGE = 24


def picked(x, chosen):
    high = x.astype(BF16).astype(F32)
    rest = x - high
    middle = rest.astype(BF16).astype(F32)
    low = rest - middle
    stacked = jnp.concatenate([high, middle, low, jnp.zeros((13, x.shape[1]), F32)], axis=0)
    return jnp.sum(
        jnp.dot(stacked.astype(BF16), chosen, preferred_element_type=F32), axis=0, keepdims=True
    )


def lanes_of(channels, channels_last):
    shape = (LANES, 2 * channels) if channels_last else (2 * channels, LANES)
    channel = lax.broadcasted_iota(jnp.int32, shape, 1 if channels_last else 0)
    lane = lax.broadcasted_iota(jnp.int32, shape, 0 if channels_last else 1)
    return (channel // (channels // G) == lane).astype(BF16)


def fold(x, mean, squares, seen):
    n = float(x.shape[0])
    own = jnp.sum(x, axis=0, keepdims=True) / n
    apart = x - own
    spread = jnp.sum(apart * apart, axis=0, keepdims=True)
    both = seen + n
    gap = own - mean
    return mean + gap * (n / both), squares + spread + gap * gap * (seen * n / both), both


def pack(mean, squares, count):
    channels = mean.shape[-1]
    per = channels // G
    one = lax.broadcasted_iota(jnp.int32, (channels, channels), 0) // per
    other = lax.broadcasted_iota(jnp.int32, (channels, channels), 1) // per
    grouped = picked(mean, (one == other).astype(BF16)) / per
    apart = grouped - mean
    total = squares + count * apart * apart
    return picked(jnp.concatenate([mean / per, total], axis=1), lanes_of(channels, False))


def merge(rows, count):
    summed = jnp.sum(rows, axis=0, keepdims=True)
    average = summed / rows.shape[0]
    apart = rows - average
    spread = count * jnp.sum(apart * apart, axis=0, keepdims=True)
    lane = lax.broadcasted_iota(jnp.int32, (1, LANES), 1)
    total = jnp.where(lane < 2 * G, summed + pltpu.roll(spread, G, 1), 0.0)
    return jnp.where(lane < G, average, total)


def join_kernel(count, own_ref, other_ref, *refs):
    o_ref = refs[-1]
    row = merge(jnp.concatenate([own_ref[0], other_ref[0]], axis=0), count)
    o_ref[...] = jnp.broadcast_to(row[None], o_ref.shape)


def norm_of(stats_ref, group, gain_ref, bias_ref):
    rows = stats_ref[...]
    channels = gain_ref.shape[-1]
    wide = picked(merge(rows, float(group)), lanes_of(channels, True))
    variance = wide[:, channels:] / float(group * rows.shape[0])
    scale = lax.rsqrt(variance + EPSILON) * gain_ref[...]
    return wide[:, :channels], 0.5 * scale, 0.5 * bias_ref[...]


def active(x, norm):
    mean, half_scale, half_bias = norm
    half = (x.astype(F32) - mean) * half_scale + half_bias
    return half * jnp.tanh(half) + half


def within():
    def place(axis):
        if axis != ROW:
            return lax.axis_index(axis)
        return lax.axis_index(ROW[0]) * lax.axis_size(ROW[1]) + lax.axis_index(ROW[1])

    def unless(axis, where):
        return jnp.where(place(axis) == where, 0.0, 1.0).astype(F32)

    return (
        unless(ROW, 0),
        unless(ROW, lax.axis_size(ROW) - 1),
        unless("col", 0),
        unless("col", lax.axis_size("col") - 1),
    )


def columns_kernel(x_ref, to_left_ref, to_right_ref, rows_ref, last_ref):
    frames, height, breadth, channels = x_ref.shape
    cells = height * breadth
    target = lax.broadcasted_iota(jnp.int32, (4 * height, cells), 0)
    source = lax.broadcasted_iota(jnp.int32, (4 * height, cells), 1)
    which = target // height
    column = jnp.where(which < 2, which, which + (breadth - 4))
    chosen = (source == (target % height) * breadth + column).astype(BF16)
    last_ref[...] = x_ref[pl.ds(frames - 2, 2)]
    for t in range(frames):
        got = jnp.dot(
            chosen, x_ref[t].reshape(cells, channels), preferred_element_type=F32
        ).astype(BF16)
        got = got.reshape(4, height, channels)
        to_left_ref[t] = got[:2]
        to_right_ref[t] = got[2:]
        rows_ref[t, pl.ds(0, 2)] = x_ref[t, pl.ds(0, 2)]
        rows_ref[t, pl.ds(2, 2)] = x_ref[t, pl.ds(height - 2, 2)]


def stats_kernel(x_ref, _, o_ref):
    frames, height, breadth, channels = x_ref.shape
    carry = (jnp.zeros((1, channels), F32), jnp.zeros((1, channels), F32), 0.0)
    for t in range(frames):
        carry = fold(x_ref[t].astype(F32).reshape(height * breadth, channels), *carry)
    row = pack(carry[0], carry[1], float(frames * height * breadth))
    o_ref[...] = jnp.broadcast_to(row[None], o_ref.shape)


def rows_kernel(rows_ref, left_ref, right_ref, to_above_ref, to_below_ref):
    frames, _, height, channels = left_ref.shape
    for t in range(frames):
        corners = [
            ref[t, k].astype(F32) for ref in (left_ref, right_ref) for k in range(2)
        ]
        for k, (ref, start) in enumerate(((to_above_ref, 0), (to_below_ref, height - 2))):
            ref[t, pl.ds(0, 2)] = rows_ref[t, pl.ds(2 * k, 2)]
            line = [c[start : start + 2] for c in corners]
            line.append(jnp.zeros((LINE - 8, channels), F32))
            ref[t, 2] = jnp.concatenate(line, axis=0).astype(BF16)


def put(a_ref, t, i, y, left, right):
    a_ref[0, t, i] = jnp.concatenate([left, y[:-1]], axis=0).astype(BF16)
    a_ref[1, t, i] = y.astype(BF16)
    a_ref[2, t, i] = jnp.concatenate([y[1:], right], axis=0).astype(BF16)


def conv_frame(a_ref, e_ref, w_ref, t):
    rows, breadth, channels = a_ref.shape[2] - 2, a_ref.shape[3], a_ref.shape[4]
    total = None
    for a in range(3):
        for b in range(3):
            window = jnp.concatenate(
                [
                    a_ref[c, t + a, pl.ds(b, rows)].reshape(rows * breadth, channels)
                    for c in range(3)
                ],
                axis=1,
            )
            if e_ref is not None:
                window = jnp.concatenate([window, e_ref[b, t + a]], axis=0)
            part = jnp.dot(window, w_ref[3 * a + b], preferred_element_type=F32)
            total = part if total is None else total + part
    return total


def first_body(
    share,
    own_ref,
    above_ref,
    below_ref,
    left_ref,
    right_ref,
    early_ref,
    stats_ref,
    gain_ref,
    bias_ref,
    offset_ref,
    w_ref,
    hidden_ref,
    packed_ref,
    a_ref,
    e_ref,
    c_ref,
):
    frames, height, breadth, channels = own_ref.shape
    group = frames * height * breadth * (channels // G)
    norm = norm_of(stats_ref, share * group, gain_ref, bias_ref)
    top, bottom, leftmost, rightmost = within()
    tall = height + 4

    def frame(center, above, below, left, right, s, t):
        upper = active(above[s, 2], norm) * top
        lower = active(below[s, 2], norm) * bottom
        for k in range(4):
            side = leftmost if k < 2 else rightmost
            x = left[s, k] if k < 2 else right[s, k - 2]
            c_ref[k, pl.ds(0, 2)] = upper[2 * k : 2 * k + 2] * side
            c_ref[k, pl.ds(2, height)] = active(x, norm) * side
            c_ref[k, pl.ds(2 + height, 2)] = lower[2 * k : 2 * k + 2] * side
        for i in range(tall):
            if i < 2:
                y = active(above[s, i], norm) * top
            elif i >= height + 2:
                y = active(below[s, i - height - 2], norm) * bottom
            else:
                y = active(center[s, i - 2], norm)
            put(a_ref, t, i, y, c_ref[1, pl.ds(i, 1)], c_ref[2, pl.ds(i, 1)])
            c_ref[4, pl.ds(i, 1)] = y[:1]
            c_ref[5, pl.ds(i, 1)] = y[breadth - 1 :]
        for b in range(3):
            for c, (near, far) in enumerate(((0, 5), (1, 2), (4, 3))):
                both = jnp.concatenate(
                    [c_ref[near, pl.ds(b, EDGE)], c_ref[far, pl.ds(b, EDGE)]], axis=0
                )
                e_ref[b, t, :, pl.ds(c * channels, channels)] = both.astype(BF16)

    c_ref[...] = jnp.zeros_like(c_ref)
    own = (own_ref, above_ref, below_ref, left_ref, right_ref)
    lines = [(0, height), (height, 3), (height + 3, 3), (height + 6, 2), (height + 8, 2)]
    sent = [early_ref.at[:, pl.ds(start, size)] for start, size in lines]
    first_device = lax.axis_index("half") + lax.axis_index("pair") == 0

    @pl.when(first_device)
    def _():
        lax.fori_loop(0, 2, lambda t, _: frame(*own, 0, t), None)

    @pl.when(jnp.logical_not(first_device))
    def _():
        lax.fori_loop(0, 2, lambda t, _: frame(*sent, t, t), None)

    frame(*own, 0, 2)
    inner = (height + 2) * breadth

    def one(t, carry):
        out = conv_frame(a_ref, e_ref, w_ref, t) + offset_ref[...]
        hidden_ref[t] = out.reshape(hidden_ref.shape[1:])
        return fold(out[breadth : inner - breadth], *carry)

    carry = (jnp.zeros((1, channels), F32), jnp.zeros((1, channels), F32), 0.0)
    for t in range(frames):
        if t + 1 < frames:
            frame(*own, t + 1, t + 3)
        carry = one(t, carry)
    mean, squares, _ = carry
    row = pack(mean, squares, float(frames * height * breadth))
    packed_ref[...] = jnp.broadcast_to(row[None], packed_ref.shape)


def second_body(
    share,
    features_ref,
    own_ref,
    early_ref,
    stats_ref,
    gain_ref,
    bias_ref,
    offset_ref,
    w_ref,
    out_hbm,
    a_ref,
    c_ref,
    out_ref,
    u_ref,
    out_sem,
):
    frames, height, breadth, channels = features_ref.shape
    group = frames * height * breadth * (channels // G)
    norm = norm_of(stats_ref, share * group, gain_ref, bias_ref)
    top, bottom, leftmost, rightmost = within()
    tall = height + 2
    line = lax.broadcasted_iota(jnp.int32, (2 * EDGE, 1), 0)
    i_of = line % EDGE
    edges = jnp.where(line < EDGE, leftmost, rightmost)
    edges = edges * jnp.where(i_of == 0, top, jnp.where(i_of == tall - 1, bottom, 1.0))

    def frame(source, s, t):
        sides = source[s, pl.ds(tall, 2 * EDGE // LINE)].reshape(2 * EDGE, channels)
        c_ref[...] = active(sides, norm) * edges
        for i in range(tall):
            y = active(source[s, i], norm)
            if i == 0:
                y = y * top
            elif i == tall - 1:
                y = y * bottom
            put(a_ref, t, i, y, c_ref[pl.ds(i, 1)], c_ref[pl.ds(EDGE + i, 1)])

    first_device = lax.axis_index("half") + lax.axis_index("pair") == 0

    @pl.when(first_device)
    def _():
        lax.fori_loop(0, 2, lambda t, _: frame(own_ref, 0, t), None)

    @pl.when(jnp.logical_not(first_device))
    def _():
        lax.fori_loop(0, 2, lambda t, _: frame(early_ref, t, t), None)

    frame(own_ref, 0, 2)
    cells = height * breadth

    def one(t, carry):
        out = conv_frame(a_ref, None, w_ref, t) + offset_ref[...]
        blended = (features_ref[t].astype(F32).reshape(cells, channels) + out)
        for k in range(channels // LANES):
            half = blended[:, k * LANES : (k + 1) * LANES]
            u_ref[k, pl.ds(0, cells, stride=2), :] = half
            u_ref[k, pl.ds(1, cells, stride=2), :] = half
        wide = jnp.concatenate([u_ref[k] for k in range(channels // LANES)], axis=1)
        wide = wide.astype(BF16).reshape(height, 2 * breadth, channels)
        out_ref[t, :, 0] = wide
        out_ref[t, :, 1] = wide
        pltpu.make_async_copy(out_ref.at[t], out_hbm.at[t], out_sem.at[t]).start()
        return carry

    for t in range(frames):
        if t + 1 < frames:
            frame(own_ref, t + 1, t + 3)
        one(t, 0)
    for t in range(frames):
        pltpu.make_async_copy(out_ref.at[t], out_hbm.at[t], out_sem.at[t]).wait()


VMEM = pl.BlockSpec(memory_space=pltpu.VMEM)
HBM = pl.BlockSpec(memory_space=pltpu.HBM)
PARAMS = pltpu.CompilerParams(vmem_limit_bytes=8 * 2**20)
LARGE = pltpu.CompilerParams(vmem_limit_bytes=16 * 2**20)


def shifted(x, axis, by):
    size = lax.axis_size(axis)
    return lax.ppermute(x, axis, [(i, (i + by) % size) for i in range(size)])


def swapped(x, axis, bits):
    size = lax.axis_size(axis)
    return lax.ppermute(x, axis, [(i, i ^ bits) for i in range(size) if i ^ bits < size])


def joined(own, other, count, copies, *wanted):
    return pl.pallas_call(
        functools.partial(join_kernel, float(count)),
        out_shape=jax.ShapeDtypeStruct((copies, 1, LANES), F32),
        in_specs=[VMEM] * (2 + len(wanted)),
        out_specs=VMEM,
        compiler_params=PARAMS,
    )(own, other, *wanted)


def everyone(rows, axes):
    return lax.all_to_all(rows, axes, 0, 0).reshape(rows.shape[0], LANES)


def local(
    features,
    first_gain,
    first_bias,
    first_kernel,
    first_offset,
    second_gain,
    second_bias,
    second_kernel,
    second_offset,
):
    frames, height, breadth, channels = features.shape
    tall = height + 2
    group = frames * height * breadth * (channels // G)
    row_out = jax.ShapeDtypeStruct((1, 1, LANES), F32)
    columns_out = jax.ShapeDtypeStruct((frames, 2, height, channels), BF16)
    border_out = jax.ShapeDtypeStruct((frames, 3, breadth, channels), BF16)
    hidden_lines = tall + 2 * EDGE // LINE

    def flat(v):
        return v.reshape(1, channels)

    def weights(kernel):
        return kernel.reshape(9, 3 * channels, channels)

    to_left, to_right, outer, last = pl.pallas_call(
        columns_kernel,
        out_shape=(
            columns_out,
            columns_out,
            jax.ShapeDtypeStruct((frames, 4, breadth, channels), BF16),
            jax.ShapeDtypeStruct((2, height, breadth, channels), BF16),
        ),
        in_specs=[VMEM],
        out_specs=(VMEM,) * 4,
        compiler_params=PARAMS,
    )(features)
    right = shifted(to_left, "col", -1)
    left = shifted(to_right, "col", 1)
    near = weights(first_kernel)
    stats = pl.pallas_call(
        stats_kernel,
        out_shape=row_out,
        in_specs=[VMEM] * 2,
        out_specs=VMEM,
        compiler_params=PARAMS,
    )(features, near)
    other = swapped(stats, "core", 1)
    left, right, stats = lax.optimization_barrier((left, right, stats))
    to_above, to_below = pl.pallas_call(
        rows_kernel,
        out_shape=(border_out, border_out),
        in_specs=[VMEM] * 3,
        out_specs=(VMEM, VMEM),
        compiler_params=PARAMS,
    )(outer, left, right)
    below = shifted(to_above, ROW, -1)
    above = shifted(to_below, ROW, 1)
    other, to_above = lax.optimization_barrier((other, to_above))
    stats = joined(stats, other, group, 1)
    rest = ("half", "y", "col")
    stats = joined(stats, swapped(stats, "pair", 1), 2 * group, lax.axis_size(rest))
    tail = jnp.concatenate([x[-2:] for x in (last, above, below, left, right)], axis=1)
    tail, stats = lax.optimization_barrier((tail, stats))
    early = shifted(tail, TIME, 1)
    stats = everyone(stats, rest)
    hidden, packed = pl.pallas_call(
        functools.partial(first_body, lax.axis_size(("pair", "core"))),
        out_shape=(
            jax.ShapeDtypeStruct((frames, hidden_lines, breadth, channels), F32),
            row_out,
        ),
        in_specs=[VMEM] * 11,
        out_specs=(VMEM, VMEM),
        scratch_shapes=[
            pltpu.VMEM((3, frames + 2, height + 4, breadth, channels), BF16),
            pltpu.VMEM((3, frames + 2, 2 * EDGE, 3 * channels), BF16),
            pltpu.VMEM((6, EDGE + 8, channels), F32),
        ],
        compiler_params=LARGE,
    )(
        features,
        above,
        below,
        left,
        right,
        early,
        stats,
        flat(first_gain),
        flat(first_bias),
        flat(first_offset),
        near,
    )
    chips = (*TIME, "y", "col")
    other = swapped(packed, "core", 1)
    early = shifted(hidden[-2:], TIME, 1)
    stats = everyone(joined(packed, other, group, lax.axis_size(chips)), chips)
    out = pl.pallas_call(
        functools.partial(second_body, lax.axis_size("core")),
        out_shape=jax.ShapeDtypeStruct((frames, height, 2, 2 * breadth, channels), BF16),
        in_specs=[VMEM] * 8,
        out_specs=HBM,
        scratch_shapes=[
            pltpu.VMEM((3, frames + 2, tall, breadth, channels), BF16),
            pltpu.VMEM((2 * EDGE, channels), F32),
            pltpu.VMEM((frames, height, 2, 2 * breadth, channels), BF16),
            pltpu.VMEM((channels // LANES, 2 * height * breadth, LANES), F32),
            pltpu.SemaphoreType.DMA((frames,)),
        ],
        compiler_params=LARGE,
    )(
        features,
        hidden,
        early,
        stats,
        flat(second_gain),
        flat(second_bias),
        flat(second_offset),
        weights(second_kernel),
    )
    return out.reshape(frames, 2 * height, 2 * breadth, channels)


def solution(mesh):
    frames, rows, columns = mesh.devices.shape
    split = jax.sharding.Mesh(
        mesh.devices.reshape(frames // 2, 2, rows // 2, 2, columns), (*TIME, *ROW, "col")
    )
    cut = P(TIME, ROW, "col", None)
    placed = (cut, P(), P(), P(), P(), P(), P(), P(), P())
    return jax.shard_map(local, mesh=split, in_specs=placed, out_specs=cut, check_vma=False)
```

```python
import functools

import jax
import jax.numpy as jnp
from jax import lax
from jax.experimental import pallas as pl
from jax.experimental.pallas import tpu as pltpu
from jax.sharding import PartitionSpec as P

G = 32
EPSILON = 1e-06
LANES = 128
F32 = jnp.float32
BF16 = jnp.bfloat16
ROW = ("y", "core")
LINE = 16
EDGE = 24


def picked(x, chosen):
    high = x.astype(BF16).astype(F32)
    rest = x - high
    middle = rest.astype(BF16).astype(F32)
    low = rest - middle
    stacked = jnp.concatenate([high, middle, low, jnp.zeros((13, x.shape[1]), F32)], axis=0)
    return jnp.sum(
        jnp.dot(stacked.astype(BF16), chosen, preferred_element_type=F32), axis=0, keepdims=True
    )


def lanes_of(channels, channels_last):
    shape = (LANES, 2 * channels) if channels_last else (2 * channels, LANES)
    channel = lax.broadcasted_iota(jnp.int32, shape, 1 if channels_last else 0)
    lane = lax.broadcasted_iota(jnp.int32, shape, 0 if channels_last else 1)
    return (channel // (channels // G) == lane).astype(BF16)


def fold(x, mean, squares, seen):
    n = float(x.shape[0])
    own = jnp.sum(x, axis=0, keepdims=True) / n
    apart = x - own
    spread = jnp.sum(apart * apart, axis=0, keepdims=True)
    both = seen + n
    gap = own - mean
    return mean + gap * (n / both), squares + spread + gap * gap * (seen * n / both), both


def pack(mean, squares, count):
    channels = mean.shape[-1]
    per = channels // G
    one = lax.broadcasted_iota(jnp.int32, (channels, channels), 0) // per
    other = lax.broadcasted_iota(jnp.int32, (channels, channels), 1) // per
    grouped = picked(mean, (one == other).astype(BF16)) / per
    apart = grouped - mean
    total = squares + count * apart * apart
    return picked(jnp.concatenate([mean / per, total], axis=1), lanes_of(channels, False))


def merge(rows, count):
    summed = jnp.sum(rows, axis=0, keepdims=True)
    average = summed / rows.shape[0]
    apart = rows - average
    spread = count * jnp.sum(apart * apart, axis=0, keepdims=True)
    lane = lax.broadcasted_iota(jnp.int32, (1, LANES), 1)
    total = jnp.where(lane < 2 * G, summed + pltpu.roll(spread, G, 1), 0.0)
    return jnp.where(lane < G, average, total)


def join_kernel(count, own_ref, other_ref, o_ref):
    row = merge(jnp.concatenate([own_ref[0], other_ref[0]], axis=0), count)
    o_ref[...] = jnp.broadcast_to(row[None], o_ref.shape)


def norm_of(stats_ref, group, gain_ref, bias_ref):
    rows = stats_ref[...]
    channels = gain_ref.shape[-1]
    wide = picked(merge(rows, float(group)), lanes_of(channels, True))
    variance = wide[:, channels:] / float(group * rows.shape[0])
    scale = lax.rsqrt(variance + EPSILON) * gain_ref[...]
    return wide[:, :channels], 0.5 * scale, 0.5 * bias_ref[...]


def active(x, norm):
    mean, half_scale, half_bias = norm
    half = (x.astype(F32) - mean) * half_scale + half_bias
    return half * jnp.tanh(half) + half


def within():
    def place(axis):
        if axis != ROW:
            return lax.axis_index(axis)
        return lax.axis_index("y") * lax.axis_size("core") + lax.axis_index("core")

    def unless(axis, where):
        return jnp.where(place(axis) == where, 0.0, 1.0).astype(F32)

    return (
        unless(ROW, 0),
        unless(ROW, lax.axis_size(ROW) - 1),
        unless("col", 0),
        unless("col", lax.axis_size("col") - 1),
    )


def columns_kernel(x_ref, to_left_ref, to_right_ref, rows_ref, last_ref):
    frames, height, breadth, channels = x_ref.shape
    cells = height * breadth
    target = lax.broadcasted_iota(jnp.int32, (4 * height, cells), 0)
    source = lax.broadcasted_iota(jnp.int32, (4 * height, cells), 1)
    which = target // height
    column = jnp.where(which < 2, which, which + (breadth - 4))
    chosen = (source == (target % height) * breadth + column).astype(BF16)
    last_ref[...] = x_ref[pl.ds(frames - 2, 2)]
    for t in range(frames):
        got = jnp.dot(
            chosen, x_ref[t].reshape(cells, channels), preferred_element_type=F32
        ).astype(BF16)
        got = got.reshape(4, height, channels)
        to_left_ref[t] = got[:2]
        to_right_ref[t] = got[2:]
        rows_ref[t, pl.ds(0, 2)] = x_ref[t, pl.ds(0, 2)]
        rows_ref[t, pl.ds(2, 2)] = x_ref[t, pl.ds(height - 2, 2)]


def stats_kernel(x_ref, _, o_ref):
    frames, height, breadth, channels = x_ref.shape
    carry = (jnp.zeros((1, channels), F32), jnp.zeros((1, channels), F32), 0.0)
    for t in range(frames):
        carry = fold(x_ref[t].astype(F32).reshape(height * breadth, channels), *carry)
    row = pack(carry[0], carry[1], float(frames * height * breadth))
    o_ref[...] = jnp.broadcast_to(row[None], o_ref.shape)


def rows_kernel(rows_ref, left_ref, right_ref, to_above_ref, to_below_ref):
    frames, _, height, channels = left_ref.shape
    for t in range(frames):
        corners = [
            ref[t, k].astype(F32) for ref in (left_ref, right_ref) for k in range(2)
        ]
        for k, (ref, start) in enumerate(((to_above_ref, 0), (to_below_ref, height - 2))):
            ref[t, pl.ds(0, 2)] = rows_ref[t, pl.ds(2 * k, 2)]
            line = [c[start : start + 2] for c in corners]
            line.append(jnp.zeros((LINE - 8, channels), F32))
            ref[t, 2] = jnp.concatenate(line, axis=0).astype(BF16)


def put(a_ref, t, i, y, left, right):
    a_ref[0, t, i] = jnp.concatenate([left, y[:-1]], axis=0).astype(BF16)
    a_ref[1, t, i] = y.astype(BF16)
    a_ref[2, t, i] = jnp.concatenate([y[1:], right], axis=0).astype(BF16)


def conv_frame(a_ref, e_ref, w_ref, t):
    rows, breadth, channels = a_ref.shape[2] - 2, a_ref.shape[3], a_ref.shape[4]
    total = None
    for a in range(3):
        for b in range(3):
            window = jnp.concatenate(
                [
                    a_ref[c, t + a, pl.ds(b, rows)].reshape(rows * breadth, channels)
                    for c in range(3)
                ],
                axis=1,
            )
            if e_ref is not None:
                window = jnp.concatenate([window, e_ref[b, t + a]], axis=0)
            part = jnp.dot(window, w_ref[3 * a + b], preferred_element_type=F32)
            total = part if total is None else total + part
    return total


def first_body(
    share,
    own_ref,
    above_ref,
    below_ref,
    left_ref,
    right_ref,
    early_ref,
    stats_ref,
    gain_ref,
    bias_ref,
    offset_ref,
    w_ref,
    hidden_ref,
    packed_ref,
    a_ref,
    e_ref,
    c_ref,
):
    frames, height, breadth, channels = own_ref.shape
    group = frames * height * breadth * (channels // G)
    norm = norm_of(stats_ref, share * group, gain_ref, bias_ref)
    top, bottom, leftmost, rightmost = within()
    tall = height + 4

    def frame(center, above, below, left, right, s, t):
        upper = active(above[s, 2], norm) * top
        lower = active(below[s, 2], norm) * bottom
        for k in range(4):
            side = leftmost if k < 2 else rightmost
            x = left[s, k] if k < 2 else right[s, k - 2]
            c_ref[k, pl.ds(0, 2)] = upper[2 * k : 2 * k + 2] * side
            c_ref[k, pl.ds(2, height)] = active(x, norm) * side
            c_ref[k, pl.ds(2 + height, 2)] = lower[2 * k : 2 * k + 2] * side
        for i in range(tall):
            if i < 2:
                y = active(above[s, i], norm) * top
            elif i >= height + 2:
                y = active(below[s, i - height - 2], norm) * bottom
            else:
                y = active(center[s, i - 2], norm)
            put(a_ref, t, i, y, c_ref[1, pl.ds(i, 1)], c_ref[2, pl.ds(i, 1)])
            c_ref[4, pl.ds(i, 1)] = y[:1]
            c_ref[5, pl.ds(i, 1)] = y[breadth - 1 :]
        for b in range(3):
            for c, (near, far) in enumerate(((0, 5), (1, 2), (4, 3))):
                both = jnp.concatenate(
                    [c_ref[near, pl.ds(b, EDGE)], c_ref[far, pl.ds(b, EDGE)]], axis=0
                )
                e_ref[b, t, :, pl.ds(c * channels, channels)] = both.astype(BF16)

    c_ref[...] = jnp.zeros_like(c_ref)
    own = (own_ref, above_ref, below_ref, left_ref, right_ref)
    lines = [(0, height), (height, 3), (height + 3, 3), (height + 6, 2), (height + 8, 2)]
    sent = [early_ref.at[:, pl.ds(start, size)] for start, size in lines]
    first_device = lax.axis_index("tm") == 0

    @pl.when(first_device)
    def _():
        lax.fori_loop(0, 2, lambda t, _: frame(*own, 0, t), None)

    @pl.when(jnp.logical_not(first_device))
    def _():
        lax.fori_loop(0, 2, lambda t, _: frame(*sent, t, t), None)

    frame(*own, 0, 2)
    inner = (height + 2) * breadth

    def one(t, carry):
        out = conv_frame(a_ref, e_ref, w_ref, t) + offset_ref[...]
        hidden_ref[t] = out.reshape(hidden_ref.shape[1:])
        return fold(out[breadth : inner - breadth], *carry)

    carry = (jnp.zeros((1, channels), F32), jnp.zeros((1, channels), F32), 0.0)
    for t in range(frames):
        if t + 1 < frames:
            frame(*own, t + 1, t + 3)
        carry = one(t, carry)
    mean, squares, _ = carry
    row = pack(mean, squares, float(frames * height * breadth))
    packed_ref[...] = jnp.broadcast_to(row[None], packed_ref.shape)


def second_body(
    share,
    features_ref,
    own_ref,
    early_ref,
    stats_ref,
    gain_ref,
    bias_ref,
    offset_ref,
    w_ref,
    out_hbm,
    a_ref,
    c_ref,
    out_ref,
    u_ref,
    out_sem,
):
    frames, height, breadth, channels = features_ref.shape
    group = frames * height * breadth * (channels // G)
    norm = norm_of(stats_ref, share * group, gain_ref, bias_ref)
    top, bottom, leftmost, rightmost = within()
    tall = height + 2
    line = lax.broadcasted_iota(jnp.int32, (2 * EDGE, 1), 0)
    i_of = line % EDGE
    edges = jnp.where(line < EDGE, leftmost, rightmost)
    edges = edges * jnp.where(i_of == 0, top, jnp.where(i_of == tall - 1, bottom, 1.0))

    def frame(source, s, t):
        sides = source[s, pl.ds(tall, 2 * EDGE // LINE)].reshape(2 * EDGE, channels)
        c_ref[...] = active(sides, norm) * edges
        for i in range(tall):
            y = active(source[s, i], norm)
            if i == 0:
                y = y * top
            elif i == tall - 1:
                y = y * bottom
            put(a_ref, t, i, y, c_ref[pl.ds(i, 1)], c_ref[pl.ds(EDGE + i, 1)])

    first_device = lax.axis_index("tm") == 0

    @pl.when(first_device)
    def _():
        lax.fori_loop(0, 2, lambda t, _: frame(own_ref, 0, t), None)

    @pl.when(jnp.logical_not(first_device))
    def _():
        lax.fori_loop(0, 2, lambda t, _: frame(early_ref, t, t), None)

    frame(own_ref, 0, 2)
    cells = height * breadth

    def one(t, carry):
        out = conv_frame(a_ref, None, w_ref, t) + offset_ref[...]
        blended = (features_ref[t].astype(F32).reshape(cells, channels) + out)
        for k in range(channels // LANES):
            half = blended[:, k * LANES : (k + 1) * LANES]
            u_ref[k, pl.ds(0, cells, stride=2), :] = half
            u_ref[k, pl.ds(1, cells, stride=2), :] = half
        wide = jnp.concatenate([u_ref[k] for k in range(channels // LANES)], axis=1)
        wide = wide.astype(BF16).reshape(height, 2 * breadth, channels)
        out_ref[t, :, 0] = wide
        out_ref[t, :, 1] = wide
        pltpu.make_async_copy(out_ref.at[t], out_hbm.at[t], out_sem.at[t]).start()
        return carry

    for t in range(frames):
        if t + 1 < frames:
            frame(own_ref, t + 1, t + 3)
        one(t, 0)
    for t in range(frames):
        pltpu.make_async_copy(out_ref.at[t], out_hbm.at[t], out_sem.at[t]).wait()


VMEM = pl.BlockSpec(memory_space=pltpu.VMEM)
HBM = pl.BlockSpec(memory_space=pltpu.HBM)
PARAMS = pltpu.CompilerParams(vmem_limit_bytes=8 * 2**20)
LARGE = pltpu.CompilerParams(vmem_limit_bytes=16 * 2**20)


def shifted(x, axis, by):
    size = lax.axis_size(axis)
    return lax.ppermute(x, axis, [(i, (i + by) % size) for i in range(size)])


def swapped(x, axis, bits):
    size = lax.axis_size(axis)
    return lax.ppermute(x, axis, [(i, i ^ bits) for i in range(size) if i ^ bits < size])


def joined(own, other, count, copies):
    return pl.pallas_call(
        functools.partial(join_kernel, float(count)),
        out_shape=jax.ShapeDtypeStruct((copies, 1, LANES), F32),
        in_specs=[VMEM] * 2,
        out_specs=VMEM,
        compiler_params=PARAMS,
    )(own, other)


def everyone(rows, axes):
    return lax.all_to_all(rows, axes, 0, 0).reshape(rows.shape[0], LANES)


def local(
    features,
    first_gain,
    first_bias,
    first_kernel,
    first_offset,
    second_gain,
    second_bias,
    second_kernel,
    second_offset,
):
    frames, height, breadth, channels = features.shape
    tall = height + 2
    group = frames * height * breadth * (channels // G)
    row_out = jax.ShapeDtypeStruct((1, 1, LANES), F32)
    columns_out = jax.ShapeDtypeStruct((frames, 2, height, channels), BF16)
    border_out = jax.ShapeDtypeStruct((frames, 3, breadth, channels), BF16)
    hidden_lines = tall + 2 * EDGE // LINE

    def flat(v):
        return v.reshape(1, channels)

    def weights(kernel):
        return kernel.reshape(9, 3 * channels, channels)

    to_left, to_right, outer, last = pl.pallas_call(
        columns_kernel,
        out_shape=(
            columns_out,
            columns_out,
            jax.ShapeDtypeStruct((frames, 4, breadth, channels), BF16),
            jax.ShapeDtypeStruct((2, height, breadth, channels), BF16),
        ),
        in_specs=[VMEM],
        out_specs=(VMEM,) * 4,
        compiler_params=PARAMS,
    )(features)
    right = shifted(to_left, "col", -1)
    left = shifted(to_right, "col", 1)
    near = weights(first_kernel)
    stats = pl.pallas_call(
        stats_kernel,
        out_shape=row_out,
        in_specs=[VMEM] * 2,
        out_specs=VMEM,
        compiler_params=PARAMS,
    )(features, near)
    stats = joined(stats, swapped(stats, "core", 1), group, 1)
    left, right, stats = lax.optimization_barrier((left, right, stats))
    other = swapped(stats, "tm", 1)
    to_above, to_below = pl.pallas_call(
        rows_kernel,
        out_shape=(border_out, border_out),
        in_specs=[VMEM] * 3,
        out_specs=(VMEM, VMEM),
        compiler_params=PARAMS,
    )(outer, left, right)
    below = shifted(to_above, ROW, -1)
    above = shifted(to_below, ROW, 1)
    stats, below = lax.optimization_barrier((stats, below))
    stats = joined(stats, other, 2 * group, 1)
    planes = ("y", "col")
    stats = joined(stats, swapped(stats, "tm", 3), 4 * group, lax.axis_size(planes))
    tail = jnp.concatenate([x[-2:] for x in (last, above, below, left, right)], axis=1)
    tail, stats = lax.optimization_barrier((tail, stats))
    early = shifted(tail, "tm", 1)
    stats = everyone(stats, planes)
    hidden, packed = pl.pallas_call(
        functools.partial(first_body, lax.axis_size(("tm", "core"))),
        out_shape=(
            jax.ShapeDtypeStruct((frames, hidden_lines, breadth, channels), F32),
            row_out,
        ),
        in_specs=[VMEM] * 11,
        out_specs=(VMEM, VMEM),
        scratch_shapes=[
            pltpu.VMEM((3, frames + 2, height + 4, breadth, channels), BF16),
            pltpu.VMEM((3, frames + 2, 2 * EDGE, 3 * channels), BF16),
            pltpu.VMEM((6, EDGE + 8, channels), F32),
        ],
        compiler_params=LARGE,
    )(
        features,
        above,
        below,
        left,
        right,
        early,
        stats,
        flat(first_gain),
        flat(first_bias),
        flat(first_offset),
        near,
    )
    chips = ("tm", "y", "col")
    other = swapped(packed, "core", 1)
    hidden, other = lax.optimization_barrier((hidden, other))
    early = shifted(hidden[-2:], "tm", 1)
    stats = everyone(joined(packed, other, group, lax.axis_size(chips)), chips)
    out = pl.pallas_call(
        functools.partial(second_body, lax.axis_size("core")),
        out_shape=jax.ShapeDtypeStruct((frames, height, 2, 2 * breadth, channels), BF16),
        in_specs=[VMEM] * 8,
        out_specs=HBM,
        scratch_shapes=[
            pltpu.VMEM((3, frames + 2, tall, breadth, channels), BF16),
            pltpu.VMEM((2 * EDGE, channels), F32),
            pltpu.VMEM((frames, height, 2, 2 * breadth, channels), BF16),
            pltpu.VMEM((channels // LANES, 2 * height * breadth, LANES), F32),
            pltpu.SemaphoreType.DMA((frames,)),
        ],
        compiler_params=LARGE,
    )(
        features,
        hidden,
        early,
        stats,
        flat(second_gain),
        flat(second_bias),
        flat(second_offset),
        weights(second_kernel),
    )
    return out.reshape(frames, 2 * height, 2 * breadth, channels)


def solution(mesh):
    frames, rows, columns = mesh.devices.shape
    split = jax.sharding.Mesh(
        mesh.devices.reshape(frames, rows // 2, 2, columns), ("tm", "y", "core", "col")
    )
    cut = P("tm", ROW, "col", None)
    placed = (cut, P(), P(), P(), P(), P(), P(), P(), P())
    return jax.shard_map(local, mesh=split, in_specs=placed, out_specs=cut, check_vma=False)
```

```python
import functools

import jax
import jax.numpy as jnp
from jax import lax
from jax.experimental import pallas as pl
from jax.experimental.pallas import tpu as pltpu
from jax.sharding import PartitionSpec as P

G = 32
EPSILON = 1e-06
LANES = 128
F32 = jnp.float32
BF16 = jnp.bfloat16
ROW = ("y", "core")
LINE = 16
EDGE = 24


def picked(x, chosen):
    high = x.astype(BF16).astype(F32)
    rest = x - high
    middle = rest.astype(BF16).astype(F32)
    low = rest - middle
    stacked = jnp.concatenate([high, middle, low, jnp.zeros((13, x.shape[1]), F32)], axis=0)
    return jnp.sum(
        jnp.dot(stacked.astype(BF16), chosen, preferred_element_type=F32), axis=0, keepdims=True
    )


def lanes_of(channels, channels_last):
    shape = (LANES, 2 * channels) if channels_last else (2 * channels, LANES)
    channel = lax.broadcasted_iota(jnp.int32, shape, 1 if channels_last else 0)
    lane = lax.broadcasted_iota(jnp.int32, shape, 0 if channels_last else 1)
    return (channel // (channels // G) == lane).astype(BF16)


def fold(x, mean, squares, seen):
    n = float(x.shape[0])
    own = jnp.sum(x, axis=0, keepdims=True) / n
    apart = x - own
    spread = jnp.sum(apart * apart, axis=0, keepdims=True)
    both = seen + n
    gap = own - mean
    return mean + gap * (n / both), squares + spread + gap * gap * (seen * n / both), both


def pack(mean, squares, count):
    channels = mean.shape[-1]
    per = channels // G
    one = lax.broadcasted_iota(jnp.int32, (channels, channels), 0) // per
    other = lax.broadcasted_iota(jnp.int32, (channels, channels), 1) // per
    grouped = picked(mean, (one == other).astype(BF16)) / per
    apart = grouped - mean
    total = squares + count * apart * apart
    return picked(jnp.concatenate([mean / per, total], axis=1), lanes_of(channels, False))


def merge(rows, count):
    summed = jnp.sum(rows, axis=0, keepdims=True)
    average = summed / rows.shape[0]
    apart = rows - average
    spread = count * jnp.sum(apart * apart, axis=0, keepdims=True)
    lane = lax.broadcasted_iota(jnp.int32, (1, LANES), 1)
    total = jnp.where(lane < 2 * G, summed + pltpu.roll(spread, G, 1), 0.0)
    return jnp.where(lane < G, average, total)


def join_kernel(count, own_ref, other_ref, *refs):
    o_ref = refs[-1]
    row = merge(jnp.concatenate([own_ref[0], other_ref[0]], axis=0), count)
    o_ref[...] = jnp.broadcast_to(row[None], o_ref.shape)


def norm_of(stats_ref, group, gain_ref, bias_ref):
    rows = stats_ref[...]
    channels = gain_ref.shape[-1]
    wide = picked(merge(rows, float(group)), lanes_of(channels, True))
    variance = wide[:, channels:] / float(group * rows.shape[0])
    scale = lax.rsqrt(variance + EPSILON) * gain_ref[...]
    return wide[:, :channels], 0.5 * scale, 0.5 * bias_ref[...]


def active(x, norm):
    mean, half_scale, half_bias = norm
    half = (x.astype(F32) - mean) * half_scale + half_bias
    return half * jnp.tanh(half) + half


def within():
    def place(axis):
        if axis != ROW:
            return lax.axis_index(axis)
        return lax.axis_index("y") * lax.axis_size("core") + lax.axis_index("core")

    def unless(axis, where):
        return jnp.where(place(axis) == where, 0.0, 1.0).astype(F32)

    return (
        unless(ROW, 0),
        unless(ROW, lax.axis_size(ROW) - 1),
        unless("col", 0),
        unless("col", lax.axis_size("col") - 1),
    )


def columns_kernel(x_ref, to_left_ref, to_right_ref, rows_ref, all_ref):
    frames, height, breadth, channels = x_ref.shape
    cells = height * breadth
    target = lax.broadcasted_iota(jnp.int32, (4 * height, cells), 0)
    source = lax.broadcasted_iota(jnp.int32, (4 * height, cells), 1)
    which = target // height
    column = jnp.where(which < 2, which, which + (breadth - 4))
    chosen = (source == (target % height) * breadth + column).astype(BF16)
    all_ref[...] = x_ref[...]
    for t in range(frames):
        got = jnp.dot(
            chosen, x_ref[t].reshape(cells, channels), preferred_element_type=F32
        ).astype(BF16)
        got = got.reshape(4, height, channels)
        to_left_ref[t] = got[:2]
        to_right_ref[t] = got[2:]
        rows_ref[t, pl.ds(0, 2)] = x_ref[t, pl.ds(0, 2)]
        rows_ref[t, pl.ds(2, 2)] = x_ref[t, pl.ds(height - 2, 2)]


def stats_kernel(x_ref, o_ref):
    frames, height, breadth, channels = x_ref.shape
    carry = (jnp.zeros((1, channels), F32), jnp.zeros((1, channels), F32), 0.0)
    for t in range(frames):
        carry = fold(x_ref[t].astype(F32).reshape(height * breadth, channels), *carry)
    row = pack(carry[0], carry[1], float(frames * height * breadth))
    o_ref[...] = jnp.broadcast_to(row[None], o_ref.shape)


def rows_kernel(rows_ref, left_ref, right_ref, to_above_ref, to_below_ref):
    frames, _, height, channels = left_ref.shape
    for t in range(frames):
        corners = [
            ref[t, k].astype(F32) for ref in (left_ref, right_ref) for k in range(2)
        ]
        for k, (ref, start) in enumerate(((to_above_ref, 0), (to_below_ref, height - 2))):
            ref[t, pl.ds(0, 2)] = rows_ref[t, pl.ds(2 * k, 2)]
            line = [c[start : start + 2] for c in corners]
            line.append(jnp.zeros((LINE - 8, channels), F32))
            ref[t, 2] = jnp.concatenate(line, axis=0).astype(BF16)


def put(a_ref, t, i, y, left, right):
    a_ref[0, t, i] = jnp.concatenate([left, y[:-1]], axis=0).astype(BF16)
    a_ref[1, t, i] = y.astype(BF16)
    a_ref[2, t, i] = jnp.concatenate([y[1:], right], axis=0).astype(BF16)


def conv_frame(a_ref, e_ref, w_ref, t):
    rows, breadth, channels = a_ref.shape[2] - 2, a_ref.shape[3], a_ref.shape[4]
    total = None
    for a in range(3):
        for b in range(3):
            window = jnp.concatenate(
                [
                    a_ref[c, t + a, pl.ds(b, rows)].reshape(rows * breadth, channels)
                    for c in range(3)
                ],
                axis=1,
            )
            if e_ref is not None:
                window = jnp.concatenate([window, e_ref[b, t + a]], axis=0)
            part = jnp.dot(window, w_ref[3 * a + b], preferred_element_type=F32)
            total = part if total is None else total + part
    return total


def first_body(
    share,
    own_ref,
    above_ref,
    below_ref,
    left_ref,
    right_ref,
    early_ref,
    stats_ref,
    gain_ref,
    bias_ref,
    offset_ref,
    w_ref,
    hidden_ref,
    packed_ref,
    a_ref,
    e_ref,
    c_ref,
):
    frames, height, breadth, channels = own_ref.shape
    group = frames * height * breadth * (channels // G)
    norm = norm_of(stats_ref, share * group, gain_ref, bias_ref)
    top, bottom, leftmost, rightmost = within()
    tall = height + 4

    def frame(center, above, below, left, right, s, t):
        upper = active(above[s, 2], norm) * top
        lower = active(below[s, 2], norm) * bottom
        for k in range(4):
            side = leftmost if k < 2 else rightmost
            x = left[s, k] if k < 2 else right[s, k - 2]
            c_ref[k, pl.ds(0, 2)] = upper[2 * k : 2 * k + 2] * side
            c_ref[k, pl.ds(2, height)] = active(x, norm) * side
            c_ref[k, pl.ds(2 + height, 2)] = lower[2 * k : 2 * k + 2] * side
        for i in range(tall):
            if i < 2:
                y = active(above[s, i], norm) * top
            elif i >= height + 2:
                y = active(below[s, i - height - 2], norm) * bottom
            else:
                y = active(center[s, i - 2], norm)
            put(a_ref, t, i, y, c_ref[1, pl.ds(i, 1)], c_ref[2, pl.ds(i, 1)])
            c_ref[4, pl.ds(i, 1)] = y[:1]
            c_ref[5, pl.ds(i, 1)] = y[breadth - 1 :]
        for b in range(3):
            for c, (near, far) in enumerate(((0, 5), (1, 2), (4, 3))):
                both = jnp.concatenate(
                    [c_ref[near, pl.ds(b, EDGE)], c_ref[far, pl.ds(b, EDGE)]], axis=0
                )
                e_ref[b, t, :, pl.ds(c * channels, channels)] = both.astype(BF16)

    c_ref[...] = jnp.zeros_like(c_ref)
    own = (own_ref, above_ref, below_ref, left_ref, right_ref)
    lines = [(0, height), (height, 3), (height + 3, 3), (height + 6, 2), (height + 8, 2)]
    sent = [early_ref.at[:, pl.ds(start, size)] for start, size in lines]
    first_device = lax.axis_index("tm") == 0

    @pl.when(first_device)
    def _():
        lax.fori_loop(0, 2, lambda t, _: frame(*own, 0, t), None)

    @pl.when(jnp.logical_not(first_device))
    def _():
        lax.fori_loop(0, 2, lambda t, _: frame(*sent, t, t), None)

    frame(*own, 0, 2)
    inner = (height + 2) * breadth

    def one(t, carry):
        out = conv_frame(a_ref, e_ref, w_ref, t) + offset_ref[...]
        hidden_ref[t] = out.reshape(hidden_ref.shape[1:])
        return fold(out[breadth : inner - breadth], *carry)

    carry = (jnp.zeros((1, channels), F32), jnp.zeros((1, channels), F32), 0.0)
    for t in range(frames):
        if t + 1 < frames:
            frame(*own, t + 1, t + 3)
        carry = one(t, carry)
    mean, squares, _ = carry
    row = pack(mean, squares, float(frames * height * breadth))
    packed_ref[...] = jnp.broadcast_to(row[None], packed_ref.shape)


def second_body(
    share,
    features_ref,
    own_ref,
    early_ref,
    stats_ref,
    gain_ref,
    bias_ref,
    offset_ref,
    w_ref,
    out_hbm,
    a_ref,
    c_ref,
    out_ref,
    u_ref,
    out_sem,
):
    frames, height, breadth, channels = features_ref.shape
    group = frames * height * breadth * (channels // G)
    norm = norm_of(stats_ref, share * group, gain_ref, bias_ref)
    top, bottom, leftmost, rightmost = within()
    tall = height + 2
    line = lax.broadcasted_iota(jnp.int32, (2 * EDGE, 1), 0)
    i_of = line % EDGE
    edges = jnp.where(line < EDGE, leftmost, rightmost)
    edges = edges * jnp.where(i_of == 0, top, jnp.where(i_of == tall - 1, bottom, 1.0))

    def frame(source, s, t):
        sides = source[s, pl.ds(tall, 2 * EDGE // LINE)].reshape(2 * EDGE, channels)
        c_ref[...] = active(sides, norm) * edges
        for i in range(tall):
            y = active(source[s, i], norm)
            if i == 0:
                y = y * top
            elif i == tall - 1:
                y = y * bottom
            put(a_ref, t, i, y, c_ref[pl.ds(i, 1)], c_ref[pl.ds(EDGE + i, 1)])

    first_device = lax.axis_index("tm") == 0

    @pl.when(first_device)
    def _():
        lax.fori_loop(0, 2, lambda t, _: frame(own_ref, 0, t), None)

    @pl.when(jnp.logical_not(first_device))
    def _():
        lax.fori_loop(0, 2, lambda t, _: frame(early_ref, t, t), None)

    frame(own_ref, 0, 2)
    cells = height * breadth

    def one(t, carry):
        out = conv_frame(a_ref, None, w_ref, t) + offset_ref[...]
        blended = (features_ref[t].astype(F32).reshape(cells, channels) + out)
        for k in range(channels // LANES):
            half = blended[:, k * LANES : (k + 1) * LANES]
            u_ref[k, pl.ds(0, cells, stride=2), :] = half
            u_ref[k, pl.ds(1, cells, stride=2), :] = half
        wide = jnp.concatenate([u_ref[k] for k in range(channels // LANES)], axis=1)
        wide = wide.astype(BF16).reshape(height, 2 * breadth, channels)
        out_ref[t, :, 0] = wide
        out_ref[t, :, 1] = wide
        pltpu.make_async_copy(out_ref.at[t], out_hbm.at[t], out_sem.at[t]).start()
        return carry

    for t in range(frames):
        if t + 1 < frames:
            frame(own_ref, t + 1, t + 3)
        one(t, 0)
    for t in range(frames):
        pltpu.make_async_copy(out_ref.at[t], out_hbm.at[t], out_sem.at[t]).wait()


VMEM = pl.BlockSpec(memory_space=pltpu.VMEM)
HBM = pl.BlockSpec(memory_space=pltpu.HBM)
PARAMS = pltpu.CompilerParams(vmem_limit_bytes=8 * 2**20)
LARGE = pltpu.CompilerParams(vmem_limit_bytes=16 * 2**20)


def shifted(x, axis, by):
    size = lax.axis_size(axis)
    return lax.ppermute(x, axis, [(i, (i + by) % size) for i in range(size)])


def swapped(x, axis, bits):
    size = lax.axis_size(axis)
    return lax.ppermute(x, axis, [(i, i ^ bits) for i in range(size) if i ^ bits < size])


def joined(own, other, count, copies, *wanted):
    return pl.pallas_call(
        functools.partial(join_kernel, float(count)),
        out_shape=jax.ShapeDtypeStruct((copies, 1, LANES), F32),
        in_specs=[VMEM] * (2 + len(wanted)),
        out_specs=VMEM,
        compiler_params=PARAMS,
    )(own, other, *wanted)


def everyone(rows, axes):
    return lax.all_to_all(rows, axes, 0, 0).reshape(rows.shape[0], LANES)


def local(
    features,
    first_gain,
    first_bias,
    first_kernel,
    first_offset,
    second_gain,
    second_bias,
    second_kernel,
    second_offset,
):
    frames, height, breadth, channels = features.shape
    tall = height + 2
    group = frames * height * breadth * (channels // G)
    row_out = jax.ShapeDtypeStruct((1, 1, LANES), F32)
    columns_out = jax.ShapeDtypeStruct((frames, 2, height, channels), BF16)
    border_out = jax.ShapeDtypeStruct((frames, 3, breadth, channels), BF16)
    hidden_lines = tall + 2 * EDGE // LINE

    def flat(v):
        return v.reshape(1, channels)

    def weights(kernel):
        return kernel.reshape(9, 3 * channels, channels)

    to_left, to_right, outer, held = pl.pallas_call(
        columns_kernel,
        out_shape=(
            columns_out,
            columns_out,
            jax.ShapeDtypeStruct((frames, 4, breadth, channels), BF16),
            jax.ShapeDtypeStruct(features.shape, BF16),
        ),
        in_specs=[VMEM],
        out_specs=(VMEM,) * 4,
        compiler_params=PARAMS,
    )(features)
    right = shifted(to_left, "col", -1)
    left = shifted(to_right, "col", 1)
    stats = pl.pallas_call(
        stats_kernel,
        out_shape=row_out,
        in_specs=[VMEM],
        out_specs=VMEM,
        compiler_params=PARAMS,
    )(held)
    stats = joined(stats, swapped(stats, "core", 1), group, 1)
    other = swapped(stats, "tm", 1)
    to_above, to_below = pl.pallas_call(
        rows_kernel,
        out_shape=(border_out, border_out),
        in_specs=[VMEM] * 3,
        out_specs=(VMEM, VMEM),
        compiler_params=PARAMS,
    )(outer, left, right)
    below = shifted(to_above, ROW, -1)
    above = shifted(to_below, ROW, 1)
    stats, _ = lax.optimization_barrier((stats, to_above))
    stats = joined(stats, other, 2 * group, 1)
    planes = ("y", "col")
    near = weights(first_kernel)
    stats = joined(stats, swapped(stats, "tm", 3), 4 * group, lax.axis_size(planes), near)
    tail = jnp.concatenate([x[-2:] for x in (held, above, below, left, right)], axis=1)
    tail, stats = lax.optimization_barrier((tail, stats))
    early = shifted(tail, "tm", 1)
    stats = everyone(stats, planes)
    hidden, packed = pl.pallas_call(
        functools.partial(first_body, lax.axis_size(("tm", "core"))),
        out_shape=(
            jax.ShapeDtypeStruct((frames, hidden_lines, breadth, channels), F32),
            row_out,
        ),
        in_specs=[VMEM] * 11,
        out_specs=(VMEM, VMEM),
        scratch_shapes=[
            pltpu.VMEM((3, frames + 2, height + 4, breadth, channels), BF16),
            pltpu.VMEM((3, frames + 2, 2 * EDGE, 3 * channels), BF16),
            pltpu.VMEM((6, EDGE + 8, channels), F32),
        ],
        compiler_params=LARGE,
    )(
        held,
        above,
        below,
        left,
        right,
        early,
        stats,
        flat(first_gain),
        flat(first_bias),
        flat(first_offset),
        near,
    )
    chips = ("tm", "y", "col")
    other = swapped(packed, "core", 1)
    early = shifted(hidden[-2:], "tm", 1)
    stats = everyone(joined(packed, other, group, lax.axis_size(chips)), chips)
    out = pl.pallas_call(
        functools.partial(second_body, lax.axis_size("core")),
        out_shape=jax.ShapeDtypeStruct((frames, height, 2, 2 * breadth, channels), BF16),
        in_specs=[VMEM] * 8,
        out_specs=HBM,
        scratch_shapes=[
            pltpu.VMEM((3, frames + 2, tall, breadth, channels), BF16),
            pltpu.VMEM((2 * EDGE, channels), F32),
            pltpu.VMEM((frames, height, 2, 2 * breadth, channels), BF16),
            pltpu.VMEM((channels // LANES, 2 * height * breadth, LANES), F32),
            pltpu.SemaphoreType.DMA((frames,)),
        ],
        compiler_params=LARGE,
    )(
        held,
        hidden,
        early,
        stats,
        flat(second_gain),
        flat(second_bias),
        flat(second_offset),
        weights(second_kernel),
    )
    return out.reshape(frames, 2 * height, 2 * breadth, channels)


def solution(mesh):
    frames, rows, columns = mesh.devices.shape
    split = jax.sharding.Mesh(
        mesh.devices.reshape(frames, rows // 2, 2, columns), ("tm", "y", "core", "col")
    )
    cut = P("tm", ROW, "col", None)
    placed = (cut, P(), P(), P(), P(), P(), P(), P(), P())
    return jax.shard_map(local, mesh=split, in_specs=placed, out_specs=cut, check_vma=False)
```

```python
import functools

import jax
import jax.numpy as jnp
from jax import lax
from jax.experimental import pallas as pl
from jax.experimental.pallas import tpu as pltpu
from jax.sharding import PartitionSpec as P

G = 32
EPSILON = 1e-06
LANES = 128
F32 = jnp.float32
BF16 = jnp.bfloat16
ROW = ("y", "core")
LINE = 16
EDGE = 24


def picked(x, chosen):
    high = x.astype(BF16).astype(F32)
    rest = x - high
    middle = rest.astype(BF16).astype(F32)
    low = rest - middle
    stacked = jnp.concatenate([high, middle, low, jnp.zeros((13, x.shape[1]), F32)], axis=0)
    return jnp.sum(
        jnp.dot(stacked.astype(BF16), chosen, preferred_element_type=F32), axis=0, keepdims=True
    )


def lanes_of(channels, channels_last):
    shape = (LANES, 2 * channels) if channels_last else (2 * channels, LANES)
    channel = lax.broadcasted_iota(jnp.int32, shape, 1 if channels_last else 0)
    lane = lax.broadcasted_iota(jnp.int32, shape, 0 if channels_last else 1)
    return (channel // (channels // G) == lane).astype(BF16)


def fold(x, mean, squares, seen):
    n = float(x.shape[0])
    own = jnp.sum(x, axis=0, keepdims=True) / n
    apart = x - own
    spread = jnp.sum(apart * apart, axis=0, keepdims=True)
    both = seen + n
    gap = own - mean
    return mean + gap * (n / both), squares + spread + gap * gap * (seen * n / both), both


def pack(mean, squares, count):
    channels = mean.shape[-1]
    per = channels // G
    one = lax.broadcasted_iota(jnp.int32, (channels, channels), 0) // per
    other = lax.broadcasted_iota(jnp.int32, (channels, channels), 1) // per
    grouped = picked(mean, (one == other).astype(BF16)) / per
    apart = grouped - mean
    total = squares + count * apart * apart
    return picked(jnp.concatenate([mean / per, total], axis=1), lanes_of(channels, False))


def merge(rows, count):
    summed = jnp.sum(rows, axis=0, keepdims=True)
    average = summed / rows.shape[0]
    apart = rows - average
    spread = count * jnp.sum(apart * apart, axis=0, keepdims=True)
    lane = lax.broadcasted_iota(jnp.int32, (1, LANES), 1)
    total = jnp.where(lane < 2 * G, summed + pltpu.roll(spread, G, 1), 0.0)
    return jnp.where(lane < G, average, total)


def join_kernel(count, own_ref, other_ref, *refs):
    o_ref = refs[-1]
    row = merge(jnp.concatenate([own_ref[0], other_ref[0]], axis=0), count)
    o_ref[...] = jnp.broadcast_to(row[None], o_ref.shape)


def norm_of(stats_ref, group, gain_ref, bias_ref):
    rows = stats_ref[...]
    channels = gain_ref.shape[-1]
    wide = picked(merge(rows, float(group)), lanes_of(channels, True))
    variance = wide[:, channels:] / float(group * rows.shape[0])
    scale = lax.rsqrt(variance + EPSILON) * gain_ref[...]
    return wide[:, :channels], 0.5 * scale, 0.5 * bias_ref[...]


def active(x, norm):
    mean, half_scale, half_bias = norm
    half = (x.astype(F32) - mean) * half_scale + half_bias
    return half * jnp.tanh(half) + half


def within():
    def place(axis):
        if axis != ROW:
            return lax.axis_index(axis)
        return lax.axis_index("y") * lax.axis_size("core") + lax.axis_index("core")

    def unless(axis, where):
        return jnp.where(place(axis) == where, 0.0, 1.0).astype(F32)

    return (
        unless(ROW, 0),
        unless(ROW, lax.axis_size(ROW) - 1),
        unless("col", 0),
        unless("col", lax.axis_size("col") - 1),
    )


def columns_kernel(x_ref, to_left_ref, to_right_ref, rows_ref, all_ref):
    frames, height, breadth, channels = x_ref.shape
    cells = height * breadth
    target = lax.broadcasted_iota(jnp.int32, (4 * height, cells), 0)
    source = lax.broadcasted_iota(jnp.int32, (4 * height, cells), 1)
    which = target // height
    column = jnp.where(which < 2, which, which + (breadth - 4))
    chosen = (source == (target % height) * breadth + column).astype(BF16)
    all_ref[...] = x_ref[...]
    for t in range(frames):
        got = jnp.dot(
            chosen, x_ref[t].reshape(cells, channels), preferred_element_type=F32
        ).astype(BF16)
        got = got.reshape(4, height, channels)
        to_left_ref[t] = got[:2]
        to_right_ref[t] = got[2:]
        rows_ref[t, pl.ds(0, 2)] = x_ref[t, pl.ds(0, 2)]
        rows_ref[t, pl.ds(2, 2)] = x_ref[t, pl.ds(height - 2, 2)]


def stats_kernel(x_ref, o_ref):
    frames, height, breadth, channels = x_ref.shape
    carry = (jnp.zeros((1, channels), F32), jnp.zeros((1, channels), F32), 0.0)
    for t in range(frames):
        carry = fold(x_ref[t].astype(F32).reshape(height * breadth, channels), *carry)
    row = pack(carry[0], carry[1], float(frames * height * breadth))
    o_ref[...] = jnp.broadcast_to(row[None], o_ref.shape)


def rows_kernel(rows_ref, left_ref, right_ref, to_above_ref, to_below_ref):
    frames, _, height, channels = left_ref.shape
    for t in range(frames):
        corners = [
            ref[t, k].astype(F32) for ref in (left_ref, right_ref) for k in range(2)
        ]
        for k, (ref, start) in enumerate(((to_above_ref, 0), (to_below_ref, height - 2))):
            ref[t, pl.ds(0, 2)] = rows_ref[t, pl.ds(2 * k, 2)]
            line = [c[start : start + 2] for c in corners]
            line.append(jnp.zeros((LINE - 8, channels), F32))
            ref[t, 2] = jnp.concatenate(line, axis=0).astype(BF16)


def put(a_ref, t, i, y, left, right):
    a_ref[0, t, i] = jnp.concatenate([left, y[:-1]], axis=0).astype(BF16)
    a_ref[1, t, i] = y.astype(BF16)
    a_ref[2, t, i] = jnp.concatenate([y[1:], right], axis=0).astype(BF16)


def conv_frame(a_ref, e_ref, w_ref, t):
    rows, breadth, channels = a_ref.shape[2] - 2, a_ref.shape[3], a_ref.shape[4]
    total = None
    for a in range(3):
        for b in range(3):
            window = jnp.concatenate(
                [
                    a_ref[c, t + a, pl.ds(b, rows)].reshape(rows * breadth, channels)
                    for c in range(3)
                ],
                axis=1,
            )
            if e_ref is not None:
                window = jnp.concatenate([window, e_ref[b, t + a]], axis=0)
            part = jnp.dot(window, w_ref[3 * a + b], preferred_element_type=F32)
            total = part if total is None else total + part
    return total


def first_body(
    share,
    own_ref,
    above_ref,
    below_ref,
    left_ref,
    right_ref,
    early_ref,
    stats_ref,
    gain_ref,
    bias_ref,
    offset_ref,
    w_ref,
    hidden_ref,
    packed_ref,
    a_ref,
    e_ref,
    c_ref,
):
    frames, height, breadth, channels = own_ref.shape
    group = frames * height * breadth * (channels // G)
    norm = norm_of(stats_ref, share * group, gain_ref, bias_ref)
    top, bottom, leftmost, rightmost = within()
    tall = height + 4

    def frame(pick, t):
        upper = active(pick(1, 2), norm) * top
        lower = active(pick(2, 2), norm) * bottom
        for k in range(4):
            side = leftmost if k < 2 else rightmost
            x = pick(3, k) if k < 2 else pick(4, k - 2)
            c_ref[k, pl.ds(0, 2)] = upper[2 * k : 2 * k + 2] * side
            c_ref[k, pl.ds(2, height)] = active(x, norm) * side
            c_ref[k, pl.ds(2 + height, 2)] = lower[2 * k : 2 * k + 2] * side
        for i in range(tall):
            if i < 2:
                y = active(pick(1, i), norm) * top
            elif i >= height + 2:
                y = active(pick(2, i - height - 2), norm) * bottom
            else:
                y = active(pick(0, i - 2), norm)
            put(a_ref, t, i, y, c_ref[1, pl.ds(i, 1)], c_ref[2, pl.ds(i, 1)])
            c_ref[4, pl.ds(i, 1)] = y[:1]
            c_ref[5, pl.ds(i, 1)] = y[breadth - 1 :]
        for b in range(3):
            for c, (near, far) in enumerate(((0, 5), (1, 2), (4, 3))):
                both = jnp.concatenate(
                    [c_ref[near, pl.ds(b, EDGE)], c_ref[far, pl.ds(b, EDGE)]], axis=0
                )
                e_ref[b, t, :, pl.ds(c * channels, channels)] = both.astype(BF16)

    c_ref[...] = jnp.zeros_like(c_ref)
    own = (own_ref, above_ref, below_ref, left_ref, right_ref)
    lines = [(0, height), (height, 3), (height + 3, 3), (height + 6, 2), (height + 8, 2)]
    sent = [early_ref.at[:, pl.ds(start, size)] for start, size in lines]
    first_device = lax.axis_index("tm") == 0

    def own_line(t):
        return lambda k, i: own[k][t, i]

    def early_line(t):
        return lambda k, i: jnp.where(
            first_device, own[k][0, i].astype(F32), sent[k][t, i].astype(F32)
        )

    for t in range(2):
        frame(early_line(t), t)
    frame(own_line(0), 2)
    inner = (height + 2) * breadth

    def one(t, carry):
        out = conv_frame(a_ref, e_ref, w_ref, t) + offset_ref[...]
        hidden_ref[t] = out.reshape(hidden_ref.shape[1:])
        return fold(out[breadth : inner - breadth], *carry)

    carry = (jnp.zeros((1, channels), F32), jnp.zeros((1, channels), F32), 0.0)
    for t in range(frames):
        if t + 1 < frames:
            frame(own_line(t + 1), t + 3)
        carry = one(t, carry)
    mean, squares, _ = carry
    row = pack(mean, squares, float(frames * height * breadth))
    packed_ref[...] = jnp.broadcast_to(row[None], packed_ref.shape)


def second_body(
    share,
    features_ref,
    own_ref,
    early_ref,
    stats_ref,
    gain_ref,
    bias_ref,
    offset_ref,
    w_ref,
    out_hbm,
    a_ref,
    c_ref,
    out_ref,
    u_ref,
    out_sem,
):
    frames, height, breadth, channels = features_ref.shape
    group = frames * height * breadth * (channels // G)
    norm = norm_of(stats_ref, share * group, gain_ref, bias_ref)
    top, bottom, leftmost, rightmost = within()
    tall = height + 2
    line = lax.broadcasted_iota(jnp.int32, (2 * EDGE, 1), 0)
    i_of = line % EDGE
    edges = jnp.where(line < EDGE, leftmost, rightmost)
    edges = edges * jnp.where(i_of == 0, top, jnp.where(i_of == tall - 1, bottom, 1.0))

    def frame(pick, t):
        sides = pick(pl.ds(tall, 2 * EDGE // LINE)).reshape(2 * EDGE, channels)
        c_ref[...] = active(sides, norm) * edges
        for i in range(tall):
            y = active(pick(i), norm)
            if i == 0:
                y = y * top
            elif i == tall - 1:
                y = y * bottom
            put(a_ref, t, i, y, c_ref[pl.ds(i, 1)], c_ref[pl.ds(EDGE + i, 1)])

    first_device = lax.axis_index("tm") == 0

    def own_line(t):
        return lambda i: own_ref[t, i]

    def early_line(t):
        return lambda i: jnp.where(first_device, own_ref[0, i], early_ref[t, i])

    for t in range(2):
        frame(early_line(t), t)
    frame(own_line(0), 2)
    cells = height * breadth

    def one(t, carry):
        out = conv_frame(a_ref, None, w_ref, t) + offset_ref[...]
        blended = (features_ref[t].astype(F32).reshape(cells, channels) + out)
        for k in range(channels // LANES):
            half = blended[:, k * LANES : (k + 1) * LANES]
            u_ref[k, pl.ds(0, cells, stride=2), :] = half
            u_ref[k, pl.ds(1, cells, stride=2), :] = half
        wide = jnp.concatenate([u_ref[k] for k in range(channels // LANES)], axis=1)
        wide = wide.astype(BF16).reshape(height, 2 * breadth, channels)
        out_ref[t, :, 0] = wide
        out_ref[t, :, 1] = wide
        pltpu.make_async_copy(out_ref.at[t], out_hbm.at[t], out_sem.at[t]).start()
        return carry

    for t in range(frames):
        if t + 1 < frames:
            frame(own_line(t + 1), t + 3)
        one(t, 0)
    for t in range(frames):
        pltpu.make_async_copy(out_ref.at[t], out_hbm.at[t], out_sem.at[t]).wait()


VMEM = pl.BlockSpec(memory_space=pltpu.VMEM)
HBM = pl.BlockSpec(memory_space=pltpu.HBM)
PARAMS = pltpu.CompilerParams(vmem_limit_bytes=8 * 2**20)
LARGE = pltpu.CompilerParams(vmem_limit_bytes=16 * 2**20)


def shifted(x, axis, by):
    size = lax.axis_size(axis)
    return lax.ppermute(x, axis, [(i, (i + by) % size) for i in range(size)])


def swapped(x, axis, bits):
    size = lax.axis_size(axis)
    return lax.ppermute(x, axis, [(i, i ^ bits) for i in range(size) if i ^ bits < size])


def joined(own, other, count, copies, *wanted):
    return pl.pallas_call(
        functools.partial(join_kernel, float(count)),
        out_shape=jax.ShapeDtypeStruct((copies, 1, LANES), F32),
        in_specs=[VMEM] * (2 + len(wanted)),
        out_specs=VMEM,
        compiler_params=PARAMS,
    )(own, other, *wanted)


def everyone(rows, axes):
    return lax.all_to_all(rows, axes, 0, 0).reshape(rows.shape[0], LANES)


def local(
    features,
    first_gain,
    first_bias,
    first_kernel,
    first_offset,
    second_gain,
    second_bias,
    second_kernel,
    second_offset,
):
    frames, height, breadth, channels = features.shape
    tall = height + 2
    group = frames * height * breadth * (channels // G)
    row_out = jax.ShapeDtypeStruct((1, 1, LANES), F32)
    columns_out = jax.ShapeDtypeStruct((frames, 2, height, channels), BF16)
    border_out = jax.ShapeDtypeStruct((frames, 3, breadth, channels), BF16)
    hidden_lines = tall + 2 * EDGE // LINE

    def flat(v):
        return v.reshape(1, channels)

    def weights(kernel):
        return kernel.reshape(9, 3 * channels, channels)

    to_left, to_right, outer, held = pl.pallas_call(
        columns_kernel,
        out_shape=(
            columns_out,
            columns_out,
            jax.ShapeDtypeStruct((frames, 4, breadth, channels), BF16),
            jax.ShapeDtypeStruct(features.shape, BF16),
        ),
        in_specs=[VMEM],
        out_specs=(VMEM,) * 4,
        compiler_params=PARAMS,
    )(features)
    right = shifted(to_left, "col", -1)
    left = shifted(to_right, "col", 1)
    stats = pl.pallas_call(
        stats_kernel,
        out_shape=row_out,
        in_specs=[VMEM],
        out_specs=VMEM,
        compiler_params=PARAMS,
    )(held)
    stats = joined(stats, swapped(stats, "core", 1), group, 1)
    other = swapped(stats, "tm", 1)
    to_above, to_below = pl.pallas_call(
        rows_kernel,
        out_shape=(border_out, border_out),
        in_specs=[VMEM] * 3,
        out_specs=(VMEM, VMEM),
        compiler_params=PARAMS,
    )(outer, left, right)
    below = shifted(to_above, ROW, -1)
    above = shifted(to_below, ROW, 1)
    stats, _ = lax.optimization_barrier((stats, to_above))
    stats = joined(stats, other, 2 * group, 1)
    planes = ("y", "col")
    near = weights(first_kernel)
    stats = joined(stats, swapped(stats, "tm", 3), 4 * group, lax.axis_size(planes), near)
    tail = jnp.concatenate([x[-2:] for x in (held, above, below, left, right)], axis=1)
    tail, stats = lax.optimization_barrier((tail, stats))
    early = shifted(tail, "tm", 1)
    stats = everyone(stats, planes)
    hidden, packed = pl.pallas_call(
        functools.partial(first_body, lax.axis_size(("tm", "core"))),
        out_shape=(
            jax.ShapeDtypeStruct((frames, hidden_lines, breadth, channels), F32),
            row_out,
        ),
        in_specs=[VMEM] * 11,
        out_specs=(VMEM, VMEM),
        scratch_shapes=[
            pltpu.VMEM((3, frames + 2, height + 4, breadth, channels), BF16),
            pltpu.VMEM((3, frames + 2, 2 * EDGE, 3 * channels), BF16),
            pltpu.VMEM((6, EDGE + 8, channels), F32),
        ],
        compiler_params=LARGE,
    )(
        held,
        above,
        below,
        left,
        right,
        early,
        stats,
        flat(first_gain),
        flat(first_bias),
        flat(first_offset),
        near,
    )
    chips = ("tm", "y", "col")
    other = swapped(packed, "core", 1)
    early = shifted(hidden[-2:], "tm", 1)
    stats = everyone(joined(packed, other, group, lax.axis_size(chips)), chips)
    out = pl.pallas_call(
        functools.partial(second_body, lax.axis_size("core")),
        out_shape=jax.ShapeDtypeStruct((frames, height, 2, 2 * breadth, channels), BF16),
        in_specs=[VMEM] * 8,
        out_specs=HBM,
        scratch_shapes=[
            pltpu.VMEM((3, frames + 2, tall, breadth, channels), BF16),
            pltpu.VMEM((2 * EDGE, channels), F32),
            pltpu.VMEM((frames, height, 2, 2 * breadth, channels), BF16),
            pltpu.VMEM((channels // LANES, 2 * height * breadth, LANES), F32),
            pltpu.SemaphoreType.DMA((frames,)),
        ],
        compiler_params=LARGE,
    )(
        held,
        hidden,
        early,
        stats,
        flat(second_gain),
        flat(second_bias),
        flat(second_offset),
        weights(second_kernel),
    )
    return out.reshape(frames, 2 * height, 2 * breadth, channels)


def solution(mesh):
    frames, rows, columns = mesh.devices.shape
    split = jax.sharding.Mesh(
        mesh.devices.reshape(frames, rows // 2, 2, columns), ("tm", "y", "core", "col")
    )
    cut = P("tm", ROW, "col", None)
    placed = (cut, P(), P(), P(), P(), P(), P(), P(), P())
    return jax.shard_map(local, mesh=split, in_specs=placed, out_specs=cut, check_vma=False)
```

```python
import functools

import jax
import jax.numpy as jnp
from jax import lax
from jax.experimental import pallas as pl
from jax.experimental.pallas import tpu as pltpu
from jax.sharding import PartitionSpec as P

G = 32
EPSILON = 1e-06
LANES = 128
F32 = jnp.float32
BF16 = jnp.bfloat16
ROW = ("y", "core")
LINE = 16
EDGE = 24


def picked(x, chosen):
    high = x.astype(BF16).astype(F32)
    rest = x - high
    middle = rest.astype(BF16).astype(F32)
    low = rest - middle
    stacked = jnp.concatenate([high, middle, low, jnp.zeros((13, x.shape[1]), F32)], axis=0)
    return jnp.sum(
        jnp.dot(stacked.astype(BF16), chosen, preferred_element_type=F32), axis=0, keepdims=True
    )


def lanes_of(channels, channels_last):
    shape = (LANES, 2 * channels) if channels_last else (2 * channels, LANES)
    channel = lax.broadcasted_iota(jnp.int32, shape, 1 if channels_last else 0)
    lane = lax.broadcasted_iota(jnp.int32, shape, 0 if channels_last else 1)
    return (channel // (channels // G) == lane).astype(BF16)


def fold(x, mean, squares, seen):
    n = float(x.shape[0])
    own = jnp.sum(x, axis=0, keepdims=True) / n
    apart = x - own
    spread = jnp.sum(apart * apart, axis=0, keepdims=True)
    both = seen + n
    gap = own - mean
    return mean + gap * (n / both), squares + spread + gap * gap * (seen * n / both), both


def pack(mean, squares, count):
    channels = mean.shape[-1]
    per = channels // G
    one = lax.broadcasted_iota(jnp.int32, (channels, channels), 0) // per
    other = lax.broadcasted_iota(jnp.int32, (channels, channels), 1) // per
    grouped = picked(mean, (one == other).astype(BF16)) / per
    apart = grouped - mean
    total = squares + count * apart * apart
    return picked(jnp.concatenate([mean / per, total], axis=1), lanes_of(channels, False))


def merge(rows, count):
    summed = jnp.sum(rows, axis=0, keepdims=True)
    average = summed / rows.shape[0]
    apart = rows - average
    spread = count * jnp.sum(apart * apart, axis=0, keepdims=True)
    lane = lax.broadcasted_iota(jnp.int32, (1, LANES), 1)
    total = jnp.where(lane < 2 * G, summed + pltpu.roll(spread, G, 1), 0.0)
    return jnp.where(lane < G, average, total)


def join_kernel(count, own_ref, other_ref, *refs):
    o_ref = refs[-1]
    row = merge(jnp.concatenate([own_ref[0], other_ref[0]], axis=0), count)
    o_ref[...] = jnp.broadcast_to(row[None], o_ref.shape)


def norm_of(stats_ref, group, gain_ref, bias_ref):
    rows = stats_ref[...]
    channels = gain_ref.shape[-1]
    wide = picked(merge(rows, float(group)), lanes_of(channels, True))
    variance = wide[:, channels:] / float(group * rows.shape[0])
    scale = lax.rsqrt(variance + EPSILON) * gain_ref[...]
    return wide[:, :channels], 0.5 * scale, 0.5 * bias_ref[...]


def active(x, norm):
    mean, half_scale, half_bias = norm
    half = (x.astype(F32) - mean) * half_scale + half_bias
    return half * jnp.tanh(half) + half


def within():
    def place(axis):
        if axis != ROW:
            return lax.axis_index(axis)
        return lax.axis_index("y") * lax.axis_size("core") + lax.axis_index("core")

    def unless(axis, where):
        return jnp.where(place(axis) == where, 0.0, 1.0).astype(F32)

    return (
        unless(ROW, 0),
        unless(ROW, lax.axis_size(ROW) - 1),
        unless("col", 0),
        unless("col", lax.axis_size("col") - 1),
    )


def columns_kernel(x_ref, to_left_ref, to_right_ref, rows_ref, all_ref):
    frames, height, breadth, channels = x_ref.shape
    cells = height * breadth
    target = lax.broadcasted_iota(jnp.int32, (4 * height, cells), 0)
    source = lax.broadcasted_iota(jnp.int32, (4 * height, cells), 1)
    which = target // height
    column = jnp.where(which < 2, which, which + (breadth - 4))
    chosen = (source == (target % height) * breadth + column).astype(BF16)
    all_ref[...] = x_ref[...]
    for t in range(frames):
        got = jnp.dot(
            chosen, x_ref[t].reshape(cells, channels), preferred_element_type=F32
        ).astype(BF16)
        got = got.reshape(4, height, channels)
        to_left_ref[t] = got[:2]
        to_right_ref[t] = got[2:]
        rows_ref[t, pl.ds(0, 2)] = x_ref[t, pl.ds(0, 2)]
        rows_ref[t, pl.ds(2, 2)] = x_ref[t, pl.ds(height - 2, 2)]


def stats_kernel(x_ref, o_ref):
    frames, height, breadth, channels = x_ref.shape
    carry = (jnp.zeros((1, channels), F32), jnp.zeros((1, channels), F32), 0.0)
    for t in range(frames):
        carry = fold(x_ref[t].astype(F32).reshape(height * breadth, channels), *carry)
    row = pack(carry[0], carry[1], float(frames * height * breadth))
    o_ref[...] = jnp.broadcast_to(row[None], o_ref.shape)


def rows_kernel(rows_ref, left_ref, right_ref, to_above_ref, to_below_ref):
    frames, _, height, channels = left_ref.shape
    for t in range(frames):
        corners = [
            ref[t, k].astype(F32) for ref in (left_ref, right_ref) for k in range(2)
        ]
        for k, (ref, start) in enumerate(((to_above_ref, 0), (to_below_ref, height - 2))):
            ref[t, pl.ds(0, 2)] = rows_ref[t, pl.ds(2 * k, 2)]
            line = [c[start : start + 2] for c in corners]
            line.append(jnp.zeros((LINE - 8, channels), F32))
            ref[t, 2] = jnp.concatenate(line, axis=0).astype(BF16)


def put(a_ref, t, i, y, left, right):
    a_ref[0, t, i] = jnp.concatenate([left, y[:-1]], axis=0).astype(BF16)
    a_ref[1, t, i] = y.astype(BF16)
    a_ref[2, t, i] = jnp.concatenate([y[1:], right], axis=0).astype(BF16)


def conv_frame(a_ref, e_ref, w_ref, t):
    rows, breadth, channels = a_ref.shape[2] - 2, a_ref.shape[3], a_ref.shape[4]
    total = None
    for a in range(3):
        for b in range(3):
            window = jnp.concatenate(
                [
                    a_ref[c, t + a, pl.ds(b, rows)].reshape(rows * breadth, channels)
                    for c in range(3)
                ],
                axis=1,
            )
            if e_ref is not None:
                window = jnp.concatenate([window, e_ref[b, t + a]], axis=0)
            part = jnp.dot(window, w_ref[3 * a + b], preferred_element_type=F32)
            total = part if total is None else total + part
    return total


def first_body(
    share,
    own_ref,
    above_ref,
    below_ref,
    left_ref,
    right_ref,
    early_ref,
    stats_ref,
    gain_ref,
    bias_ref,
    offset_ref,
    w_ref,
    hidden_ref,
    packed_ref,
    a_ref,
    e_ref,
    c_ref,
):
    frames, height, breadth, channels = own_ref.shape
    group = frames * height * breadth * (channels // G)
    norm = norm_of(stats_ref, share * group, gain_ref, bias_ref)
    top, bottom, leftmost, rightmost = within()
    tall = height + 4

    def frame(pick, t):
        upper = active(pick(1, 2), norm) * top
        lower = active(pick(2, 2), norm) * bottom
        for k in range(4):
            side = leftmost if k < 2 else rightmost
            x = pick(3, k) if k < 2 else pick(4, k - 2)
            c_ref[k, pl.ds(0, 2)] = upper[2 * k : 2 * k + 2] * side
            c_ref[k, pl.ds(2, height)] = active(x, norm) * side
            c_ref[k, pl.ds(2 + height, 2)] = lower[2 * k : 2 * k + 2] * side
        for i in range(tall):
            if i < 2:
                y = active(pick(1, i), norm) * top
            elif i >= height + 2:
                y = active(pick(2, i - height - 2), norm) * bottom
            else:
                y = active(pick(0, i - 2), norm)
            put(a_ref, t, i, y, c_ref[1, pl.ds(i, 1)], c_ref[2, pl.ds(i, 1)])
            c_ref[4, pl.ds(i, 1)] = y[:1]
            c_ref[5, pl.ds(i, 1)] = y[breadth - 1 :]
        for b in range(3):
            for c, (near, far) in enumerate(((0, 5), (1, 2), (4, 3))):
                both = jnp.concatenate(
                    [c_ref[near, pl.ds(b, EDGE)], c_ref[far, pl.ds(b, EDGE)]], axis=0
                )
                e_ref[b, t, :, pl.ds(c * channels, channels)] = both.astype(BF16)

    c_ref[...] = jnp.zeros_like(c_ref)
    own = (own_ref, above_ref, below_ref, left_ref, right_ref)
    lines = [(0, height), (height, 3), (height + 3, 3), (height + 6, 2), (height + 8, 2)]
    sent = [early_ref.at[:, pl.ds(start, size)] for start, size in lines]
    first_device = lax.axis_index("tm") == 0

    def own_line(t):
        return lambda k, i: own[k][t, i]

    def early_line(t):
        return lambda k, i: jnp.where(
            first_device, own[k][0, i], sent[k][t, i]
        )

    for t in range(2):
        frame(early_line(t), t)
    frame(own_line(0), 2)
    inner = (height + 2) * breadth

    def one(t, carry):
        out = conv_frame(a_ref, e_ref, w_ref, t) + offset_ref[...]
        hidden_ref[t] = out.reshape(hidden_ref.shape[1:])
        return fold(out[breadth : inner - breadth], *carry)

    carry = (jnp.zeros((1, channels), F32), jnp.zeros((1, channels), F32), 0.0)
    for t in range(frames):
        if t + 1 < frames:
            frame(own_line(t + 1), t + 3)
        carry = one(t, carry)
    mean, squares, _ = carry
    row = pack(mean, squares, float(frames * height * breadth))
    packed_ref[...] = jnp.broadcast_to(row[None], packed_ref.shape)


def second_body(
    share,
    features_ref,
    own_ref,
    early_ref,
    stats_ref,
    gain_ref,
    bias_ref,
    offset_ref,
    w_ref,
    out_hbm,
    a_ref,
    c_ref,
    out_ref,
    u_ref,
    out_sem,
):
    frames, height, breadth, channels = features_ref.shape
    group = frames * height * breadth * (channels // G)
    norm = norm_of(stats_ref, share * group, gain_ref, bias_ref)
    top, bottom, leftmost, rightmost = within()
    tall = height + 2
    line = lax.broadcasted_iota(jnp.int32, (2 * EDGE, 1), 0)
    i_of = line % EDGE
    edges = jnp.where(line < EDGE, leftmost, rightmost)
    edges = edges * jnp.where(i_of == 0, top, jnp.where(i_of == tall - 1, bottom, 1.0))

    def frame(pick, t):
        sides = pick(pl.ds(tall, 2 * EDGE // LINE)).reshape(2 * EDGE, channels)
        c_ref[...] = active(sides, norm) * edges
        for i in range(tall):
            y = active(pick(i), norm)
            if i == 0:
                y = y * top
            elif i == tall - 1:
                y = y * bottom
            put(a_ref, t, i, y, c_ref[pl.ds(i, 1)], c_ref[pl.ds(EDGE + i, 1)])

    first_device = lax.axis_index("tm") == 0

    def own_line(t):
        return lambda i: own_ref[t, i]

    def early_line(t):
        return lambda i: jnp.where(first_device, own_ref[0, i], early_ref[t, i])

    for t in range(2):
        frame(early_line(t), t)
    frame(own_line(0), 2)
    cells = height * breadth

    def one(t, carry):
        out = conv_frame(a_ref, None, w_ref, t) + offset_ref[...]
        blended = (features_ref[t].astype(F32).reshape(cells, channels) + out)
        for k in range(channels // LANES):
            half = blended[:, k * LANES : (k + 1) * LANES]
            u_ref[k, pl.ds(0, cells, stride=2), :] = half
            u_ref[k, pl.ds(1, cells, stride=2), :] = half
        wide = jnp.concatenate([u_ref[k] for k in range(channels // LANES)], axis=1)
        wide = wide.astype(BF16).reshape(height, 2 * breadth, channels)
        out_ref[t, :, 0] = wide
        out_ref[t, :, 1] = wide
        pltpu.make_async_copy(out_ref.at[t], out_hbm.at[t], out_sem.at[t]).start()
        return carry

    for t in range(frames):
        if t + 1 < frames:
            frame(own_line(t + 1), t + 3)
        one(t, 0)
    for t in range(frames):
        pltpu.make_async_copy(out_ref.at[t], out_hbm.at[t], out_sem.at[t]).wait()


VMEM = pl.BlockSpec(memory_space=pltpu.VMEM)
HBM = pl.BlockSpec(memory_space=pltpu.HBM)
PARAMS = pltpu.CompilerParams(vmem_limit_bytes=8 * 2**20)
LARGE = pltpu.CompilerParams(vmem_limit_bytes=16 * 2**20)


def shifted(x, axis, by):
    size = lax.axis_size(axis)
    return lax.ppermute(x, axis, [(i, (i + by) % size) for i in range(size)])


def swapped(x, axis, bits):
    size = lax.axis_size(axis)
    return lax.ppermute(x, axis, [(i, i ^ bits) for i in range(size) if i ^ bits < size])


def joined(own, other, count, copies, *wanted):
    return pl.pallas_call(
        functools.partial(join_kernel, float(count)),
        out_shape=jax.ShapeDtypeStruct((copies, 1, LANES), F32),
        in_specs=[VMEM] * (2 + len(wanted)),
        out_specs=VMEM,
        compiler_params=PARAMS,
    )(own, other, *wanted)


def everyone(rows, axes):
    return lax.all_to_all(rows, axes, 0, 0).reshape(rows.shape[0], LANES)


def local(
    features,
    first_gain,
    first_bias,
    first_kernel,
    first_offset,
    second_gain,
    second_bias,
    second_kernel,
    second_offset,
):
    frames, height, breadth, channels = features.shape
    tall = height + 2
    group = frames * height * breadth * (channels // G)
    row_out = jax.ShapeDtypeStruct((1, 1, LANES), F32)
    columns_out = jax.ShapeDtypeStruct((frames, 2, height, channels), BF16)
    border_out = jax.ShapeDtypeStruct((frames, 3, breadth, channels), BF16)
    hidden_lines = tall + 2 * EDGE // LINE

    def flat(v):
        return v.reshape(1, channels)

    def weights(kernel):
        return kernel.reshape(9, 3 * channels, channels)

    to_left, to_right, outer, held = pl.pallas_call(
        columns_kernel,
        out_shape=(
            columns_out,
            columns_out,
            jax.ShapeDtypeStruct((frames, 4, breadth, channels), BF16),
            jax.ShapeDtypeStruct(features.shape, BF16),
        ),
        in_specs=[VMEM],
        out_specs=(VMEM,) * 4,
        compiler_params=PARAMS,
    )(features)
    right = shifted(to_left, "col", -1)
    left = shifted(to_right, "col", 1)
    stats = pl.pallas_call(
        stats_kernel,
        out_shape=row_out,
        in_specs=[VMEM],
        out_specs=VMEM,
        compiler_params=PARAMS,
    )(held)
    stats = joined(stats, swapped(stats, "core", 1), group, 1)
    other = swapped(stats, "tm", 1)
    to_above, to_below = pl.pallas_call(
        rows_kernel,
        out_shape=(border_out, border_out),
        in_specs=[VMEM] * 3,
        out_specs=(VMEM, VMEM),
        compiler_params=PARAMS,
    )(outer, left, right)
    below = shifted(to_above, ROW, -1)
    above = shifted(to_below, ROW, 1)
    stats, _ = lax.optimization_barrier((stats, to_above))
    stats = joined(stats, other, 2 * group, 1)
    planes = ("y", "col")
    near = weights(first_kernel)
    stats = joined(stats, swapped(stats, "tm", 3), 4 * group, lax.axis_size(planes), near)
    tail = jnp.concatenate([x[-2:] for x in (held, above, below, left, right)], axis=1)
    tail, stats = lax.optimization_barrier((tail, stats))
    early = shifted(tail, "tm", 1)
    stats = everyone(stats, planes)
    hidden, packed = pl.pallas_call(
        functools.partial(first_body, lax.axis_size(("tm", "core"))),
        out_shape=(
            jax.ShapeDtypeStruct((frames, hidden_lines, breadth, channels), F32),
            row_out,
        ),
        in_specs=[VMEM] * 11,
        out_specs=(VMEM, VMEM),
        scratch_shapes=[
            pltpu.VMEM((3, frames + 2, height + 4, breadth, channels), BF16),
            pltpu.VMEM((3, frames + 2, 2 * EDGE, 3 * channels), BF16),
            pltpu.VMEM((6, EDGE + 8, channels), F32),
        ],
        compiler_params=LARGE,
    )(
        held,
        above,
        below,
        left,
        right,
        early,
        stats,
        flat(first_gain),
        flat(first_bias),
        flat(first_offset),
        near,
    )
    chips = ("tm", "y", "col")
    other = swapped(packed, "core", 1)
    early = shifted(hidden[-2:], "tm", 1)
    stats = everyone(joined(packed, other, group, lax.axis_size(chips)), chips)
    out = pl.pallas_call(
        functools.partial(second_body, lax.axis_size("core")),
        out_shape=jax.ShapeDtypeStruct((frames, height, 2, 2 * breadth, channels), BF16),
        in_specs=[VMEM] * 8,
        out_specs=HBM,
        scratch_shapes=[
            pltpu.VMEM((3, frames + 2, tall, breadth, channels), BF16),
            pltpu.VMEM((2 * EDGE, channels), F32),
            pltpu.VMEM((frames, height, 2, 2 * breadth, channels), BF16),
            pltpu.VMEM((channels // LANES, 2 * height * breadth, LANES), F32),
            pltpu.SemaphoreType.DMA((frames,)),
        ],
        compiler_params=LARGE,
    )(
        held,
        hidden,
        early,
        stats,
        flat(second_gain),
        flat(second_bias),
        flat(second_offset),
        weights(second_kernel),
    )
    return out.reshape(frames, 2 * height, 2 * breadth, channels)


def solution(mesh):
    frames, rows, columns = mesh.devices.shape
    split = jax.sharding.Mesh(
        mesh.devices.reshape(frames, rows // 2, 2, columns), ("tm", "y", "core", "col")
    )
    cut = P("tm", ROW, "col", None)
    placed = (cut, P(), P(), P(), P(), P(), P(), P(), P())
    return jax.shard_map(local, mesh=split, in_specs=placed, out_specs=cut, check_vma=False)
```
